128 devices in a mesh: section: 2 (over x_hi), expert: 32 (over y, z, core), shard: 2 (over x_lo).
Axes of the slice: x: 4 (x_hi: 2, x_lo: 2; x = x_hi * 2 + x_lo), y: 4, z: 4, core: 2. Of those that a mesh axis runs over, the one named last changes fastest.
Arguments:
- boundary: bfloat16 [2, 2, 32, 128, 768], P('section', None, 'expert', 'shard'), may hold values from -6 to 6
- routes: int32 [2, 2, 32, 128, 2], P('section', None, 'expert', 'shard'), may hold values from 0 to 63, all different within a row; in each aligned block of 64 rows (0 to 63, 64 to 127, ..., all dimensions but the last counted through in order) at most 3 rows name the same one
- buckets: int32 [128, 128], P('shard'), may hold values from 0 to 31
- query_key_value_weight: bfloat16 [2, 768, 2304], P('section', 'shard'), may hold values from -0.21875 to 0.21875
- attention_output_weight: bfloat16 [2, 768, 768], P('section', 'shard'), may hold values from -0.625 to 0.625
- w_router: bfloat16 [2, 768, 64], P('section', 'shard'), may hold values from -0.15625 to 0.15625
- gain_attn: bfloat16 [2, 768], P('section', 'shard'), may hold values from 0.25 to 1.75
- gain_moe: bfloat16 [2, 768], P('section', 'shard'), may hold values from 0.25 to 1.75
- bias_table: bfloat16 [2, 32, 12], P('section', 'shard'), may hold values from -5 to 5
- expert_in: bfloat16 [2, 64, 768, 3072], P('section', ('expert', 'shard')), may hold values from -0.21875 to 0.21875
- expert_out: bfloat16 [2, 64, 3072, 768], P('section', ('expert', 'shard')), may hold values from -0.15625 to 0.15625
Outputs:
- boundary_out: bfloat16 [2, 2, 32, 128, 768], P('section', None, 'expert', 'shard')
- d_w_qkv: bfloat16 [2, 768, 2304], P('section', 'shard')
- d_w_attn_out: bfloat16 [2, 768, 768], P('section', 'shard')
- d_w_router: bfloat16 [2, 768, 64], P('section', 'shard')
- d_gain_attn: bfloat16 [2, 768], P('section', 'shard')
- d_gain_moe: bfloat16 [2, 768], P('section', 'shard')
- d_bias_table: bfloat16 [2, 32, 12], P('section', 'shard')
- d_expert_in: bfloat16 [2, 64, 768, 3072], P('section', ('expert', 'shard'))
- d_expert_out: bfloat16 [2, 64, 3072, 768], P('section', ('expert', 'shard'))
The draws below stay inside these ranges and needn't reach their ends.
Inputs may be any that keep to these rules, and one draw needn't show every extreme that they name: `routes`: A token's two experts differ. Within one layer, micro-batch and sequence, split the positions into the aligned blocks that the shard axis gives; in each block no expert is named by more than 3 rows, and in some blocks one expert by exactly 3. Every expert is named somewhere.
All inputs are finite; a program needn't handle non-finite values.
Results may differ from the reference program's by a relative error of at most 0.025.
Values may be sent and summed in bfloat16 or wider, within the bound.
No kernel may reach another device: no remote copies, remote signals or barrier semaphores. Data moves between devices by JAX's collectives and lax.ppermute only.
A program may use at most 256 MiB of HBM per device.

```python
import math
import jax
import jax.numpy as jnp
import numpy as np
from jax import lax

D = 768
HEADS = 12
HEAD_DIM = 64
FF = 3072
BUCKETS = 32
LEN = 128
MICRO = 2
SEQS = 32
EXPERTS = 64
MOST = 3
N_SHARD = 2


def with_ends(values, own_key, least, top_value):
    spot = [jax.random.randint(jax.random.fold_in(own_key, axis), (), 0, length) for axis, length in enumerate(values.shape)]
    widest = values.shape.index(max(values.shape))
    next_to = spot[:widest] + [(spot[widest] + 1) % values.shape[widest]] + spot[widest + 1:]
    return values.at[tuple(spot)].set(least).at[tuple(next_to)].set(top_value)


def block_scale(own_key, shape, cuts, least, largest):
    factor_of, own = 1.0, jax.random.fold_in(own_key, 6)
    for position, parts in cuts:
        steps = jnp.exp(jax.random.uniform(jax.random.fold_in(own, position), (parts,), jnp.float32, least / len(cuts), largest / len(cuts)))
        factor_of = factor_of * jnp.repeat(steps, shape[position] // parts).reshape([-1 if axis == position else 1 for axis in range(len(shape))])
    return factor_of


def shared_out(rng, own, number, rows, number_of, top, most, slope):
    ranking = jax.random.permutation(rng, number_of)
    packed, usual = load_shares(number_of, rows * top, most, slope, True), load_shares(number_of, rows * top, most, slope, False)
    places = jnp.arange(number_of)

    def named(tallies, rotation):
        used = int((tallies > 0).sum())
        fixed = max(1, used // 4)
        shifted = fixed + (places - fixed + rotation * (used - fixed)) % max(1, number_of - fixed)
        return jnp.zeros((number_of,), jnp.int32).at[ranking[jnp.where(places < fixed, places, shifted)]].set(jnp.asarray(tallies, jnp.int32))

    tallies = jnp.where(number % 4 == 0, named(packed, number // 4), named(usual, number - number // 4 - 1))
    mixed = jax.random.permutation(jax.random.fold_in(own, 3), number_of)
    donor, receiver = mixed[0:number_of // 2 * 2:2], mixed[1:number_of // 2 * 2:2]
    room = jnp.minimum(tallies[donor] - 1, most - tallies[receiver]) // 2
    room = jnp.where((donor == ranking[0]) | (receiver == ranking[0]) | (tallies[receiver] == 0), 0, jnp.maximum(room, 0))
    shifted = jax.random.randint(jax.random.fold_in(own, 4), (number_of // 2,), 0, 1 << 20) % (room + 1)
    tallies = tallies.at[donor].add(-shifted).at[receiver].add(shifted)
    members = jnp.searchsorted(jnp.cumsum(tallies), jnp.arange(rows * top), side="right").astype(jnp.int32)
    grid = members.reshape(top, rows).T
    grid = grid[jax.random.permutation(jax.random.fold_in(own, 1), rows)]
    rotation = jax.random.randint(jax.random.fold_in(own, 2), (rows, 1), 0, top)
    return jnp.take_along_axis(grid, (jnp.arange(top)[None, :] + rotation) % top, axis=1)


def load_shares(number_of, total, reach, lean, full):
    loads = [(1 << 20) // math.isqrt(grade ** lean) + 1 for grade in range(1, number_of + 1)]
    largest = reach if full else min(reach, max(-(-total // number_of), total * loads[0] // sum(loads)))
    least = 1 if total - largest >= number_of - 1 else 0
    holding, spare = [largest] + [least] * (number_of - 1), total - largest - least * (number_of - 1)
    while spare > 0:
        free = [i for i in range(1, number_of) if holding[i] < largest] or [i for i in range(1, number_of) if holding[i] < reach]
        whole, left = sum([loads[i] for i in free]), spare
        for i in free:
            addition = min(reach - holding[i], max(1, left * loads[i] // whole), spare)
            holding[i] = holding[i] + addition
            spare = spare - addition
    return np.array(holding)


def centred(key, extent, deviation, most, split=(), held_as=jnp.bfloat16):
    drawn = deviation * jax.random.normal(key, extent, jnp.float32)
    if split:
        drawn = drawn * block_scale(key, extent, split, -0.22, 0.18)
    return jnp.clip(drawn, -most, most).astype(held_as)


def setup_inputs(seed: int = 0) -> dict:
    splits = jax.random.split(jax.random.key(seed), 12)
    boundary = centred(splits[0], (2, MICRO, SEQS, LEN, D), 1.0, 6.0, ((0, 2), (2, 32), (3, 2)))
    routes_keys = jax.random.split(jax.random.fold_in(splits[1], 1), 2 * MICRO * SEQS * LEN // (LEN // N_SHARD))
    routes_turns = jax.random.permutation(jax.random.fold_in(splits[1], 3), 2 * MICRO * SEQS * LEN // (LEN // N_SHARD))
    routes = jax.vmap(lambda own, number: shared_out(jax.random.fold_in(splits[1], 2), own, number, LEN // N_SHARD, EXPERTS, 2, MOST, 2))(routes_keys, routes_turns).reshape((2, MICRO, SEQS, LEN, 2))
    buckets = with_ends(jax.random.randint(splits[2], (LEN, LEN), 0, BUCKETS), jax.random.fold_in(splits[2], 1), 0, BUCKETS - 1).astype(jnp.int32)
    query_key_value_weight = centred(splits[3], (2, D, 3 * D), D ** -0.5, 0.21875, ((0, 2), (1, 2)))
    attention_output_weight = centred(splits[4], (2, D, D), (D // 8) ** -0.5, 0.625, ((0, 2), (1, 2)))
    w_router = centred(splits[5], (2, D, EXPERTS), (2 * D) ** -0.5, 0.15625, ((0, 2), (1, 2)))
    gain_attn = jnp.clip(1.0 + 0.15 * jax.random.normal(splits[6], (2, D), jnp.float32), 0.25, 1.75).astype(jnp.bfloat16)
    gain_moe = jnp.clip(1.0 + 0.15 * jax.random.normal(splits[7], (2, D), jnp.float32), 0.25, 1.75).astype(jnp.bfloat16)
    bias_table = centred(splits[8], (2, BUCKETS, HEADS), 1.0, 5.0, ((0, 2), (1, 2)))
    expert_in = centred(splits[9], (2, EXPERTS, D, FF), D ** -0.5, 0.21875, ((0, 2), (1, 64)))
    expert_out = centred(splits[10], (2, EXPERTS, FF, D), (FF // 2) ** -0.5, 0.15625, ((0, 2), (1, 64)))
    return dict(boundary=boundary, routes=routes, buckets=buckets, query_key_value_weight=query_key_value_weight, attention_output_weight=attention_output_weight, w_router=w_router, gain_attn=gain_attn, gain_moe=gain_moe, bias_table=bias_table, expert_in=expert_in, expert_out=expert_out)


@jax.custom_vjp
def low(v):
    return lax.optimization_barrier(v.astype(jnp.bfloat16)).astype(jnp.float32)

@jax.custom_vjp
def lower_returned(v):
    return v

def low_keep(v):
    return (low(v), None)

def low_pass(kept, grad):
    return (grad,)

def back_keep(v):
    return (v, None)

def back_low(kept, grad):
    return (low(grad),)
low.defvjp(low_keep, low_pass)
lower_returned.defvjp(back_keep, back_low)
EPS = 1e-06
FULL_ACCURACY = lax.Precision.HIGHEST

def rms_scale(values, gain_row):
    return values * lax.rsqrt(lax.optimization_barrier(jnp.mean(values * values, axis=-1, keepdims=True)) + EPS) * gain_row

def attend(normalized_rows, query_key_value_weight, attention_output_weight, table, buckets):
    projected_rows = jnp.einsum('kqt,tn->kqn', normalized_rows, query_key_value_weight, precision=FULL_ACCURACY)
    queries = lower_returned(low(projected_rows[..., :D]))
    key_rows = lower_returned(low(projected_rows[..., D:2 * D]))
    value_rows = lower_returned(low(projected_rows[..., 2 * D:]))
    head_shape = (SEQS, LEN, HEADS, HEAD_DIM)
    raw_scores = jnp.einsum('sihd,sjhd->shij', queries.reshape(head_shape), key_rows.reshape(head_shape), precision=FULL_ACCURACY)
    score_bias = jnp.transpose(table[buckets], (2, 0, 1))
    scores = lower_returned(raw_scores * HEAD_DIM ** (-0.5) + score_bias[None])
    positions = jnp.arange(LEN, dtype=jnp.int32)
    causal = positions[None, :] <= positions[:, None]
    masked = jnp.where(causal, scores, -jnp.inf)
    top_score = lax.optimization_barrier(jnp.max(masked, axis=-1, keepdims=True))
    log_total = top_score + jnp.log(lax.optimization_barrier(jnp.sum(jnp.exp(masked - top_score), axis=-1, keepdims=True)))
    prob_low = low(jnp.exp(masked - log_total))
    blended_rows = jnp.einsum('shij,sjhd->sihd', prob_low, value_rows.reshape(head_shape), precision=FULL_ACCURACY)
    blended_rows = lower_returned(low(blended_rows.reshape(SEQS, LEN, D)))
    return lower_returned(jnp.einsum('kqt,tn->kqn', blended_rows, attention_output_weight, precision=FULL_ACCURACY))

def expert_apply(operands):
    expert_rows, w_in, w_out = operands
    pre_values = lower_returned(jnp.dot(expert_rows, w_in, precision=FULL_ACCURACY))
    activated = low(jax.nn.gelu(pre_values, approximate=False))
    return lower_returned(low(jnp.dot(activated, w_out, precision=FULL_ACCURACY)))

def moe_block(normalized_rows, w_router, w_in, w_out, route_pick):
    token_count = normalized_rows.shape[0]
    logits = lower_returned(jnp.dot(normalized_rows, w_router, precision=FULL_ACCURACY))
    chosen = jnp.take_along_axis(logits, route_pick, axis=1)
    gate_top = lax.optimization_barrier(jnp.max(chosen, axis=1, keepdims=True))
    gate_raw = jnp.exp(chosen - gate_top)
    gate_values = gate_raw / lax.optimization_barrier(jnp.sum(gate_raw, axis=1, keepdims=True))
    copies = lower_returned(jnp.broadcast_to(normalized_rows[:, None, :], (token_count, 2, D))).reshape(token_count * 2, D)
    flat_routes = route_pick.reshape(-1).astype(jnp.int32)
    route_hits = (flat_routes[:, None] == jnp.arange(EXPERTS, dtype=jnp.int32)[None, :]).astype(jnp.int32)
    slot_rank = (lax.optimization_barrier(jnp.sum(jnp.cumsum(route_hits, axis=0) * route_hits, axis=1)) - 1).astype(jnp.int32)
    capacity = MICRO * SEQS * N_SHARD * MOST
    buffer = jnp.zeros((EXPERTS, capacity, D), jnp.float32).at[flat_routes, slot_rank].add(copies)
    expert_outs = lax.map(jax.checkpoint(expert_apply), (buffer, w_in, w_out))
    results = expert_outs[flat_routes, slot_rank].reshape(token_count, 2, D)
    return lax.optimization_barrier(jnp.sum(gate_values[:, :, None] * results, axis=1))

def layer(inputs, weights, route_pick, buckets):
    query_key_value_weight, attention_output_weight, w_router, gain_attn, gain_moe, table, w_in, w_out = weights
    inputs = lower_returned(inputs)
    normalized_rows = low(rms_scale(inputs, gain_attn))

    def attend_block(normed_block):
        return attend(normed_block, query_key_value_weight, attention_output_weight, table, buckets)
    attended = lax.map(jax.checkpoint(attend_block), normalized_rows)
    hidden = inputs + attended
    normed_two = low(rms_scale(hidden, gain_moe))
    expert_mix = moe_block(normed_two.reshape(-1, D), w_router, w_in, w_out, route_pick.reshape(-1, 2))
    return low(hidden + expert_mix.reshape(hidden.shape))

def reference(boundary, routes, buckets, query_key_value_weight, attention_output_weight, w_router, gain_attn, gain_moe, bias_table, expert_in, expert_out):
    weights = tuple((tensor.astype(jnp.float32) for tensor in (query_key_value_weight, attention_output_weight, w_router, gain_attn, gain_moe, bias_table, expert_in, expert_out)))
    first_in = boundary[0].astype(jnp.float32)
    out_grad = boundary[1].astype(jnp.float32)

    def network(inputs, params):
        middle = layer(inputs, tuple((tensor[0] for tensor in params)), routes[0], buckets)
        return layer(middle, tuple((tensor[1] for tensor in params)), routes[1], buckets)
    result, pullback = jax.vjp(network, first_in, weights)
    input_grad, weight_grads = pullback(out_grad)
    boundary_out = jnp.stack([input_grad, result]).astype(jnp.bfloat16)
    return (boundary_out, weight_grads[0].astype(jnp.bfloat16), weight_grads[1].astype(jnp.bfloat16), weight_grads[2].astype(jnp.bfloat16), weight_grads[3].astype(jnp.bfloat16), weight_grads[4].astype(jnp.bfloat16), weight_grads[5].astype(jnp.bfloat16), weight_grads[6].astype(jnp.bfloat16), weight_grads[7].astype(jnp.bfloat16))
```

```python
import functools

import jax
import jax.numpy as jnp
from jax import lax
from jax.experimental import pallas as pl
from jax.experimental.pallas import tpu as pltpu
from jax.sharding import Mesh
from jax.sharding import PartitionSpec as P

EPS = 1e-06
F32 = jnp.float32
BF16 = jnp.bfloat16
SLOTS = 8
LANES = 128
HEAD = 64
MEMBERS = ("y", "z", "core", "shard")
VMEM_BYTES = 50 * 1024 * 1024


def dot(a, b):
    return jnp.dot(a, b, preferred_element_type=F32)


def dot_nt(a, b):
    return lax.dot_general(a, b, (((1,), (1,)), ((), ())), preferred_element_type=F32)


def dot_tn(a, b):
    return lax.dot_general(a, b, (((0,), (0,)), ((), ())), preferred_element_type=F32)


def row_scale(values):
    return lax.rsqrt(jnp.mean(values * values, axis=-1, keepdims=True) + EPS)


def iota(shape, axis):
    return lax.broadcasted_iota(jnp.int32, shape, axis)


def one_hot(matches):
    return jnp.where(matches, 1.0, 0.0).astype(BF16)


def head_parts(pair):
    lane = iota(pair.shape, 1)
    zero = jnp.zeros_like(pair)
    return jnp.where(lane < HEAD, pair, zero), jnp.where(lane >= HEAD, pair, zero)


def soft_probs(query, key, bias, causal):
    scores = dot_nt(query, key) * (HEAD**-0.5) + bias
    scores = jnp.where(causal, scores, -jnp.inf)
    raised = jnp.exp(scores - jnp.max(scores, axis=-1, keepdims=True))
    return raised / jnp.sum(raised, axis=-1, keepdims=True)


def mixer_forward(with_grads, *refs):
    if with_grads:
        x_ref, dy_ref, wqkv, wout, wr, gains, bias, srow, scol = refs[:9]
        send, hidden_out, gates_out, proj, mixed, norm1_out, norm2_out = refs[9:]
    else:
        x_ref, wqkv, wout, wr, gains, bias, srow, scol = refs[:8]
        send, hidden_out, gates_out, proj, mixed = refs[8:]
    tokens, width = x_ref.shape
    x = x_ref[...].astype(F32)
    norm1 = (x * row_scale(x) * gains[0:1, :]).astype(BF16)
    proj[...] = dot(norm1, wqkv[...]).astype(BF16)
    causal = iota((tokens, tokens), 1) <= iota((tokens, tokens), 0)
    for pair in range(width // LANES):
        at = pair * LANES
        queries = head_parts(proj[:, at : at + LANES])
        key = proj[:, width + at : width + at + LANES]
        values = head_parts(proj[:, 2 * width + at : 2 * width + at + LANES])
        total = None
        for half in range(2):
            probs = soft_probs(queries[half], key, bias[2 * pair + half], causal).astype(BF16)
            part = dot(probs, values[half])
            total = part if total is None else total + part
        mixed[:, at : at + LANES] = total.astype(BF16)
    hidden = x + dot(mixed[...], wout[...])
    hidden_out[...] = hidden
    norm2 = (hidden * row_scale(hidden) * gains[1:2, :]).astype(BF16)
    logits = dot(norm2, wr[...])
    lane = iota((tokens, LANES), 1)
    first = jnp.sum(jnp.where(lane == scol[:, 2:3], logits, 0.0), axis=1, keepdims=True)
    second = jnp.sum(jnp.where(lane == scol[:, 3:4], logits, 0.0), axis=1, keepdims=True)
    top = jnp.maximum(first, second)
    first = jnp.exp(first - top)
    second = jnp.exp(second - top)
    gate0 = first / (first + second)
    gate1 = second / (first + second)
    gates_out[...] = jnp.where(lane == 0, gate0, jnp.where(lane == 1, gate1, 0.0))
    slot = iota((send.shape[0], tokens), 0)
    hits0 = slot == srow[0:1, :]
    hits1 = slot == srow[1:2, :]
    send[:, :width] = dot(one_hot(hits0 | hits1), norm2).astype(BF16)
    if with_grads:
        dy = dy_ref[...].astype(F32)
        send[:, width:] = (
            dot(one_hot(hits0), (gate0 * dy).astype(BF16))
            + dot(one_hot(hits1), (gate1 * dy).astype(BF16))
        ).astype(BF16)
        norm1_out[...] = norm1
        norm2_out[...] = norm2


def grads_out(dy_ref, gates, srow, send):
    tokens = dy_ref.shape[0]
    dy = dy_ref[...].astype(F32)
    slot = iota((send.shape[0], tokens), 0)
    send[...] = (
        dot(one_hot(slot == srow[0:1, :]), (gates[:, 0:1] * dy).astype(BF16))
        + dot(one_hot(slot == srow[1:2, :]), (gates[:, 1:2] * dy).astype(BF16))
    ).astype(BF16)


def combine(back, hidden, gates, scol, out):
    tokens = hidden.shape[0]
    slot = iota((tokens, back.shape[0]), 1)
    result0 = dot(one_hot(slot == scol[:, 0:1]), back[...])
    result1 = dot(one_hot(slot == scol[:, 1:2]), back[...])
    out[...] = (hidden[...] + gates[:, 0:1] * result0 + gates[:, 1:2] * result1).astype(BF16)


def bell(pre):
    return 0.5 * (1.0 + lax.erf(pre * 0.7071067811865476))


def experts_forward(rows, up, down, out, total):
    step = pl.program_id(0)
    pre = dot(rows[...], up[...])
    part = dot((pre * bell(pre)).astype(BF16), down[...])

    @pl.when(step == 0)
    def _():
        total[...] = part

    @pl.when(step > 0)
    def _():
        total[...] += part

    @pl.when(step == pl.num_programs(0) - 1)
    def _():
        out[...] = total[...].astype(BF16)


def experts_both(rows, up, down, out, act_out, slope_out, total, total_back):
    step = pl.program_id(0)
    width = up.shape[0]
    pre = dot(rows[:, :width], up[...])
    lower = bell(pre)
    act = (pre * lower).astype(BF16)
    slope = lower + pre * jnp.exp(-0.5 * pre * pre) * 0.3989422804014327
    act_out[...] = act
    slope_out[...] = slope.astype(BF16)
    part = dot(act, down[...])
    pre_grads = (dot_nt(rows[:, width:], down[...]) * slope).astype(BF16)
    part_back = dot_nt(pre_grads, up[...])

    @pl.when(step == 0)
    def _():
        total[...] = part
        total_back[...] = part_back

    @pl.when(step > 0)
    def _():
        total[...] += part
        total_back[...] += part_back

    @pl.when(step == pl.num_programs(0) - 1)
    def _():
        out[:, :width] = total[...].astype(BF16)
        out[:, width:] = total_back[...].astype(BF16)


def experts_backward(grads, up, down, slope, out, pre_out, total_back):
    step = pl.program_id(0)
    pre_grads = (dot_nt(grads[...], down[...]) * slope[...].astype(F32)).astype(BF16)
    pre_out[...] = pre_grads
    part_back = dot_nt(pre_grads, up[...])

    @pl.when(step == 0)
    def _():
        total_back[...] = part_back

    @pl.when(step > 0)
    def _():
        total_back[...] += part_back

    @pl.when(step == pl.num_programs(0) - 1)
    def _():
        out[...] = total_back[...].astype(BF16)


def mixer_backward(last, *refs):
    if last:
        (core, back, dy_ref, x_ref, res_in, wqkv, wout, wr, gains, bias, scol) = refs[:11]
        (hidden_ref, gates, proj, mixed, norm1, norm2) = refs[11:17]
        (input_grad, keep, give, stats, score_out, proj_grad) = refs[17:]
    else:
        (back, dy_ref, x_ref, wqkv, wout, wr, gains, bias, scol) = refs[:9]
        (hidden_ref, gates, proj) = refs[9:12]
        (input_grad, y_out, res_out, proj_grad) = refs[12:]
    tokens, width = x_ref.shape
    dy = dy_ref[...].astype(F32)
    hidden = hidden_ref[...]
    gate0 = gates[:, 0:1]
    gate1 = gates[:, 1:2]
    slot = iota((tokens, back.shape[0]), 1)
    hits0 = slot == scol[:, 0:1]
    hits1 = slot == scol[:, 1:2]
    if last:
        result0 = res_in[0].astype(F32)
        result1 = res_in[1].astype(F32)
        copy_rows = back[...]
    else:
        result0 = dot(one_hot(hits0), back[:, :width])
        result1 = dot(one_hot(hits1), back[:, :width])
        res_out[0] = result0.astype(BF16)
        res_out[1] = result1.astype(BF16)
        y_out[...] = (hidden + gate0 * result0 + gate1 * result1).astype(BF16)
        copy_rows = back[:, width:]
    gate_grad0 = jnp.sum(result0 * dy, axis=1, keepdims=True)
    gate_grad1 = jnp.sum(result1 * dy, axis=1, keepdims=True)
    inner = gate0 * gate_grad0 + gate1 * gate_grad1
    lane = iota((tokens, LANES), 1)
    logit_grads = (
        jnp.where(lane == scol[:, 2:3], gate0 * (gate_grad0 - inner), 0.0)
        + jnp.where(lane == scol[:, 3:4], gate1 * (gate_grad1 - inner), 0.0)
    ).astype(BF16)
    norm2_grads = dot(one_hot(hits0 | hits1), copy_rows) + dot_nt(logit_grads, wr[...])
    scale2 = row_scale(hidden)
    weighted = norm2_grads * gains[1:2, :]
    inner = jnp.mean(weighted * hidden, axis=-1, keepdims=True)
    hidden_grad = dy + scale2 * weighted - hidden * (scale2 * scale2 * scale2 * inner)
    branch = hidden_grad.astype(BF16)
    mixed_grad = dot_nt(branch, wout[...]).astype(BF16)
    causal = iota((tokens, tokens), 1) <= iota((tokens, tokens), 0)
    for pair in range(width // LANES):
        at = pair * LANES
        queries = head_parts(proj[:, at : at + LANES])
        key = proj[:, width + at : width + at + LANES]
        keys = head_parts(key)
        value = proj[:, 2 * width + at : 2 * width + at + LANES]
        outer = head_parts(mixed_grad[:, at : at + LANES])
        query_sum = key_sum = value_sum = None
        for half in range(2):
            probs = soft_probs(queries[half], key, bias[2 * pair + half], causal)
            prob_grad = dot_nt(outer[half], value)
            inner = jnp.sum(probs * prob_grad, axis=-1, keepdims=True)
            score_grad = (probs * (prob_grad - inner)).astype(BF16)
            if last:
                score_out[2 * pair + half] = score_grad
            query_part = dot(score_grad, keys[half])
            key_part = dot_tn(score_grad, queries[half])
            value_part = dot_tn(probs.astype(BF16), outer[half])
            query_sum = query_part if half == 0 else query_sum + query_part
            key_sum = key_part if half == 0 else key_sum + key_part
            value_sum = value_part if half == 0 else value_sum + value_part
        proj_grad[:, at : at + LANES] = (query_sum * HEAD**-0.5).astype(BF16)
        proj_grad[:, width + at : width + at + LANES] = (key_sum * HEAD**-0.5).astype(BF16)
        proj_grad[:, 2 * width + at : 2 * width + at + LANES] = value_sum.astype(BF16)
    norm1_grads = dot_nt(proj_grad[...], wqkv[...])
    x = x_ref[...].astype(F32)
    scale1 = row_scale(x)
    weighted = norm1_grads * gains[0:1, :]
    inner = jnp.mean(weighted * x, axis=-1, keepdims=True)
    input_grad[...] = (
        hidden_grad + scale1 * weighted - x * (scale1 * scale1 * scale1 * inner)
    ).astype(BF16)
    if last:
        stats[0:1, :] = jnp.sum(norm1_grads * x * scale1, axis=0, keepdims=True)
        stats[1:2, :] = jnp.sum(norm2_grads * hidden * scale2, axis=0, keepdims=True)
        stats[2:8, :] = jnp.zeros((6, width), F32)
        split = keep.shape[1]
        tail = 3 * width - split

        def fill(low, high):
            low[...] = dot_tn(norm1[...], proj_grad[:, :split]).astype(BF16)
            high[:, :tail] = dot_tn(norm1[...], proj_grad[:, split:]).astype(BF16)
            high[:, tail : tail + width] = dot_tn(mixed[...], branch).astype(BF16)
            high[:, tail + width : tail + width + LANES] = dot_tn(
                norm2[...], logit_grads
            ).astype(BF16)
            high[:, tail + width + LANES :] = jnp.zeros(
                (width, split - tail - width - LANES), BF16
            )

        @pl.when(core[0] == 0)
        def _():
            fill(keep, give)

        @pl.when(core[0] == 1)
        def _():
            fill(give, keep)


def shape_of(*dims, dtype=BF16):
    return jax.ShapeDtypeStruct(dims, dtype)


def whole(kernel, outs, operands, scratch=(), scalar=False, flops=0, name=None):
    vmem = pl.BlockSpec(memory_space=pltpu.VMEM)
    specs = [vmem] * len(operands)
    if scalar:
        specs[0] = pl.BlockSpec(memory_space=pltpu.SMEM)
    moved = sum(o.size * o.dtype.itemsize for o in list(operands) + list(outs))
    return pl.pallas_call(
        kernel,
        out_shape=outs,
        in_specs=specs,
        out_specs=[vmem] * len(outs),
        scratch_shapes=list(scratch),
        cost_estimate=pl.CostEstimate(flops=flops, bytes_accessed=moved, transcendentals=0),
        compiler_params=pltpu.CompilerParams(vmem_limit_bytes=VMEM_BYTES),
        name=name,
    )(*operands)


CHUNK = 512


def expert_call(kernel, rows, up, down, slope, wide_outs, out_cols, sums, name):
    count = rows.shape[0]
    width, hidden_units = up.shape
    specs = [
        pl.BlockSpec(rows.shape, lambda i: (0, 0)),
        pl.BlockSpec((width, CHUNK), lambda i: (0, i)),
        pl.BlockSpec((CHUNK, width), lambda i: (i, 0)),
    ]
    operands = [rows, up, down]
    per_chunk = pl.BlockSpec((count, CHUNK), lambda i: (0, i))
    if slope is not None:
        specs.append(per_chunk)
        operands.append(slope)
    outs = [shape_of(count, out_cols)] + [shape_of(count, hidden_units)] * wide_outs
    moved = sum(o.size * o.dtype.itemsize for o in operands + outs)
    return pl.pallas_call(
        kernel,
        out_shape=outs,
        grid=(hidden_units // CHUNK,),
        in_specs=specs,
        out_specs=[pl.BlockSpec((count, out_cols), lambda i: (0, 0))] + [per_chunk] * wide_outs,
        scratch_shapes=[pltpu.VMEM((count, width), F32)] * sums,
        cost_estimate=pl.CostEstimate(
            flops=4 * sums * count * width * hidden_units,
            bytes_accessed=moved,
            transcendentals=0,
        ),
        compiler_params=pltpu.CompilerParams(
            dimension_semantics=("arbitrary",), vmem_limit_bytes=VMEM_BYTES
        ),
        name=name,
    )(*operands)


def trade(rows):
    count, columns = rows.shape
    pieces = rows.reshape(count // SLOTS, SLOTS, columns)
    return lax.all_to_all(pieces, MEMBERS, 0, 0, tiled=True).reshape(count, columns)


def swap(value, axis):
    return lax.ppermute(value, axis, [(0, 1), (1, 0)])


def in_order(index, mine, other, axis):
    return jnp.where(
        index == 0,
        jnp.concatenate([mine, other], axis=axis),
        jnp.concatenate([other, mine], axis=axis),
    )


def fetch_other(half, core):
    columns = half.shape[1] // 2
    piece = swap(lax.dynamic_slice_in_dim(half, core * columns, columns, 1), "shard")
    return in_order(core, piece, swap(piece, "core"), 1)


def local(
    boundary,
    routes,
    buckets,
    query_key_value_weight,
    attention_output_weight,
    w_router,
    gain_attn,
    gain_moe,
    bias_table,
    expert_in,
    expert_out,
):
    section = lax.axis_index("section")
    shard = lax.axis_index("shard")
    core = lax.axis_index("core")
    _, micro, _, positions, width = boundary.shape
    tokens = 2 * positions
    heads = bias_table.shape[2]
    bucket_count = 2 * bias_table.shape[1]
    experts = w_router.shape[2]
    half_width = width // 2
    count = experts * SLOTS

    own_rows = boundary.reshape(micro, positions, width)
    own_routes = routes.reshape(micro, positions, 2)
    up = expert_in[0, 0]
    down = expert_out[0, 0]

    def pick(stacked, index):
        return lax.dynamic_index_in_dim(stacked, index, 0, keepdims=False)

    qkv_half = query_key_value_weight[0]
    out_half = attention_output_weight[0]
    own_extra = jnp.concatenate(
        [
            w_router[0],
            gain_attn[0][:, None],
            gain_moe[0][:, None],
            jnp.pad(bias_table[0], ((0, half_width - bucket_count // 2), (0, 0))),
            jnp.zeros((half_width, LANES - experts - 2 - heads), BF16),
        ],
        axis=1,
    )
    wqkv = in_order(shard, qkv_half, fetch_other(qkv_half, core), 0)
    wout = in_order(shard, out_half, fetch_other(out_half, core), 0)
    extra = in_order(shard, own_extra, swap(own_extra, "shard"), 0)
    gains = jnp.pad(extra[:, experts : experts + 2].T.astype(F32), ((0, 6), (0, 0)))
    table = jnp.concatenate(
        [
            extra[: bucket_count // 2, experts + 2 : experts + 2 + heads],
            extra[half_width : half_width + bucket_count // 2, experts + 2 : experts + 2 + heads],
        ],
        axis=0,
    )
    mine = in_order(
        shard, pick(own_rows, shard), swap(pick(own_rows, 1 - shard), "shard"), 0
    )
    pairs = in_order(
        shard, pick(own_routes, shard), swap(pick(own_routes, 1 - shard), "shard"), 0
    )
    bucket_full = in_order(shard, buckets, swap(buckets, "shard"), 0)
    bucket_hot = (
        bucket_full[None] == jnp.arange(bucket_count, dtype=jnp.int32)[:, None, None]
    ).astype(BF16)
    bias = jnp.einsum("bts,bh->hts", bucket_hot, table, preferred_element_type=F32)

    flat = pairs.reshape(-1)
    hits = (flat[:, None] == jnp.arange(experts, dtype=jnp.int32)[None, :]).astype(jnp.int32)
    ranks = jnp.sum(jnp.cumsum(hits, axis=0) * hits, axis=1) - 1
    slots = (flat * SLOTS + ranks).reshape(tokens, 2)
    srow = jnp.pad(slots.T, ((0, 6), (0, 0)))
    scol = jnp.pad(jnp.concatenate([slots, pairs], axis=1), ((0, 0), (0, LANES - 4)))

    mixer_flops = 2 * tokens * width * 4 * width
    forward_shapes = [
        shape_of(tokens, width, dtype=F32),
        shape_of(tokens, LANES, dtype=F32),
    ]
    send, hidden, gates = whole(
        functools.partial(mixer_forward, False),
        [shape_of(count, width)] + forward_shapes,
        (mine, wqkv, wout, extra, gains, bias, srow, scol),
        scratch=[pltpu.VMEM((tokens, 3 * width), BF16), pltpu.VMEM((tokens, width), BF16)],
        flops=mixer_flops,
        name="mixer_forward",
    )
    (result_rows,) = expert_call(
        experts_forward, trade(send), up, down, None, 0, width, 1, "experts_forward"
    )
    (layer_out,) = whole(
        combine,
        [shape_of(tokens, width)],
        (trade(result_rows), hidden, gates, scol),
        name="combine",
    )
    arriving = lax.ppermute(layer_out, "section", [(0, 1)])
    layer_in = jnp.where(section == 0, mine, arriving)

    send, hidden, gates, proj, mixed, norm1, norm2 = whole(
        functools.partial(mixer_forward, True),
        [shape_of(count, 2 * width)]
        + forward_shapes
        + [
            shape_of(tokens, 3 * width),
            shape_of(tokens, width),
            shape_of(tokens, width),
            shape_of(tokens, width),
        ],
        (layer_in, mine, wqkv, wout, extra, gains, bias, srow, scol),
        flops=mixer_flops,
        name="mixer_forward_keep",
    )
    arrived = trade(send)
    both, act, slope = expert_call(
        experts_both, arrived, up, down, None, 2, 2 * width, 2, "experts_both"
    )
    input_grad, forward_rows, results = whole(
        functools.partial(mixer_backward, False),
        [
            shape_of(tokens, width),
            shape_of(tokens, width),
            shape_of(2, tokens, width),
        ],
        (trade(both), mine, layer_in, wqkv, wout, extra, gains, bias, scol, hidden, gates, proj),
        scratch=[pltpu.VMEM((tokens, 3 * width), BF16)],
        flops=2 * mixer_flops,
        name="mixer_backward",
    )
    arriving = lax.ppermute(input_grad, "section", [(1, 0)])
    grad_in = jnp.where(section == 0, arriving, mine)

    (send,) = whole(
        grads_out, [shape_of(count, width)], (grad_in, gates, srow), name="grads_out"
    )
    arrived_grads = trade(send)
    copy_rows, pre_grads = expert_call(
        experts_backward, arrived_grads, up, down, slope, 1, width, 1, "experts_backward"
    )
    returned = trade(copy_rows)
    d_expert_in = lax.dot_general(
        arrived[:, :width], pre_grads, (((0,), (0,)), ((), ())), preferred_element_type=F32
    ).astype(BF16)
    d_expert_out = lax.dot_general(
        act, arrived_grads, (((0,), (0,)), ((), ())), preferred_element_type=F32
    ).astype(BF16)
    split = 13 * LANES
    tail = 3 * width - split
    input_grad, keep, give, stats, score_grads = whole(
        functools.partial(mixer_backward, True),
        [
            shape_of(tokens, width),
            shape_of(width, split),
            shape_of(width, split),
            shape_of(8, width, dtype=F32),
            shape_of(heads, tokens, tokens),
        ],
        (
            core.reshape(1),
            returned,
            grad_in,
            layer_in,
            results,
            wqkv,
            wout,
            extra,
            gains,
            bias,
            scol,
            hidden,
            gates,
            proj,
            mixed,
            norm1,
            norm2,
        ),
        scratch=[pltpu.VMEM((tokens, 3 * width), BF16)],
        scalar=True,
        flops=3 * mixer_flops,
        name="mixer_backward_last",
    )

    finished = jnp.where(section == 0, input_grad, forward_rows).reshape(2, positions, width)
    from_other = swap(pick(finished, 1 - shard), "shard")
    boundary_out = jnp.stack(
        [
            jnp.where(shard == 0, pick(finished, shard), from_other),
            jnp.where(shard == 0, from_other, pick(finished, shard)),
        ]
    ).reshape(boundary.shape)

    table_grad = jnp.einsum(
        "bts,hts->bh", bucket_hot, score_grads, preferred_element_type=F32
    )
    half_rows = half_width // LANES
    table_rows = bucket_count // 2
    small = jnp.concatenate(
        [
            stats[0].reshape(2, half_rows, LANES),
            stats[1].reshape(2, half_rows, LANES),
            jnp.zeros((2, 8 - 2 * half_rows, LANES), F32),
            jnp.pad(
                table_grad.reshape(2, table_rows, heads), ((0, 0), (0, 0), (0, LANES - heads))
            ),
        ],
        axis=1,
    )
    small = (small + swap(small, "core")).astype(BF16)
    summed = (keep.astype(F32) + swap(give, "core").astype(F32)).astype(BF16)
    summed = summed.reshape(2, half_width, split)
    spot = (slice(None), slice(0, small.shape[1]), slice(split - LANES, split))
    summed = summed.at[spot].set(jnp.where(core == 1, small, summed[spot]))
    gathered = lax.all_to_all(
        summed.reshape(32, width // 32, split), ("shard", "y", "z"), 0, 0, tiled=True
    )
    piece = jnp.sum(gathered.astype(F32), axis=0).astype(BF16)
    spread = lax.all_to_all(
        jnp.broadcast_to(piece[None], (16,) + piece.shape), ("y", "z"), 0, 0, tiled=True
    ).reshape(half_width, split)
    other = swap(spread, "core")
    low = jnp.where(core == 0, spread, other)
    high = jnp.where(core == 0, other, spread)
    totals = high[: 8 + table_rows, split - LANES :]
    gain_one_sum = totals[:half_rows].reshape(half_width)
    gain_two_sum = totals[half_rows : 2 * half_rows].reshape(half_width)
    table_sum = totals[8:, :heads]
    return (
        boundary_out,
        jnp.concatenate([low, high[:, :tail]], axis=1)[None],
        high[:, tail : tail + width][None],
        high[:, tail + width : tail + width + experts][None],
        gain_one_sum[None],
        gain_two_sum[None],
        table_sum[None],
        d_expert_in.reshape(expert_in.shape),
        d_expert_out.reshape(expert_out.shape),
    )


def solution(mesh):
    fine = Mesh(
        mesh.devices.reshape(2, 4, 4, 2, 2), ("section", "y", "z", "core", "shard")
    )
    expert = ("y", "z", "core")
    rows = P("section", None, expert, "shard", None)
    by_pair = P("section", "shard", None)
    by_expert = P("section", MEMBERS, None, None)
    in_specs = (
        rows,
        rows,
        P("shard", None),
        by_pair,
        by_pair,
        by_pair,
        P("section", "shard"),
        P("section", "shard"),
        by_pair,
        by_expert,
        by_expert,
    )
    out_specs = (
        rows,
        by_pair,
        by_pair,
        by_pair,
        P("section", "shard"),
        P("section", "shard"),
        by_pair,
        by_expert,
        by_expert,
    )
    return jax.shard_map(local, mesh=fine, in_specs=in_specs, out_specs=out_specs, check_vma=False)
```

```python
import functools

import jax
import jax.numpy as jnp
from jax import lax
from jax.experimental import pallas as pl
from jax.experimental.pallas import tpu as pltpu
from jax.sharding import Mesh
from jax.sharding import PartitionSpec as P

EPS = 1e-06
F32 = jnp.float32
BF16 = jnp.bfloat16
SLOTS = 8
LANES = 128
HEAD = 64
MEMBERS = ("y", "z", "core", "shard")
VMEM_BYTES = 50 * 1024 * 1024


def dot(a, b):
    return jnp.dot(a, b, preferred_element_type=F32)


def dot_nt(a, b):
    return lax.dot_general(a, b, (((1,), (1,)), ((), ())), preferred_element_type=F32)


def dot_tn(a, b):
    return lax.dot_general(a, b, (((0,), (0,)), ((), ())), preferred_element_type=F32)


def row_scale(values):
    return lax.rsqrt(jnp.mean(values * values, axis=-1, keepdims=True) + EPS)


def iota(shape, axis):
    return lax.broadcasted_iota(jnp.int32, shape, axis)


def one_hot(matches):
    return jnp.where(matches, 1.0, 0.0).astype(BF16)


def head_parts(pair):
    lane = iota(pair.shape, 1)
    zero = jnp.zeros_like(pair)
    return jnp.where(lane < HEAD, pair, zero), jnp.where(lane >= HEAD, pair, zero)


def soft_probs(query, key, bias, causal):
    scores = dot_nt(query, key) * (HEAD**-0.5) + bias
    scores = jnp.where(causal, scores, -jnp.inf)
    raised = jnp.exp(scores - jnp.max(scores, axis=-1, keepdims=True))
    return raised / jnp.sum(raised, axis=-1, keepdims=True)


def assemble(place, parts, full):
    own, near, far = parts
    rows, piece = own.shape[0], near.shape[0]
    full[pl.ds(pl.multiple_of(place[0] * rows, rows), rows), :] = own[...]
    base = (1 - place[0]) * rows
    full[pl.ds(pl.multiple_of(base + place[1] * piece, piece), piece), :] = near[...]
    full[pl.ds(pl.multiple_of(base + (1 - place[1]) * piece, piece), piece), :] = far[...]


def merge(core, keep, arrived, own_small, other_small, out):
    out[...] = (keep[...].astype(F32) + arrived[...].astype(F32)).astype(BF16)
    rows, half, lanes = own_small.shape[1], keep.shape[0] // 2, keep.shape[1] - LANES

    @pl.when(core[0] == 1)
    def _():
        for share in range(2):
            out[share * half : share * half + rows, lanes:] = (
                own_small[share] + other_small[share]
            ).astype(BF16)


def finish(core, mine, other, qkv_out, out_out, rest_out):
    split, tail, width = mine.shape[1], qkv_out.shape[1] - mine.shape[1], out_out.shape[1]

    def fill(low, high):
        qkv_out[:, :split] = low[...]
        qkv_out[:, split:] = high[:, :tail]
        out_out[...] = high[:, tail : tail + width]
        rest_out[...] = high[:, tail + width :]

    @pl.when(core[0] == 0)
    def _():
        fill(mine, other)

    @pl.when(core[0] == 1)
    def _():
        fill(other, mine)


def mixer_forward(with_grads, *refs):
    if with_grads:
        x_ref, dy_ref, wqkv, wout, wr, gains, bias, srow, scol = refs[:9]
        send, hidden_out, gates_out, proj, mixed, norm1_out, norm2_out = refs[9:]
    else:
        place, x_ref = refs[:2]
        parts, (wr, gains, bias, srow, scol) = refs[2:8], refs[8:13]
        send, hidden_out, gates_out, wqkv, wout, proj, mixed = refs[13:]
        assemble(place, parts[:3], wqkv)
        assemble(place, parts[3:], wout)
    tokens, width = x_ref.shape
    x = x_ref[...].astype(F32)
    norm1 = (x * row_scale(x) * gains[0:1, :]).astype(BF16)
    proj[...] = dot(norm1, wqkv[...]).astype(BF16)
    causal = iota((tokens, tokens), 1) <= iota((tokens, tokens), 0)
    for pair in range(width // LANES):
        at = pair * LANES
        queries = head_parts(proj[:, at : at + LANES])
        key = proj[:, width + at : width + at + LANES]
        values = head_parts(proj[:, 2 * width + at : 2 * width + at + LANES])
        total = None
        for half in range(2):
            probs = soft_probs(queries[half], key, bias[2 * pair + half], causal).astype(BF16)
            part = dot(probs, values[half])
            total = part if total is None else total + part
        mixed[:, at : at + LANES] = total.astype(BF16)
    hidden = x + dot(mixed[...], wout[...])
    hidden_out[...] = hidden
    norm2 = (hidden * row_scale(hidden) * gains[1:2, :]).astype(BF16)
    logits = dot(norm2, wr[...])
    lane = iota((tokens, LANES), 1)
    first = jnp.sum(jnp.where(lane == scol[:, 2:3], logits, 0.0), axis=1, keepdims=True)
    second = jnp.sum(jnp.where(lane == scol[:, 3:4], logits, 0.0), axis=1, keepdims=True)
    top = jnp.maximum(first, second)
    first = jnp.exp(first - top)
    second = jnp.exp(second - top)
    gate0 = first / (first + second)
    gate1 = second / (first + second)
    gates_out[...] = jnp.where(lane == 0, gate0, jnp.where(lane == 1, gate1, 0.0))
    slot = iota((send.shape[0], tokens), 0)
    hits0 = slot == srow[0:1, :]
    hits1 = slot == srow[1:2, :]
    send[:, :width] = dot(one_hot(hits0 | hits1), norm2).astype(BF16)
    if with_grads:
        dy = dy_ref[...].astype(F32)
        send[:, width:] = (
            dot(one_hot(hits0), (gate0 * dy).astype(BF16))
            + dot(one_hot(hits1), (gate1 * dy).astype(BF16))
        ).astype(BF16)
        norm1_out[...] = norm1
        norm2_out[...] = norm2


def grads_out(dy_ref, gates, srow, send):
    tokens = dy_ref.shape[0]
    dy = dy_ref[...].astype(F32)
    slot = iota((send.shape[0], tokens), 0)
    send[...] = (
        dot(one_hot(slot == srow[0:1, :]), (gates[:, 0:1] * dy).astype(BF16))
        + dot(one_hot(slot == srow[1:2, :]), (gates[:, 1:2] * dy).astype(BF16))
    ).astype(BF16)


def combine(back, hidden, gates, scol, out):
    tokens = hidden.shape[0]
    slot = iota((tokens, back.shape[0]), 1)
    result0 = dot(one_hot(slot == scol[:, 0:1]), back[...])
    result1 = dot(one_hot(slot == scol[:, 1:2]), back[...])
    out[...] = (hidden[...] + gates[:, 0:1] * result0 + gates[:, 1:2] * result1).astype(BF16)


def bell(pre):
    return 0.5 * (1.0 + lax.erf(pre * 0.7071067811865476))


def grow(total, step, part):
    total[...] = jnp.where(step == 0, part, total[...] + part)


def experts_forward(rows, up, down, out, total):
    step = pl.program_id(0)
    pre = dot(rows[...], up[...])
    grow(total, step, dot((pre * bell(pre)).astype(BF16), down[...]))

    @pl.when(step == pl.num_programs(0) - 1)
    def _():
        out[...] = total[...].astype(BF16)


def experts_both(rows, up, down, out, act_out, slope_out, total, total_back):
    step = pl.program_id(0)
    width = up.shape[0]
    pre = dot(rows[:, :width], up[...])
    lower = bell(pre)
    act = (pre * lower).astype(BF16)
    slope = lower + pre * jnp.exp(-0.5 * pre * pre) * 0.3989422804014327
    act_out[...] = act
    slope_out[...] = slope.astype(BF16)
    pre_grads = (dot_nt(rows[:, width:], down[...]) * slope).astype(BF16)
    grow(total, step, dot(act, down[...]))
    grow(total_back, step, dot_nt(pre_grads, up[...]))

    @pl.when(step == pl.num_programs(0) - 1)
    def _():
        out[:, :width] = total[...].astype(BF16)
        out[:, width:] = total_back[...].astype(BF16)


def experts_backward(grads, up, down, slope, out, pre_out, total_back):
    step = pl.program_id(0)
    pre_grads = (dot_nt(grads[...], down[...]) * slope[...].astype(F32)).astype(BF16)
    pre_out[...] = pre_grads
    grow(total_back, step, dot_nt(pre_grads, up[...]))

    @pl.when(step == pl.num_programs(0) - 1)
    def _():
        out[...] = total_back[...].astype(BF16)


def mixer_backward(last, *refs):
    if last:
        (core, back, dy_ref, x_ref, res_in, wqkv, wout, wr, gains, bias, scol) = refs[:11]
        (hidden_ref, gates, proj, mixed, norm1, norm2) = refs[11:17]
        (input_grad, keep, give, stats, score_out, proj_grad) = refs[17:]
    else:
        (back, dy_ref, x_ref, wqkv, wout, wr, gains, bias, scol) = refs[:9]
        (hidden_ref, gates, proj) = refs[9:12]
        (input_grad, y_out, res_out, proj_grad) = refs[12:]
    tokens, width = x_ref.shape
    dy = dy_ref[...].astype(F32)
    hidden = hidden_ref[...]
    gate0 = gates[:, 0:1]
    gate1 = gates[:, 1:2]
    slot = iota((tokens, back.shape[0]), 1)
    hits0 = slot == scol[:, 0:1]
    hits1 = slot == scol[:, 1:2]
    if last:
        result0 = res_in[0].astype(F32)
        result1 = res_in[1].astype(F32)
        copy_rows = back[...]
    else:
        result0 = dot(one_hot(hits0), back[:, :width])
        result1 = dot(one_hot(hits1), back[:, :width])
        res_out[0] = result0.astype(BF16)
        res_out[1] = result1.astype(BF16)
        y_out[...] = (hidden + gate0 * result0 + gate1 * result1).astype(BF16)
        copy_rows = back[:, width:]
    gate_grad0 = jnp.sum(result0 * dy, axis=1, keepdims=True)
    gate_grad1 = jnp.sum(result1 * dy, axis=1, keepdims=True)
    inner = gate0 * gate_grad0 + gate1 * gate_grad1
    lane = iota((tokens, LANES), 1)
    logit_grads = (
        jnp.where(lane == scol[:, 2:3], gate0 * (gate_grad0 - inner), 0.0)
        + jnp.where(lane == scol[:, 3:4], gate1 * (gate_grad1 - inner), 0.0)
    ).astype(BF16)
    norm2_grads = dot(one_hot(hits0 | hits1), copy_rows) + dot_nt(logit_grads, wr[...])
    scale2 = row_scale(hidden)
    weighted = norm2_grads * gains[1:2, :]
    inner = jnp.mean(weighted * hidden, axis=-1, keepdims=True)
    hidden_grad = dy + scale2 * weighted - hidden * (scale2 * scale2 * scale2 * inner)
    branch = hidden_grad.astype(BF16)
    mixed_grad = dot_nt(branch, wout[...]).astype(BF16)
    causal = iota((tokens, tokens), 1) <= iota((tokens, tokens), 0)
    for pair in range(width // LANES):
        at = pair * LANES
        queries = head_parts(proj[:, at : at + LANES])
        key = proj[:, width + at : width + at + LANES]
        keys = head_parts(key)
        value = proj[:, 2 * width + at : 2 * width + at + LANES]
        outer = head_parts(mixed_grad[:, at : at + LANES])
        query_sum = key_sum = value_sum = None
        for half in range(2):
            probs = soft_probs(queries[half], key, bias[2 * pair + half], causal)
            prob_grad = dot_nt(outer[half], value)
            inner = jnp.sum(probs * prob_grad, axis=-1, keepdims=True)
            score_grad = (probs * (prob_grad - inner)).astype(BF16)
            if last:
                score_out[2 * pair + half] = score_grad
            query_part = dot(score_grad, keys[half])
            key_part = dot_tn(score_grad, queries[half])
            value_part = dot_tn(probs.astype(BF16), outer[half])
            query_sum = query_part if half == 0 else query_sum + query_part
            key_sum = key_part if half == 0 else key_sum + key_part
            value_sum = value_part if half == 0 else value_sum + value_part
        proj_grad[:, at : at + LANES] = (query_sum * HEAD**-0.5).astype(BF16)
        proj_grad[:, width + at : width + at + LANES] = (key_sum * HEAD**-0.5).astype(BF16)
        proj_grad[:, 2 * width + at : 2 * width + at + LANES] = value_sum.astype(BF16)
    norm1_grads = dot_nt(proj_grad[...], wqkv[...])
    x = x_ref[...].astype(F32)
    scale1 = row_scale(x)
    weighted = norm1_grads * gains[0:1, :]
    inner = jnp.mean(weighted * x, axis=-1, keepdims=True)
    input_grad[...] = (
        hidden_grad + scale1 * weighted - x * (scale1 * scale1 * scale1 * inner)
    ).astype(BF16)
    if last:
        stats[0:1, :] = jnp.sum(norm1_grads * x * scale1, axis=0, keepdims=True)
        stats[1:2, :] = jnp.sum(norm2_grads * hidden * scale2, axis=0, keepdims=True)
        stats[2:8, :] = jnp.zeros((6, width), F32)
        split = keep.shape[1]
        tail = 3 * width - split

        def fill(low, high):
            low[...] = dot_tn(norm1[...], proj_grad[:, :split]).astype(BF16)
            high[:, :tail] = dot_tn(norm1[...], proj_grad[:, split:]).astype(BF16)
            high[:, tail : tail + width] = dot_tn(mixed[...], branch).astype(BF16)
            high[:, tail + width : tail + width + LANES] = dot_tn(
                norm2[...], logit_grads
            ).astype(BF16)
            high[:, tail + width + LANES :] = jnp.zeros(
                (width, split - tail - width - LANES), BF16
            )

        @pl.when(core[0] == 0)
        def _():
            fill(keep, give)

        @pl.when(core[0] == 1)
        def _():
            fill(give, keep)


def shape_of(*dims, dtype=BF16):
    return jax.ShapeDtypeStruct(dims, dtype)


def whole(kernel, outs, operands, scratch=(), scalar=False, flops=0, name=None):
    vmem = pl.BlockSpec(memory_space=pltpu.VMEM)
    specs = [vmem] * len(operands)
    if scalar:
        specs[0] = pl.BlockSpec(memory_space=pltpu.SMEM)
    moved = sum(o.size * o.dtype.itemsize for o in list(operands) + list(outs))
    return pl.pallas_call(
        kernel,
        out_shape=outs,
        in_specs=specs,
        out_specs=[vmem] * len(outs),
        scratch_shapes=list(scratch),
        cost_estimate=pl.CostEstimate(flops=flops, bytes_accessed=moved, transcendentals=0),
        compiler_params=pltpu.CompilerParams(vmem_limit_bytes=VMEM_BYTES),
        name=name,
    )(*operands)


CHUNK = 768


def expert_call(kernel, rows, up, down, slope, wide_outs, out_cols, sums, name):
    count = rows.shape[0]
    width, hidden_units = up.shape
    specs = [
        pl.BlockSpec(rows.shape, lambda i: (0, 0)),
        pl.BlockSpec((width, CHUNK), lambda i: (0, i)),
        pl.BlockSpec((CHUNK, width), lambda i: (i, 0)),
    ]
    operands = [rows, up, down]
    per_chunk = pl.BlockSpec((count, CHUNK), lambda i: (0, i))
    if slope is not None:
        specs.append(per_chunk)
        operands.append(slope)
    outs = [shape_of(count, out_cols)] + [shape_of(count, hidden_units)] * wide_outs
    moved = sum(o.size * o.dtype.itemsize for o in operands + outs)
    return pl.pallas_call(
        kernel,
        out_shape=outs,
        grid=(hidden_units // CHUNK,),
        in_specs=specs,
        out_specs=[pl.BlockSpec((count, out_cols), lambda i: (0, 0))] + [per_chunk] * wide_outs,
        scratch_shapes=[pltpu.VMEM((count, width), F32)] * sums,
        cost_estimate=pl.CostEstimate(
            flops=4 * sums * count * width * hidden_units,
            bytes_accessed=moved,
            transcendentals=0,
        ),
        compiler_params=pltpu.CompilerParams(
            dimension_semantics=("arbitrary",), vmem_limit_bytes=VMEM_BYTES
        ),
        name=name,
    )(*operands)


def trade(rows):
    count, columns = rows.shape
    pieces = rows.reshape(count // SLOTS, SLOTS, columns)
    return lax.all_to_all(pieces, MEMBERS, 0, 0, tiled=True).reshape(count, columns)


def swap(value, axis):
    return lax.ppermute(value, axis, [(0, 1), (1, 0)])


def in_order(index, mine, other, axis):
    return jnp.where(
        index == 0,
        jnp.concatenate([mine, other], axis=axis),
        jnp.concatenate([other, mine], axis=axis),
    )


def with_other(half, piece):
    near = swap(piece, "shard")
    return half, near, swap(near, "core")


def local(
    boundary,
    routes,
    buckets,
    query_key_value_weight,
    attention_output_weight,
    w_router,
    gain_attn,
    gain_moe,
    bias_table,
    expert_in,
    expert_out,
):
    section = lax.axis_index("section")
    shard = lax.axis_index("shard")
    core = lax.axis_index("core")
    _, micro, _, positions, width = boundary.shape
    tokens = 2 * positions
    heads = bias_table.shape[2]
    bucket_count = 2 * bias_table.shape[1]
    experts = w_router.shape[2]
    half_width = width // 2
    count = experts * SLOTS

    own_rows = boundary.reshape(micro, positions, width)
    own_routes = routes.reshape(micro, positions, 2)
    up = expert_in[0, 0]
    down = expert_out[0, 0]

    def pick(stacked, index):
        return lax.dynamic_index_in_dim(stacked, index, 0, keepdims=False)

    qkv_half = query_key_value_weight[0]
    out_half = attention_output_weight[0]
    own_extra = jnp.concatenate(
        [
            w_router[0],
            gain_attn[0][:, None],
            gain_moe[0][:, None],
            jnp.pad(bias_table[0], ((0, half_width - bucket_count // 2), (0, 0))),
            jnp.zeros((half_width, LANES - experts - 2 - heads), BF16),
        ],
        axis=1,
    )
    numbers = jnp.concatenate(
        [buckets, jnp.pad(pick(own_routes, 1 - shard), ((0, 0), (0, LANES - 2)))], axis=1
    )
    far_rows = swap(pick(own_rows, 1 - shard), "shard")
    far_numbers = swap(numbers, "shard")
    far_extra = swap(own_extra, "shard")
    half_rows_each = half_width // 2
    qkv_piece = lax.dynamic_slice_in_dim(qkv_half, core * half_rows_each, half_rows_each, 0)
    out_piece = lax.dynamic_slice_in_dim(out_half, core * half_rows_each, half_rows_each, 0)
    far_rows, far_numbers, far_extra, qkv_piece, out_piece = lax.optimization_barrier(
        (far_rows, far_numbers, far_extra, qkv_piece, out_piece)
    )
    qkv_parts = with_other(qkv_half, qkv_piece)
    out_parts = with_other(out_half, out_piece)
    extra = in_order(shard, own_extra, far_extra, 0)
    gains = jnp.pad(extra[:, experts : experts + 2].T.astype(F32), ((0, 6), (0, 0)))
    table = jnp.concatenate(
        [
            extra[: bucket_count // 2, experts + 2 : experts + 2 + heads],
            extra[half_width : half_width + bucket_count // 2, experts + 2 : experts + 2 + heads],
        ],
        axis=0,
    )
    mine = in_order(shard, pick(own_rows, shard), far_rows, 0)
    pairs = in_order(
        shard, pick(own_routes, shard), far_numbers[:, 2 * positions : 2 * positions + 2], 0
    )
    bucket_full = in_order(shard, buckets, far_numbers[:, : 2 * positions], 0)
    bucket_hot = (
        bucket_full[None] == jnp.arange(bucket_count, dtype=jnp.int32)[:, None, None]
    ).astype(BF16)
    bias = jnp.einsum("bts,bh->hts", bucket_hot, table, preferred_element_type=F32)

    flat = pairs.reshape(-1)
    hits = (flat[:, None] == jnp.arange(experts, dtype=jnp.int32)[None, :]).astype(jnp.int32)
    ranks = jnp.sum(jnp.cumsum(hits, axis=0) * hits, axis=1) - 1
    slots = (flat * SLOTS + ranks).reshape(tokens, 2)
    srow = jnp.pad(slots.T, ((0, 6), (0, 0)))
    scol = jnp.pad(jnp.concatenate([slots, pairs], axis=1), ((0, 0), (0, LANES - 4)))

    mixer_flops = 2 * tokens * width * 4 * width
    forward_shapes = [
        shape_of(tokens, width, dtype=F32),
        shape_of(tokens, LANES, dtype=F32),
    ]
    place = jnp.stack([shard, core]).astype(jnp.int32)
    send, hidden, gates, wqkv, wout = whole(
        functools.partial(mixer_forward, False),
        [shape_of(count, width)]
        + forward_shapes
        + [shape_of(width, 3 * width), shape_of(width, width)],
        (place, mine) + qkv_parts + out_parts + (extra, gains, bias, srow, scol),
        scalar=True,
        scratch=[pltpu.VMEM((tokens, 3 * width), BF16), pltpu.VMEM((tokens, width), BF16)],
        flops=mixer_flops,
        name="mixer_forward",
    )
    (result_rows,) = expert_call(
        experts_forward, trade(send), up, down, None, 0, width, 1, "experts_forward"
    )
    (layer_out,) = whole(
        combine,
        [shape_of(tokens, width)],
        (trade(result_rows), hidden, gates, scol),
        name="combine",
    )
    arriving = lax.ppermute(layer_out, "section", [(0, 1)])
    layer_in = jnp.where(section == 0, mine, arriving)

    send, hidden, gates, proj, mixed, norm1, norm2 = whole(
        functools.partial(mixer_forward, True),
        [shape_of(count, 2 * width)]
        + forward_shapes
        + [
            shape_of(tokens, 3 * width),
            shape_of(tokens, width),
            shape_of(tokens, width),
            shape_of(tokens, width),
        ],
        (layer_in, mine, wqkv, wout, extra, gains, bias, srow, scol),
        flops=mixer_flops,
        name="mixer_forward_keep",
    )
    arrived = trade(send)
    both, act, slope = expert_call(
        experts_both, arrived, up, down, None, 2, 2 * width, 2, "experts_both"
    )
    input_grad, forward_rows, results = whole(
        functools.partial(mixer_backward, False),
        [
            shape_of(tokens, width),
            shape_of(tokens, width),
            shape_of(2, tokens, width),
        ],
        (trade(both), mine, layer_in, wqkv, wout, extra, gains, bias, scol, hidden, gates, proj),
        scratch=[pltpu.VMEM((tokens, 3 * width), BF16)],
        flops=2 * mixer_flops,
        name="mixer_backward",
    )
    arriving = lax.ppermute(input_grad, "section", [(1, 0)])
    grad_in = jnp.where(section == 0, arriving, mine)

    (send,) = whole(
        grads_out, [shape_of(count, width)], (grad_in, gates, srow), name="grads_out"
    )
    arrived_grads = trade(send)
    copy_rows, pre_grads = expert_call(
        experts_backward, arrived_grads, up, down, slope, 1, width, 1, "experts_backward"
    )
    returned = trade(copy_rows)
    split = 13 * LANES
    tail = 3 * width - split
    input_grad, keep, give, stats, score_grads = whole(
        functools.partial(mixer_backward, True),
        [
            shape_of(tokens, width),
            shape_of(width, split),
            shape_of(width, split),
            shape_of(8, width, dtype=F32),
            shape_of(heads, tokens, tokens),
        ],
        (
            core.reshape(1),
            returned,
            grad_in,
            layer_in,
            results,
            wqkv,
            wout,
            extra,
            gains,
            bias,
            scol,
            hidden,
            gates,
            proj,
            mixed,
            norm1,
            norm2,
        ),
        scratch=[pltpu.VMEM((tokens, 3 * width), BF16)],
        scalar=True,
        flops=3 * mixer_flops,
        name="mixer_backward_last",
    )

    finished = jnp.where(section == 0, input_grad, forward_rows).reshape(2, positions, width)
    from_other = swap(pick(finished, 1 - shard), "shard")
    boundary_out = jnp.stack(
        [
            jnp.where(shard == 0, pick(finished, shard), from_other),
            jnp.where(shard == 0, from_other, pick(finished, shard)),
        ]
    ).reshape(boundary.shape)

    table_grad = jnp.einsum(
        "bts,hts->bh", bucket_hot, score_grads, preferred_element_type=F32
    )
    half_rows = half_width // LANES
    table_rows = bucket_count // 2
    small = jnp.concatenate(
        [
            stats[0].reshape(2, half_rows, LANES),
            stats[1].reshape(2, half_rows, LANES),
            jnp.zeros((2, 8 - 2 * half_rows, LANES), F32),
            jnp.pad(
                table_grad.reshape(2, table_rows, heads), ((0, 0), (0, 0), (0, LANES - heads))
            ),
        ],
        axis=1,
    )
    small = jnp.pad(small, ((0, 0), (0, 32 - small.shape[1]), (0, 0)))
    (summed,) = whole(
        merge,
        [shape_of(width, split)],
        (core.reshape(1), keep, swap(give, "core"), small, swap(small, "core")),
        scalar=True,
        name="merge",
    )
    summed, arrived, arrived_grads, act, pre_grads = lax.optimization_barrier(
        (summed, arrived, arrived_grads, act, pre_grads)
    )
    d_expert_in = lax.dot_general(
        arrived[:, :width], pre_grads, (((0,), (0,)), ((), ())), preferred_element_type=F32
    ).astype(BF16)
    d_expert_out = lax.dot_general(
        act, arrived_grads, (((0,), (0,)), ((), ())), preferred_element_type=F32
    ).astype(BF16)
    gathered = lax.all_to_all(
        summed.reshape(32, width // 32, split), ("shard", "y", "z"), 0, 0, tiled=True
    )
    gathered, d_expert_in, d_expert_out = lax.optimization_barrier(
        (gathered, d_expert_in, d_expert_out)
    )
    piece = jnp.sum(gathered.astype(F32), axis=0).astype(BF16)
    spread = lax.all_to_all(
        jnp.broadcast_to(piece[None], (16,) + piece.shape), ("y", "z"), 0, 0, tiled=True
    ).reshape(half_width, split)
    qkv_sum, out_sum, rest = whole(
        finish,
        [
            shape_of(half_width, 3 * width),
            shape_of(half_width, width),
            shape_of(half_width, 2 * LANES),
        ],
        (core.reshape(1), spread, swap(spread, "core")),
        scalar=True,
        name="finish",
    )
    totals = rest[: 8 + table_rows, LANES:]
    gain_one_sum = totals[:half_rows].reshape(half_width)
    gain_two_sum = totals[half_rows : 2 * half_rows].reshape(half_width)
    table_sum = totals[8:, :heads]
    return (
        boundary_out,
        qkv_sum[None],
        out_sum[None],
        rest[:, :experts][None],
        gain_one_sum[None],
        gain_two_sum[None],
        table_sum[None],
        d_expert_in.reshape(expert_in.shape),
        d_expert_out.reshape(expert_out.shape),
    )


def solution(mesh):
    fine = Mesh(
        mesh.devices.reshape(2, 4, 4, 2, 2), ("section", "y", "z", "core", "shard")
    )
    expert = ("y", "z", "core")
    rows = P("section", None, expert, "shard", None)
    by_pair = P("section", "shard", None)
    by_expert = P("section", MEMBERS, None, None)
    in_specs = (
        rows,
        rows,
        P("shard", None),
        by_pair,
        by_pair,
        by_pair,
        P("section", "shard"),
        P("section", "shard"),
        by_pair,
        by_expert,
        by_expert,
    )
    out_specs = (
        rows,
        by_pair,
        by_pair,
        by_pair,
        P("section", "shard"),
        P("section", "shard"),
        by_pair,
        by_expert,
        by_expert,
    )
    return jax.shard_map(local, mesh=fine, in_specs=in_specs, out_specs=out_specs, check_vma=False)
```

```python
import functools

import jax
import jax.numpy as jnp
from jax import lax
from jax.experimental import pallas as pl
from jax.experimental.pallas import tpu as pltpu
from jax.sharding import Mesh
from jax.sharding import PartitionSpec as P

EPS = 1e-06
F32 = jnp.float32
BF16 = jnp.bfloat16
SLOTS = 8
LANES = 128
HEAD = 64
MEMBERS = ("y", "z", "core", "shard")
VMEM_BYTES = 50 * 1024 * 1024


def dot(a, b):
    return jnp.dot(a, b, preferred_element_type=F32)


def dot_nt(a, b):
    return lax.dot_general(a, b, (((1,), (1,)), ((), ())), preferred_element_type=F32)


def dot_tn(a, b):
    return lax.dot_general(a, b, (((0,), (0,)), ((), ())), preferred_element_type=F32)


def row_scale(values):
    return lax.rsqrt(jnp.mean(values * values, axis=-1, keepdims=True) + EPS)


def iota(shape, axis):
    return lax.broadcasted_iota(jnp.int32, shape, axis)


def one_hot(matches):
    return jnp.where(matches, 1.0, 0.0).astype(BF16)


def head_parts(pair):
    lane = iota(pair.shape, 1)
    zero = jnp.zeros_like(pair)
    return jnp.where(lane < HEAD, pair, zero), jnp.where(lane >= HEAD, pair, zero)


def soft_probs(query, key, bias, causal):
    scores = dot_nt(query, key) * (HEAD**-0.5) + bias
    scores = jnp.where(causal, scores, -jnp.inf)
    raised = jnp.exp(scores - jnp.max(scores, axis=-1, keepdims=True))
    return raised / jnp.sum(raised, axis=-1, keepdims=True)


def assemble(place, parts, wqkv, wout):
    qkv_own, out_own, near, far = parts
    rows, piece, split = qkv_own.shape[0], near.shape[0], qkv_own.shape[1]
    own_at = pl.ds(pl.multiple_of(place[0] * rows, rows), rows)
    base = (1 - place[0]) * rows
    near_at = pl.ds(pl.multiple_of(base + place[1] * piece, piece), piece)
    far_at = pl.ds(pl.multiple_of(base + (1 - place[1]) * piece, piece), piece)
    wqkv[own_at, :] = qkv_own[...]
    wqkv[near_at, :] = near[:, :split]
    wqkv[far_at, :] = far[:, :split]
    wout[own_at, :] = out_own[...]
    wout[near_at, :] = near[:, split:]
    wout[far_at, :] = far[:, split:]


def spread_bias(table, buckets, out):
    picked = buckets[...]
    heads = out.shape[0]
    count = table.shape[0] // heads
    for head in range(heads):
        values = jnp.zeros(picked.shape, F32)
        for bucket in range(count):
            values = jnp.where(picked == bucket, table[bucket * heads + head], values)
        out[head] = values


def merge(core, keep, arrived, own_small, other_small, out):
    out[...] = (keep[...].astype(F32) + arrived[...].astype(F32)).astype(BF16)
    rows, lanes = own_small.shape[1], keep.shape[1] - LANES
    step = pl.program_id(0)

    @pl.when((core[0] == 1) & (step % 2 == 0))
    def _():
        share = step // 2
        out[:rows, lanes:] = (own_small[share] + other_small[share]).astype(BF16)


def finish(core, mine, other, qkv_out, out_out, rest_out):
    split, tail, width = mine.shape[1], qkv_out.shape[1] - mine.shape[1], out_out.shape[1]

    def fill(low, high):
        qkv_out[:, :split] = low[...]
        qkv_out[:, split:] = high[:, :tail]
        out_out[...] = high[:, tail : tail + width]
        rest_out[...] = high[:, tail + width :]

    @pl.when(core[0] == 0)
    def _():
        fill(mine, other)

    @pl.when(core[0] == 1)
    def _():
        fill(other, mine)


def mixer_forward(with_grads, *refs):
    if with_grads:
        x_ref, dy_ref, wqkv, wout, wr, gains, bias, srow, scol = refs[:9]
        send, hidden_out, gates_out, proj, mixed, norm1_out, norm2_out = refs[9:]
    else:
        place, x_ref = refs[:2]
        parts, (wr, gains, bias, srow, scol) = refs[2:6], refs[6:11]
        send, hidden_out, gates_out, wqkv, wout, proj, mixed = refs[11:]
        assemble(place, parts, wqkv, wout)
    tokens, width = x_ref.shape
    x = x_ref[...].astype(F32)
    norm1 = (x * row_scale(x) * gains[0:1, :]).astype(BF16)
    proj[...] = dot(norm1, wqkv[...]).astype(BF16)
    causal = iota((tokens, tokens), 1) <= iota((tokens, tokens), 0)
    for pair in range(width // LANES):
        at = pair * LANES
        queries = head_parts(proj[:, at : at + LANES])
        key = proj[:, width + at : width + at + LANES]
        values = head_parts(proj[:, 2 * width + at : 2 * width + at + LANES])
        total = None
        for half in range(2):
            probs = soft_probs(queries[half], key, bias[2 * pair + half], causal).astype(BF16)
            part = dot(probs, values[half])
            total = part if total is None else total + part
        mixed[:, at : at + LANES] = total.astype(BF16)
    hidden = x + dot(mixed[...], wout[...])
    hidden_out[...] = hidden
    norm2 = (hidden * row_scale(hidden) * gains[1:2, :]).astype(BF16)
    logits = dot_nt(norm2, wr[...])
    lane = iota(logits.shape, 1)
    first = jnp.sum(jnp.where(lane == scol[:, 2:3], logits, 0.0), axis=1, keepdims=True)
    second = jnp.sum(jnp.where(lane == scol[:, 3:4], logits, 0.0), axis=1, keepdims=True)
    top = jnp.maximum(first, second)
    first = jnp.exp(first - top)
    second = jnp.exp(second - top)
    gate0 = first / (first + second)
    gate1 = second / (first + second)
    lane = iota((tokens, LANES), 1)
    gates_out[...] = jnp.where(lane == 0, gate0, jnp.where(lane == 1, gate1, 0.0))
    slot = iota((send.shape[0], tokens), 0)
    hits0 = slot == srow[0:1, :]
    hits1 = slot == srow[1:2, :]
    send[:, :width] = dot(one_hot(hits0 | hits1), norm2).astype(BF16)
    if with_grads:
        dy = dy_ref[...].astype(F32)
        send[:, width:] = (
            dot(one_hot(hits0), (gate0 * dy).astype(BF16))
            + dot(one_hot(hits1), (gate1 * dy).astype(BF16))
        ).astype(BF16)
        norm1_out[...] = norm1
        norm2_out[...] = norm2


def grads_out(dy_ref, gates, srow, send):
    tokens = dy_ref.shape[0]
    dy = dy_ref[...].astype(F32)
    slot = iota((send.shape[0], tokens), 0)
    send[...] = (
        dot(one_hot(slot == srow[0:1, :]), (gates[:, 0:1] * dy).astype(BF16))
        + dot(one_hot(slot == srow[1:2, :]), (gates[:, 1:2] * dy).astype(BF16))
    ).astype(BF16)


def combine(back, hidden, gates, scol, out):
    tokens = hidden.shape[0]
    slot = iota((tokens, back.shape[0]), 1)
    result0 = dot(one_hot(slot == scol[:, 0:1]), back[...])
    result1 = dot(one_hot(slot == scol[:, 1:2]), back[...])
    out[...] = (hidden[...] + gates[:, 0:1] * result0 + gates[:, 1:2] * result1).astype(BF16)


def bell(pre):
    return 0.5 * (1.0 + lax.erf(pre * 0.7071067811865476))


def grow(total, step, part):
    total[...] = jnp.where(step == 0, part, total[...] + part)


def experts_forward(rows, up, down, out, total):
    step = pl.program_id(0)
    pre = dot(rows[...], up[...])
    grow(total, step, dot((pre * bell(pre)).astype(BF16), down[...]))

    @pl.when(step == pl.num_programs(0) - 1)
    def _():
        out[...] = total[...].astype(BF16)


def experts_both(rows, up, down, out, act_out, slope_out, total, total_back):
    step = pl.program_id(0)
    width = up.shape[0]
    pre = dot(rows[:, :width], up[...])
    lower = bell(pre)
    act = (pre * lower).astype(BF16)
    slope = lower + pre * jnp.exp(-0.5 * pre * pre) * 0.3989422804014327
    act_out[...] = act
    slope_out[...] = slope.astype(BF16)
    pre_grads = (dot_nt(rows[:, width:], down[...]) * slope).astype(BF16)
    grow(total, step, dot(act, down[...]))
    grow(total_back, step, dot_nt(pre_grads, up[...]))

    @pl.when(step == pl.num_programs(0) - 1)
    def _():
        out[:, :width] = total[...].astype(BF16)
        out[:, width:] = total_back[...].astype(BF16)


def experts_backward(grads, up, down, slope, out, pre_out, total_back):
    step = pl.program_id(0)
    pre_grads = (dot_nt(grads[...], down[...]) * slope[...].astype(F32)).astype(BF16)
    pre_out[...] = pre_grads
    grow(total_back, step, dot_nt(pre_grads, up[...]))

    @pl.when(step == pl.num_programs(0) - 1)
    def _():
        out[...] = total_back[...].astype(BF16)


def mixer_backward(last, *refs):
    if last:
        (core, back, dy_ref, x_ref, res_in, wqkv, wout, wr, gains, bias, scol) = refs[:11]
        (hidden_ref, gates, proj, mixed, norm1, norm2) = refs[11:17]
        (input_grad, keep, give, stats, score_out, proj_grad) = refs[17:]
    else:
        (back, dy_ref, x_ref, wqkv, wout, wr, gains, bias, scol) = refs[:9]
        (hidden_ref, gates, proj) = refs[9:12]
        (input_grad, y_out, res_out, proj_grad) = refs[12:]
    tokens, width = x_ref.shape
    dy = dy_ref[...].astype(F32)
    hidden = hidden_ref[...]
    gate0 = gates[:, 0:1]
    gate1 = gates[:, 1:2]
    slot = iota((tokens, back.shape[0]), 1)
    hits0 = slot == scol[:, 0:1]
    hits1 = slot == scol[:, 1:2]
    if last:
        result0 = res_in[0].astype(F32)
        result1 = res_in[1].astype(F32)
        copy_rows = back[...]
    else:
        result0 = dot(one_hot(hits0), back[:, :width])
        result1 = dot(one_hot(hits1), back[:, :width])
        res_out[0] = result0.astype(BF16)
        res_out[1] = result1.astype(BF16)
        y_out[...] = (hidden + gate0 * result0 + gate1 * result1).astype(BF16)
        copy_rows = back[:, width:]
    gate_grad0 = jnp.sum(result0 * dy, axis=1, keepdims=True)
    gate_grad1 = jnp.sum(result1 * dy, axis=1, keepdims=True)
    inner = gate0 * gate_grad0 + gate1 * gate_grad1
    experts = wr.shape[0]
    lane = iota((tokens, experts), 1)
    logit_grads = (
        jnp.where(lane == scol[:, 2:3], gate0 * (gate_grad0 - inner), 0.0)
        + jnp.where(lane == scol[:, 3:4], gate1 * (gate_grad1 - inner), 0.0)
    ).astype(BF16)
    norm2_grads = dot(one_hot(hits0 | hits1), copy_rows) + dot(logit_grads, wr[...])
    scale2 = row_scale(hidden)
    weighted = norm2_grads * gains[1:2, :]
    inner = jnp.mean(weighted * hidden, axis=-1, keepdims=True)
    hidden_grad = dy + scale2 * weighted - hidden * (scale2 * scale2 * scale2 * inner)
    branch = hidden_grad.astype(BF16)
    mixed_grad = dot_nt(branch, wout[...]).astype(BF16)
    causal = iota((tokens, tokens), 1) <= iota((tokens, tokens), 0)
    for pair in range(width // LANES):
        at = pair * LANES
        queries = head_parts(proj[:, at : at + LANES])
        key = proj[:, width + at : width + at + LANES]
        keys = head_parts(key)
        value = proj[:, 2 * width + at : 2 * width + at + LANES]
        outer = head_parts(mixed_grad[:, at : at + LANES])
        query_sum = key_sum = value_sum = None
        for half in range(2):
            probs = soft_probs(queries[half], key, bias[2 * pair + half], causal)
            prob_grad = dot_nt(outer[half], value)
            inner = jnp.sum(probs * prob_grad, axis=-1, keepdims=True)
            score_grad = (probs * (prob_grad - inner)).astype(BF16)
            if last:
                score_out[2 * pair + half] = score_grad
            query_part = dot(score_grad, keys[half])
            key_part = dot_tn(score_grad, queries[half])
            value_part = dot_tn(probs.astype(BF16), outer[half])
            query_sum = query_part if half == 0 else query_sum + query_part
            key_sum = key_part if half == 0 else key_sum + key_part
            value_sum = value_part if half == 0 else value_sum + value_part
        proj_grad[:, at : at + LANES] = (query_sum * HEAD**-0.5).astype(BF16)
        proj_grad[:, width + at : width + at + LANES] = (key_sum * HEAD**-0.5).astype(BF16)
        proj_grad[:, 2 * width + at : 2 * width + at + LANES] = value_sum.astype(BF16)
    norm1_grads = dot_nt(proj_grad[...], wqkv[...])
    x = x_ref[...].astype(F32)
    scale1 = row_scale(x)
    weighted = norm1_grads * gains[0:1, :]
    inner = jnp.mean(weighted * x, axis=-1, keepdims=True)
    input_grad[...] = (
        hidden_grad + scale1 * weighted - x * (scale1 * scale1 * scale1 * inner)
    ).astype(BF16)
    if last:
        stats[0:1, :] = jnp.sum(norm1_grads * x * scale1, axis=0, keepdims=True)
        stats[1:2, :] = jnp.sum(norm2_grads * hidden * scale2, axis=0, keepdims=True)
        stats[2:8, :] = jnp.zeros((6, width), F32)
        split = keep.shape[1]
        tail = 3 * width - split

        def fill(low, high):
            low[...] = dot_tn(norm1[...], proj_grad[:, :split]).astype(BF16)
            high[:, :tail] = dot_tn(norm1[...], proj_grad[:, split:]).astype(BF16)
            high[:, tail : tail + width] = dot_tn(mixed[...], branch).astype(BF16)
            rest = tail + width
            high[:, rest : rest + experts] = dot_tn(norm2[...], logit_grads).astype(BF16)
            high[:, rest + experts :] = jnp.zeros((width, split - rest - experts), BF16)

        @pl.when(core[0] == 0)
        def _():
            fill(keep, give)

        @pl.when(core[0] == 1)
        def _():
            fill(give, keep)


def shape_of(*dims, dtype=BF16):
    return jax.ShapeDtypeStruct(dims, dtype)


def whole(kernel, outs, operands, scratch=(), scalar=False, flops=0, name=None):
    vmem = pl.BlockSpec(memory_space=pltpu.VMEM)
    specs = [vmem] * len(operands)
    if scalar:
        specs[0] = pl.BlockSpec(memory_space=pltpu.SMEM)
    moved = sum(o.size * o.dtype.itemsize for o in list(operands) + list(outs))
    return pl.pallas_call(
        kernel,
        out_shape=outs,
        in_specs=specs,
        out_specs=[vmem] * len(outs),
        scratch_shapes=list(scratch),
        cost_estimate=pl.CostEstimate(flops=flops, bytes_accessed=moved, transcendentals=0),
        compiler_params=pltpu.CompilerParams(vmem_limit_bytes=VMEM_BYTES),
        name=name,
    )(*operands)


CHUNK = 768


def expert_call(kernel, rows, up, down, slope, wide_outs, out_cols, sums, name):
    count = rows.shape[0]
    width, hidden_units = up.shape
    specs = [
        pl.BlockSpec(rows.shape, lambda i: (0, 0)),
        pl.BlockSpec((width, CHUNK), lambda i: (0, i)),
        pl.BlockSpec((CHUNK, width), lambda i: (i, 0)),
    ]
    operands = [rows, up, down]
    per_chunk = pl.BlockSpec((count, CHUNK), lambda i: (0, i))
    if slope is not None:
        specs.append(per_chunk)
        operands.append(slope)
    outs = [shape_of(count, out_cols)] + [shape_of(count, hidden_units)] * wide_outs
    moved = sum(o.size * o.dtype.itemsize for o in operands + outs)
    return pl.pallas_call(
        kernel,
        out_shape=outs,
        grid=(hidden_units // CHUNK,),
        in_specs=specs,
        out_specs=[pl.BlockSpec((count, out_cols), lambda i: (0, 0))] + [per_chunk] * wide_outs,
        scratch_shapes=[pltpu.VMEM((count, width), F32)] * sums,
        cost_estimate=pl.CostEstimate(
            flops=4 * sums * count * width * hidden_units,
            bytes_accessed=moved,
            transcendentals=0,
        ),
        compiler_params=pltpu.CompilerParams(
            dimension_semantics=("arbitrary",), vmem_limit_bytes=VMEM_BYTES
        ),
        name=name,
    )(*operands)


def trade(rows):
    count, columns = rows.shape
    pieces = rows.reshape(count // SLOTS, SLOTS, columns)
    return lax.all_to_all(pieces, MEMBERS, 0, 0, tiled=True).reshape(count, columns)


def swap(value, axis):
    return lax.ppermute(value, axis, [(0, 1), (1, 0)])


def in_order(index, mine, other, axis):
    return jnp.where(
        index == 0,
        jnp.concatenate([mine, other], axis=axis),
        jnp.concatenate([other, mine], axis=axis),
    )


def local(
    boundary,
    routes,
    buckets,
    query_key_value_weight,
    attention_output_weight,
    w_router,
    gain_attn,
    gain_moe,
    bias_table,
    expert_in,
    expert_out,
):
    section = lax.axis_index("section")
    shard = lax.axis_index("shard")
    core = lax.axis_index("core")
    _, micro, _, positions, width = boundary.shape
    tokens = 2 * positions
    heads = bias_table.shape[2]
    bucket_count = 2 * bias_table.shape[1]
    experts = w_router.shape[2]
    half_width = width // 2
    count = experts * SLOTS

    own_rows = boundary.reshape(micro, positions, width)
    own_routes = routes.reshape(micro, positions, 2)
    up = expert_in[0, 0]
    down = expert_out[0, 0]

    def pick(stacked, index):
        return lax.dynamic_index_in_dim(stacked, index, 0, keepdims=False)

    qkv_half = query_key_value_weight[0]
    out_half = attention_output_weight[0]
    table_rows = bucket_count // 2
    sent_routes = pick(own_routes, 1 - shard).astype(BF16).reshape(1, 2 * positions)
    own_small = jnp.concatenate(
        [
            w_router[0].T,
            gain_attn,
            gain_moe,
            jnp.zeros((5, half_width), BF16),
            jnp.pad(sent_routes, ((0, 0), (0, half_width - 2 * positions))),
            jnp.pad(bias_table[0], ((0, 0), (0, half_width - heads))),
        ],
        axis=0,
    )
    piece_rows = half_width // 2
    piece = jnp.concatenate(
        [
            lax.dynamic_slice_in_dim(qkv_half, core * piece_rows, piece_rows, 0),
            lax.dynamic_slice_in_dim(out_half, core * piece_rows, piece_rows, 0),
        ],
        axis=1,
    )
    far_rows = swap(pick(own_rows, 1 - shard), "shard")
    far_buckets = swap(buckets, "shard")
    far_small = swap(own_small, "shard")
    piece, far_rows, far_buckets, far_small = lax.optimization_barrier(
        (piece, far_rows, far_buckets, far_small)
    )
    near = swap(piece, "shard")
    gain_at, route_at, table_at = experts, experts + 7, experts + 8
    router = in_order(shard, own_small[:experts], far_small[:experts], 1)
    gains = in_order(
        shard, own_small[gain_at:table_at], far_small[gain_at:table_at], 1
    ).astype(F32)
    table = in_order(shard, own_small[table_at:, :heads], far_small[table_at:, :heads], 0)
    far_routes = far_small[route_at, : 2 * positions].astype(jnp.int32).reshape(positions, 2)
    mine = in_order(shard, pick(own_rows, shard), far_rows, 0)
    pairs = in_order(
        shard, pick(own_routes, shard), far_routes, 0
    )
    bucket_full = in_order(shard, buckets, far_buckets, 0)
    bucket_hot = (
        bucket_full[None] == jnp.arange(bucket_count, dtype=jnp.int32)[:, None, None]
    ).astype(BF16)
    (bias,) = whole(
        spread_bias,
        [shape_of(heads, tokens, tokens, dtype=F32)],
        (table.astype(F32).reshape(-1), bucket_full),
        scalar=True,
        name="spread_bias",
    )

    flat = pairs.reshape(-1)
    hits = (flat[:, None] == jnp.arange(experts, dtype=jnp.int32)[None, :]).astype(jnp.int32)
    ranks = jnp.sum(jnp.cumsum(hits, axis=0) * hits, axis=1) - 1
    slots = (flat * SLOTS + ranks).reshape(tokens, 2)
    srow = jnp.pad(slots.T, ((0, 6), (0, 0)))
    scol = jnp.pad(jnp.concatenate([slots, pairs], axis=1), ((0, 0), (0, LANES - 4)))

    mixer_flops = 2 * tokens * width * 4 * width
    forward_shapes = [
        shape_of(tokens, width, dtype=F32),
        shape_of(tokens, LANES, dtype=F32),
    ]
    place = jnp.stack([shard, core]).astype(jnp.int32)
    near, mine, router, gains, bias, bucket_hot, srow, scol = lax.optimization_barrier(
        (near, mine, router, gains, bias, bucket_hot, srow, scol)
    )
    weight_parts = (qkv_half, out_half, near, swap(near, "core"))
    send, hidden, gates, wqkv, wout = whole(
        functools.partial(mixer_forward, False),
        [shape_of(count, width)]
        + forward_shapes
        + [shape_of(width, 3 * width), shape_of(width, width)],
        (place, mine) + weight_parts + (router, gains, bias, srow, scol),
        scalar=True,
        scratch=[pltpu.VMEM((tokens, 3 * width), BF16), pltpu.VMEM((tokens, width), BF16)],
        flops=mixer_flops,
        name="mixer_forward",
    )
    (result_rows,) = expert_call(
        experts_forward, trade(send), up, down, None, 0, width, 1, "experts_forward"
    )
    (layer_out,) = whole(
        combine,
        [shape_of(tokens, width)],
        (trade(result_rows), hidden, gates, scol),
        name="combine",
    )
    arriving = lax.ppermute(layer_out, "section", [(0, 1)])
    layer_in = jnp.where(section == 0, mine, arriving)

    send, hidden, gates, proj, mixed, norm1, norm2 = whole(
        functools.partial(mixer_forward, True),
        [shape_of(count, 2 * width)]
        + forward_shapes
        + [
            shape_of(tokens, 3 * width),
            shape_of(tokens, width),
            shape_of(tokens, width),
            shape_of(tokens, width),
        ],
        (layer_in, mine, wqkv, wout, router, gains, bias, srow, scol),
        flops=mixer_flops,
        name="mixer_forward_keep",
    )
    arrived = trade(send)
    both, act, slope = expert_call(
        experts_both, arrived, up, down, None, 2, 2 * width, 2, "experts_both"
    )
    input_grad, forward_rows, results = whole(
        functools.partial(mixer_backward, False),
        [
            shape_of(tokens, width),
            shape_of(tokens, width),
            shape_of(2, tokens, width),
        ],
        (trade(both), mine, layer_in, wqkv, wout, router, gains, bias, scol, hidden, gates, proj),
        scratch=[pltpu.VMEM((tokens, 3 * width), BF16)],
        flops=2 * mixer_flops,
        name="mixer_backward",
    )
    arriving = lax.ppermute(input_grad, "section", [(1, 0)])
    grad_in = jnp.where(section == 0, arriving, mine)

    (send,) = whole(
        grads_out, [shape_of(count, width)], (grad_in, gates, srow), name="grads_out"
    )
    arrived_grads = trade(send)
    copy_rows, pre_grads = expert_call(
        experts_backward, arrived_grads, up, down, slope, 1, width, 1, "experts_backward"
    )
    returned = trade(copy_rows)
    split = 13 * LANES
    tail = 3 * width - split
    input_grad, keep, give, stats, score_grads = whole(
        functools.partial(mixer_backward, True),
        [
            shape_of(tokens, width),
            shape_of(width, split),
            shape_of(width, split),
            shape_of(8, width, dtype=F32),
            shape_of(heads, tokens, tokens),
        ],
        (
            core.reshape(1),
            returned,
            grad_in,
            layer_in,
            results,
            wqkv,
            wout,
            router,
            gains,
            bias,
            scol,
            hidden,
            gates,
            proj,
            mixed,
            norm1,
            norm2,
        ),
        scratch=[pltpu.VMEM((tokens, 3 * width), BF16)],
        scalar=True,
        flops=3 * mixer_flops,
        name="mixer_backward_last",
    )

    finished = jnp.where(section == 0, input_grad, forward_rows).reshape(2, positions, width)
    from_other = swap(pick(finished, 1 - shard), "shard")
    boundary_out = jnp.stack(
        [
            jnp.where(shard == 0, pick(finished, shard), from_other),
            jnp.where(shard == 0, from_other, pick(finished, shard)),
        ]
    ).reshape(boundary.shape)

    table_grad = jnp.einsum(
        "bts,hts->bh", bucket_hot, score_grads, preferred_element_type=F32
    )
    half_rows = half_width // LANES
    small = jnp.concatenate(
        [
            stats[0].reshape(2, half_rows, LANES),
            stats[1].reshape(2, half_rows, LANES),
            jnp.zeros((2, 8 - 2 * half_rows, LANES), F32),
            jnp.pad(
                table_grad.reshape(2, table_rows, heads), ((0, 0), (0, 0), (0, LANES - heads))
            ),
        ],
        axis=1,
    )
    small = jnp.pad(small, ((0, 0), (0, 32 - small.shape[1]), (0, 0)))
    block = pl.BlockSpec((width // 4, split), lambda i: (i, 0))
    whole_small = pl.BlockSpec(small.shape, lambda i: (0, 0, 0))
    summed = pl.pallas_call(
        merge,
        out_shape=shape_of(width, split),
        grid=(4,),
        in_specs=[
            pl.BlockSpec(memory_space=pltpu.SMEM),
            block,
            block,
            whole_small,
            whole_small,
        ],
        out_specs=block,
        compiler_params=pltpu.CompilerParams(vmem_limit_bytes=VMEM_BYTES),
        name="merge",
    )(core.reshape(1), keep, swap(give, "core"), small, swap(small, "core"))
    summed, arrived, arrived_grads, act, pre_grads = lax.optimization_barrier(
        (summed, arrived, arrived_grads, act, pre_grads)
    )
    d_expert_in = lax.dot_general(
        arrived[:, :width], pre_grads, (((0,), (0,)), ((), ())), preferred_element_type=F32
    ).astype(BF16)
    d_expert_out = lax.dot_general(
        act, arrived_grads, (((0,), (0,)), ((), ())), preferred_element_type=F32
    ).astype(BF16)
    gathered = lax.all_to_all(
        summed.reshape(32, width // 32, split), ("shard", "y", "z"), 0, 0, tiled=True
    )
    gathered, d_expert_in, d_expert_out, boundary_out = lax.optimization_barrier(
        (gathered, d_expert_in, d_expert_out, boundary_out)
    )
    piece = jnp.sum(gathered.astype(F32), axis=0).astype(BF16)
    spread = lax.all_to_all(
        jnp.broadcast_to(piece[None], (16,) + piece.shape), ("y", "z"), 0, 0, tiled=True
    ).reshape(half_width, split)
    qkv_sum, out_sum, rest = whole(
        finish,
        [
            shape_of(half_width, 3 * width),
            shape_of(half_width, width),
            shape_of(half_width, 2 * LANES),
        ],
        (core.reshape(1), spread, swap(spread, "core")),
        scalar=True,
        name="finish",
    )
    totals = rest[: 8 + table_rows, LANES:]
    gain_one_sum = totals[:half_rows].reshape(half_width)
    gain_two_sum = totals[half_rows : 2 * half_rows].reshape(half_width)
    table_sum = totals[8:, :heads]
    return (
        boundary_out,
        qkv_sum[None],
        out_sum[None],
        rest[:, :experts][None],
        gain_one_sum[None],
        gain_two_sum[None],
        table_sum[None],
        d_expert_in.reshape(expert_in.shape),
        d_expert_out.reshape(expert_out.shape),
    )


def solution(mesh):
    fine = Mesh(
        mesh.devices.reshape(2, 4, 4, 2, 2), ("section", "y", "z", "core", "shard")
    )
    expert = ("y", "z", "core")
    rows = P("section", None, expert, "shard", None)
    by_pair = P("section", "shard", None)
    by_expert = P("section", MEMBERS, None, None)
    in_specs = (
        rows,
        rows,
        P("shard", None),
        by_pair,
        by_pair,
        by_pair,
        P("section", "shard"),
        P("section", "shard"),
        by_pair,
        by_expert,
        by_expert,
    )
    out_specs = (
        rows,
        by_pair,
        by_pair,
        by_pair,
        P("section", "shard"),
        P("section", "shard"),
        by_pair,
        by_expert,
        by_expert,
    )
    return jax.shard_map(local, mesh=fine, in_specs=in_specs, out_specs=out_specs, check_vma=False)
```

```python
import functools

import jax
import jax.numpy as jnp
from jax import lax
from jax.experimental import pallas as pl
from jax.experimental.pallas import tpu as pltpu
from jax.sharding import Mesh
from jax.sharding import PartitionSpec as P

EPS = 1e-06
F32 = jnp.float32
BF16 = jnp.bfloat16
SLOTS = 8
LANES = 128
HEAD = 64
MEMBERS = ("y", "z", "core", "shard")
VMEM_BYTES = 50 * 1024 * 1024


def dot(a, b):
    return jnp.dot(a, b, preferred_element_type=F32)


def dot_nt(a, b):
    return lax.dot_general(a, b, (((1,), (1,)), ((), ())), preferred_element_type=F32)


def dot_tn(a, b):
    return lax.dot_general(a, b, (((0,), (0,)), ((), ())), preferred_element_type=F32)


def row_scale(values):
    return lax.rsqrt(jnp.mean(values * values, axis=-1, keepdims=True) + EPS)


def iota(shape, axis):
    return lax.broadcasted_iota(jnp.int32, shape, axis)


def one_hot(matches):
    return jnp.where(matches, 1.0, 0.0).astype(BF16)


def stack_heads(pair):
    lane = iota(pair.shape, 1)
    zero = jnp.zeros_like(pair)
    return jnp.concatenate(
        [jnp.where(lane < HEAD, pair, zero), jnp.where(lane >= HEAD, pair, zero)], axis=0
    )


def join_heads(stacked):
    rows = stacked.shape[0] // 2
    return jnp.where(iota((rows, LANES), 1) < HEAD, stacked[:rows], stacked[rows:])


def seen(tokens):
    shape = (2 * tokens, tokens)
    row = iota(shape, 0)
    return iota(shape, 1) <= jnp.where(row < tokens, row, row - tokens)


def soft_probs(queries, key, bias, causal):
    scores = dot_nt(queries, key) * (HEAD**-0.5) + bias
    scores = jnp.where(causal, scores, -jnp.inf)
    raised = jnp.exp(scores - jnp.max(scores, axis=-1, keepdims=True))
    return raised / jnp.sum(raised, axis=-1, keepdims=True)


def assemble(place, parts, wqkv, wout):
    qkv_own, out_own, near, far = parts
    rows, piece, split = qkv_own.shape[0], near.shape[0], qkv_own.shape[1]
    own_at = pl.ds(pl.multiple_of(place[0] * rows, rows), rows)
    base = (1 - place[0]) * rows
    near_at = pl.ds(pl.multiple_of(base + place[1] * piece, piece), piece)
    far_at = pl.ds(pl.multiple_of(base + (1 - place[1]) * piece, piece), piece)
    wqkv[own_at, :] = qkv_own[...]
    wqkv[near_at, :] = near[:, :split]
    wqkv[far_at, :] = far[:, :split]
    wout[own_at, :] = out_own[...]
    wout[near_at, :] = near[:, split:]
    wout[far_at, :] = far[:, split:]


def spread_bias(table, buckets, out):
    picked = buckets[...]
    tokens = picked.shape[0]
    heads = out.shape[0] // tokens
    count = table.shape[0] // heads
    for head in range(heads):
        values = jnp.zeros(picked.shape, F32)
        for bucket in range(count):
            values = jnp.where(picked == bucket, table[bucket * heads + head], values)
        out[head * tokens : (head + 1) * tokens, :] = values


def merge(core, keep, arrived, own_small, other_small, out):
    out[...] = (keep[...].astype(F32) + arrived[...].astype(F32)).astype(BF16)
    rows, lanes = own_small.shape[1], keep.shape[1] - LANES
    step = pl.program_id(0)

    @pl.when((core[0] == 1) & (step % 2 == 0))
    def _():
        share = step // 2
        out[:rows, lanes:] = (own_small[share] + other_small[share]).astype(BF16)


def finish(core, mine, other, qkv_out, out_out, rest_out):
    split, tail, width = mine.shape[1], qkv_out.shape[1] - mine.shape[1], out_out.shape[1]

    def fill(low, high):
        qkv_out[:, :split] = low[...]
        qkv_out[:, split:] = high[:, :tail]
        out_out[...] = high[:, tail : tail + width]
        rest_out[...] = high[:, tail + width :]

    @pl.when(core[0] == 0)
    def _():
        fill(mine, other)

    @pl.when(core[0] == 1)
    def _():
        fill(other, mine)


def mixer_forward(with_grads, *refs):
    if with_grads:
        x_ref, dy_ref, wqkv, wout, wr, gains, bias, srow, scol = refs[:9]
        send, hidden_out, gates_out, proj, mixed, norm1_out, norm2_out = refs[9:]
    else:
        place, x_ref = refs[:2]
        parts, (wr, gains, bias, srow, scol) = refs[2:6], refs[6:11]
        send, hidden_out, gates_out, wqkv, wout, proj, mixed = refs[11:]
        assemble(place, parts, wqkv, wout)
    tokens, width = x_ref.shape
    x = x_ref[...].astype(F32)
    norm1 = (x * row_scale(x) * gains[0:1, :]).astype(BF16)
    proj[...] = dot(norm1, wqkv[...]).astype(BF16)
    causal = seen(tokens)
    for pair in range(width // LANES):
        at = pair * LANES
        queries = stack_heads(proj[:, at : at + LANES])
        key = proj[:, width + at : width + at + LANES]
        value = proj[:, 2 * width + at : 2 * width + at + LANES]
        rows = slice(2 * pair * tokens, 2 * (pair + 1) * tokens)
        probs = soft_probs(queries, key, bias[rows, :], causal).astype(BF16)
        mixed[:, at : at + LANES] = join_heads(dot(probs, value)).astype(BF16)
    hidden = x + dot(mixed[...], wout[...])
    hidden_out[...] = hidden
    norm2 = (hidden * row_scale(hidden) * gains[1:2, :]).astype(BF16)
    logits = dot_nt(norm2, wr[...])
    lane = iota(logits.shape, 1)
    first = jnp.sum(jnp.where(lane == scol[:, 2:3], logits, 0.0), axis=1, keepdims=True)
    second = jnp.sum(jnp.where(lane == scol[:, 3:4], logits, 0.0), axis=1, keepdims=True)
    top = jnp.maximum(first, second)
    first = jnp.exp(first - top)
    second = jnp.exp(second - top)
    gate0 = first / (first + second)
    gate1 = second / (first + second)
    lane = iota((tokens, LANES), 1)
    gates_out[...] = jnp.where(lane == 0, gate0, jnp.where(lane == 1, gate1, 0.0))
    slot = iota((send.shape[0], tokens), 0)
    hits0 = slot == srow[0:1, :]
    hits1 = slot == srow[1:2, :]
    send[:, :width] = dot(one_hot(hits0 | hits1), norm2).astype(BF16)
    if with_grads:
        dy = dy_ref[...].astype(F32)
        send[:, width:] = (
            dot(one_hot(hits0), (gate0 * dy).astype(BF16))
            + dot(one_hot(hits1), (gate1 * dy).astype(BF16))
        ).astype(BF16)
        norm1_out[...] = norm1
        norm2_out[...] = norm2


def grads_out(dy_ref, gates, srow, send):
    tokens = dy_ref.shape[0]
    dy = dy_ref[...].astype(F32)
    slot = iota((send.shape[0], tokens), 0)
    send[...] = (
        dot(one_hot(slot == srow[0:1, :]), (gates[:, 0:1] * dy).astype(BF16))
        + dot(one_hot(slot == srow[1:2, :]), (gates[:, 1:2] * dy).astype(BF16))
    ).astype(BF16)


def combine(back, hidden, gates, scol, out):
    tokens = hidden.shape[0]
    slot = iota((tokens, back.shape[0]), 1)
    result0 = dot(one_hot(slot == scol[:, 0:1]), back[...])
    result1 = dot(one_hot(slot == scol[:, 1:2]), back[...])
    out[...] = (hidden[...] + gates[:, 0:1] * result0 + gates[:, 1:2] * result1).astype(BF16)


def bell(pre):
    return 0.5 * (1.0 + lax.erf(pre * 0.7071067811865476))


def grow(total, step, part):
    total[...] = jnp.where(step == 0, part, total[...] + part)


def experts_forward(rows, up, down, out, total):
    step = pl.program_id(0)
    pre = dot(rows[...], up[...])
    grow(total, step, dot((pre * bell(pre)).astype(BF16), down[...]))

    @pl.when(step == pl.num_programs(0) - 1)
    def _():
        out[...] = total[...].astype(BF16)


def experts_both(rows, up, down, out, act_out, slope_out, total, total_back):
    step = pl.program_id(0)
    width = up.shape[0]
    pre = dot(rows[:, :width], up[...])
    lower = bell(pre)
    act = (pre * lower).astype(BF16)
    slope = lower + pre * jnp.exp(-0.5 * pre * pre) * 0.3989422804014327
    act_out[...] = act
    slope_out[...] = slope.astype(BF16)
    pre_grads = (dot_nt(rows[:, width:], down[...]) * slope).astype(BF16)
    grow(total, step, dot(act, down[...]))
    grow(total_back, step, dot_nt(pre_grads, up[...]))

    @pl.when(step == pl.num_programs(0) - 1)
    def _():
        out[:, :width] = total[...].astype(BF16)
        out[:, width:] = total_back[...].astype(BF16)


def experts_backward(grads, up, down, slope, out, pre_out, total_back):
    step = pl.program_id(0)
    pre_grads = (dot_nt(grads[...], down[...]) * slope[...].astype(F32)).astype(BF16)
    pre_out[...] = pre_grads
    grow(total_back, step, dot_nt(pre_grads, up[...]))

    @pl.when(step == pl.num_programs(0) - 1)
    def _():
        out[...] = total_back[...].astype(BF16)


def mixer_backward(last, *refs):
    if last:
        (core, back, dy_ref, x_ref, res_in, wqkv, wout, wr, gains, bias, scol) = refs[:11]
        (hidden_ref, gates, proj, mixed, norm1, norm2) = refs[11:17]
        (input_grad, keep, give, stats, score_out, proj_grad) = refs[17:]
    else:
        (back, dy_ref, x_ref, wqkv, wout, wr, gains, bias, scol) = refs[:9]
        (hidden_ref, gates, proj) = refs[9:12]
        (input_grad, y_out, res_out, proj_grad) = refs[12:]
    tokens, width = x_ref.shape
    dy = dy_ref[...].astype(F32)
    hidden = hidden_ref[...]
    gate0 = gates[:, 0:1]
    gate1 = gates[:, 1:2]
    slot = iota((tokens, back.shape[0]), 1)
    hits0 = slot == scol[:, 0:1]
    hits1 = slot == scol[:, 1:2]
    if last:
        result0 = res_in[0].astype(F32)
        result1 = res_in[1].astype(F32)
        copy_rows = back[...]
    else:
        result0 = dot(one_hot(hits0), back[:, :width])
        result1 = dot(one_hot(hits1), back[:, :width])
        res_out[0] = result0.astype(BF16)
        res_out[1] = result1.astype(BF16)
        y_out[...] = (hidden + gate0 * result0 + gate1 * result1).astype(BF16)
        copy_rows = back[:, width:]
    gate_grad0 = jnp.sum(result0 * dy, axis=1, keepdims=True)
    gate_grad1 = jnp.sum(result1 * dy, axis=1, keepdims=True)
    inner = gate0 * gate_grad0 + gate1 * gate_grad1
    experts = wr.shape[0]
    lane = iota((tokens, experts), 1)
    logit_grads = (
        jnp.where(lane == scol[:, 2:3], gate0 * (gate_grad0 - inner), 0.0)
        + jnp.where(lane == scol[:, 3:4], gate1 * (gate_grad1 - inner), 0.0)
    ).astype(BF16)
    norm2_grads = dot(one_hot(hits0 | hits1), copy_rows) + dot(logit_grads, wr[...])
    scale2 = row_scale(hidden)
    weighted = norm2_grads * gains[1:2, :]
    inner = jnp.mean(weighted * hidden, axis=-1, keepdims=True)
    hidden_grad = dy + scale2 * weighted - hidden * (scale2 * scale2 * scale2 * inner)
    branch = hidden_grad.astype(BF16)
    mixed_grad = dot_nt(branch, wout[...]).astype(BF16)
    causal = seen(tokens)
    for pair in range(width // LANES):
        at = pair * LANES
        queries = stack_heads(proj[:, at : at + LANES])
        key = proj[:, width + at : width + at + LANES]
        value = proj[:, 2 * width + at : 2 * width + at + LANES]
        outer = stack_heads(mixed_grad[:, at : at + LANES])
        rows = slice(2 * pair * tokens, 2 * (pair + 1) * tokens)
        probs = soft_probs(queries, key, bias[rows, :], causal)
        prob_grad = dot_nt(outer, value)
        inner = jnp.sum(probs * prob_grad, axis=-1, keepdims=True)
        score_grad = (probs * (prob_grad - inner)).astype(BF16)
        if last:
            score_out[rows, :] = score_grad
        query_grad = join_heads(dot(score_grad, key)) * HEAD**-0.5
        key_grad = dot_tn(score_grad, queries) * HEAD**-0.5
        proj_grad[:, at : at + LANES] = query_grad.astype(BF16)
        proj_grad[:, width + at : width + at + LANES] = key_grad.astype(BF16)
        proj_grad[:, 2 * width + at : 2 * width + at + LANES] = dot_tn(
            probs.astype(BF16), outer
        ).astype(BF16)
    norm1_grads = dot_nt(proj_grad[...], wqkv[...])
    x = x_ref[...].astype(F32)
    scale1 = row_scale(x)
    weighted = norm1_grads * gains[0:1, :]
    inner = jnp.mean(weighted * x, axis=-1, keepdims=True)
    input_grad[...] = (
        hidden_grad + scale1 * weighted - x * (scale1 * scale1 * scale1 * inner)
    ).astype(BF16)
    if last:
        stats[0:1, :] = jnp.sum(norm1_grads * x * scale1, axis=0, keepdims=True)
        stats[1:2, :] = jnp.sum(norm2_grads * hidden * scale2, axis=0, keepdims=True)
        stats[2:8, :] = jnp.zeros((6, width), F32)
        split = keep.shape[1]
        tail = 3 * width - split

        def fill(low, high):
            low[...] = dot_tn(norm1[...], proj_grad[:, :split]).astype(BF16)
            high[:, :tail] = dot_tn(norm1[...], proj_grad[:, split:]).astype(BF16)
            high[:, tail : tail + width] = dot_tn(mixed[...], branch).astype(BF16)
            rest = tail + width
            high[:, rest : rest + experts] = dot_tn(norm2[...], logit_grads).astype(BF16)
            high[:, rest + experts :] = jnp.zeros((width, split - rest - experts), BF16)

        @pl.when(core[0] == 0)
        def _():
            fill(keep, give)

        @pl.when(core[0] == 1)
        def _():
            fill(give, keep)


def shape_of(*dims, dtype=BF16):
    return jax.ShapeDtypeStruct(dims, dtype)


def whole(kernel, outs, operands, scratch=(), scalar=False, flops=0, name=None):
    vmem = pl.BlockSpec(memory_space=pltpu.VMEM)
    specs = [vmem] * len(operands)
    if scalar:
        specs[0] = pl.BlockSpec(memory_space=pltpu.SMEM)
    moved = sum(o.size * o.dtype.itemsize for o in list(operands) + list(outs))
    return pl.pallas_call(
        kernel,
        out_shape=outs,
        in_specs=specs,
        out_specs=[vmem] * len(outs),
        scratch_shapes=list(scratch),
        cost_estimate=pl.CostEstimate(flops=flops, bytes_accessed=moved, transcendentals=0),
        compiler_params=pltpu.CompilerParams(vmem_limit_bytes=VMEM_BYTES),
        name=name,
    )(*operands)


CHUNK = 768


def expert_call(kernel, rows, up, down, slope, wide_outs, out_cols, sums, name):
    count = rows.shape[0]
    width, hidden_units = up.shape
    specs = [
        pl.BlockSpec(rows.shape, lambda i: (0, 0)),
        pl.BlockSpec((width, CHUNK), lambda i: (0, i)),
        pl.BlockSpec((CHUNK, width), lambda i: (i, 0)),
    ]
    operands = [rows, up, down]
    per_chunk = pl.BlockSpec((count, CHUNK), lambda i: (0, i))
    if slope is not None:
        specs.append(per_chunk)
        operands.append(slope)
    outs = [shape_of(count, out_cols)] + [shape_of(count, hidden_units)] * wide_outs
    moved = sum(o.size * o.dtype.itemsize for o in operands + outs)
    return pl.pallas_call(
        kernel,
        out_shape=outs,
        grid=(hidden_units // CHUNK,),
        in_specs=specs,
        out_specs=[pl.BlockSpec((count, out_cols), lambda i: (0, 0))] + [per_chunk] * wide_outs,
        scratch_shapes=[pltpu.VMEM((count, width), F32)] * sums,
        cost_estimate=pl.CostEstimate(
            flops=4 * sums * count * width * hidden_units,
            bytes_accessed=moved,
            transcendentals=0,
        ),
        compiler_params=pltpu.CompilerParams(
            dimension_semantics=("arbitrary",), vmem_limit_bytes=VMEM_BYTES
        ),
        name=name,
    )(*operands)


def trade(rows):
    count, columns = rows.shape
    pieces = rows.reshape(count // SLOTS, SLOTS, columns)
    return lax.all_to_all(pieces, MEMBERS, 0, 0, tiled=True).reshape(count, columns)


def swap(value, axis):
    return lax.ppermute(value, axis, [(0, 1), (1, 0)])


def in_order(index, mine, other, axis):
    return jnp.where(
        index == 0,
        jnp.concatenate([mine, other], axis=axis),
        jnp.concatenate([other, mine], axis=axis),
    )


def local(
    boundary,
    routes,
    buckets,
    query_key_value_weight,
    attention_output_weight,
    w_router,
    gain_attn,
    gain_moe,
    bias_table,
    expert_in,
    expert_out,
):
    section = lax.axis_index("section")
    shard = lax.axis_index("shard")
    core = lax.axis_index("core")
    _, micro, _, positions, width = boundary.shape
    tokens = 2 * positions
    heads = bias_table.shape[2]
    bucket_count = 2 * bias_table.shape[1]
    experts = w_router.shape[2]
    half_width = width // 2
    count = experts * SLOTS

    own_rows = boundary.reshape(micro, positions, width)
    own_routes = routes.reshape(micro, positions, 2)
    up = expert_in[0, 0]
    down = expert_out[0, 0]

    def pick(stacked, index):
        return lax.dynamic_index_in_dim(stacked, index, 0, keepdims=False)

    qkv_half = query_key_value_weight[0]
    out_half = attention_output_weight[0]
    table_rows = bucket_count // 2
    sent_routes = pick(own_routes, 1 - shard).astype(BF16).reshape(1, 2 * positions)
    own_small = jnp.concatenate(
        [
            w_router[0].T,
            gain_attn,
            gain_moe,
            jnp.zeros((5, half_width), BF16),
            jnp.pad(sent_routes, ((0, 0), (0, half_width - 2 * positions))),
            jnp.pad(bias_table[0], ((0, 0), (0, half_width - heads))),
        ],
        axis=0,
    )
    piece_rows = half_width // 2
    piece = jnp.concatenate(
        [
            lax.dynamic_slice_in_dim(qkv_half, core * piece_rows, piece_rows, 0),
            lax.dynamic_slice_in_dim(out_half, core * piece_rows, piece_rows, 0),
        ],
        axis=1,
    )
    far_rows = swap(pick(own_rows, 1 - shard), "shard")
    far_buckets = swap(buckets, "shard")
    far_small = swap(own_small, "shard")
    piece, far_rows, far_buckets, far_small = lax.optimization_barrier(
        (piece, far_rows, far_buckets, far_small)
    )
    near = swap(piece, "shard")
    gain_at, route_at, table_at = experts, experts + 7, experts + 8
    router = in_order(shard, own_small[:experts], far_small[:experts], 1)
    gains = in_order(
        shard, own_small[gain_at:table_at], far_small[gain_at:table_at], 1
    ).astype(F32)
    table = in_order(shard, own_small[table_at:, :heads], far_small[table_at:, :heads], 0)
    far_routes = far_small[route_at, : 2 * positions].astype(jnp.int32).reshape(positions, 2)
    mine = in_order(shard, pick(own_rows, shard), far_rows, 0)
    pairs = in_order(
        shard, pick(own_routes, shard), far_routes, 0
    )
    bucket_full = in_order(shard, buckets, far_buckets, 0)
    bucket_hot = (
        bucket_full[None] == jnp.arange(bucket_count, dtype=jnp.int32)[:, None, None]
    ).astype(BF16)
    (bias,) = whole(
        spread_bias,
        [shape_of(heads * tokens, tokens, dtype=F32)],
        (table.astype(F32).reshape(-1), bucket_full),
        scalar=True,
        name="spread_bias",
    )

    flat = pairs.reshape(-1)
    hits = (flat[:, None] == jnp.arange(experts, dtype=jnp.int32)[None, :]).astype(jnp.int32)
    ranks = jnp.sum(jnp.cumsum(hits, axis=0) * hits, axis=1) - 1
    slots = (flat * SLOTS + ranks).reshape(tokens, 2)
    srow = jnp.pad(slots.T, ((0, 6), (0, 0)))
    scol = jnp.pad(jnp.concatenate([slots, pairs], axis=1), ((0, 0), (0, LANES - 4)))

    mixer_flops = 2 * tokens * width * 4 * width
    forward_shapes = [
        shape_of(tokens, width, dtype=F32),
        shape_of(tokens, LANES, dtype=F32),
    ]
    place = jnp.stack([shard, core]).astype(jnp.int32)
    near, mine, router, gains, bias, bucket_hot, srow, scol = lax.optimization_barrier(
        (near, mine, router, gains, bias, bucket_hot, srow, scol)
    )
    weight_parts = (qkv_half, out_half, near, swap(near, "core"))
    send, hidden, gates, wqkv, wout = whole(
        functools.partial(mixer_forward, False),
        [shape_of(count, width)]
        + forward_shapes
        + [shape_of(width, 3 * width), shape_of(width, width)],
        (place, mine) + weight_parts + (router, gains, bias, srow, scol),
        scalar=True,
        scratch=[pltpu.VMEM((tokens, 3 * width), BF16), pltpu.VMEM((tokens, width), BF16)],
        flops=mixer_flops,
        name="mixer_forward",
    )
    (result_rows,) = expert_call(
        experts_forward, trade(send), up, down, None, 0, width, 1, "experts_forward"
    )
    (layer_out,) = whole(
        combine,
        [shape_of(tokens, width)],
        (trade(result_rows), hidden, gates, scol),
        name="combine",
    )
    arriving = lax.ppermute(layer_out, "section", [(0, 1)])
    layer_in = jnp.where(section == 0, mine, arriving)

    send, hidden, gates, proj, mixed, norm1, norm2 = whole(
        functools.partial(mixer_forward, True),
        [shape_of(count, 2 * width)]
        + forward_shapes
        + [
            shape_of(tokens, 3 * width),
            shape_of(tokens, width),
            shape_of(tokens, width),
            shape_of(tokens, width),
        ],
        (layer_in, mine, wqkv, wout, router, gains, bias, srow, scol),
        flops=mixer_flops,
        name="mixer_forward_keep",
    )
    arrived = trade(send)
    both, act, slope = expert_call(
        experts_both, arrived, up, down, None, 2, 2 * width, 2, "experts_both"
    )
    input_grad, forward_rows, results = whole(
        functools.partial(mixer_backward, False),
        [
            shape_of(tokens, width),
            shape_of(tokens, width),
            shape_of(2, tokens, width),
        ],
        (trade(both), mine, layer_in, wqkv, wout, router, gains, bias, scol, hidden, gates, proj),
        scratch=[pltpu.VMEM((tokens, 3 * width), BF16)],
        flops=2 * mixer_flops,
        name="mixer_backward",
    )
    arriving = lax.ppermute(input_grad, "section", [(1, 0)])
    grad_in = jnp.where(section == 0, arriving, mine)

    (send,) = whole(
        grads_out, [shape_of(count, width)], (grad_in, gates, srow), name="grads_out"
    )
    arrived_grads = trade(send)
    copy_rows, pre_grads = expert_call(
        experts_backward, arrived_grads, up, down, slope, 1, width, 1, "experts_backward"
    )
    returned = trade(copy_rows)
    split = 13 * LANES
    tail = 3 * width - split
    input_grad, keep, give, stats, score_grads = whole(
        functools.partial(mixer_backward, True),
        [
            shape_of(tokens, width),
            shape_of(width, split),
            shape_of(width, split),
            shape_of(8, width, dtype=F32),
            shape_of(heads * tokens, tokens),
        ],
        (
            core.reshape(1),
            returned,
            grad_in,
            layer_in,
            results,
            wqkv,
            wout,
            router,
            gains,
            bias,
            scol,
            hidden,
            gates,
            proj,
            mixed,
            norm1,
            norm2,
        ),
        scratch=[pltpu.VMEM((tokens, 3 * width), BF16)],
        scalar=True,
        flops=3 * mixer_flops,
        name="mixer_backward_last",
    )

    finished = jnp.where(section == 0, input_grad, forward_rows).reshape(2, positions, width)
    from_other = swap(pick(finished, 1 - shard), "shard")
    boundary_out = jnp.stack(
        [
            jnp.where(shard == 0, pick(finished, shard), from_other),
            jnp.where(shard == 0, from_other, pick(finished, shard)),
        ]
    ).reshape(boundary.shape)

    table_grad = jnp.einsum(
        "bts,hts->bh",
        bucket_hot,
        score_grads.reshape(heads, tokens, tokens),
        preferred_element_type=F32
    )
    half_rows = half_width // LANES
    small = jnp.concatenate(
        [
            stats[0].reshape(2, half_rows, LANES),
            stats[1].reshape(2, half_rows, LANES),
            jnp.zeros((2, 8 - 2 * half_rows, LANES), F32),
            jnp.pad(
                table_grad.reshape(2, table_rows, heads), ((0, 0), (0, 0), (0, LANES - heads))
            ),
        ],
        axis=1,
    )
    small = jnp.pad(small, ((0, 0), (0, 32 - small.shape[1]), (0, 0)))
    block = pl.BlockSpec((width // 4, split), lambda i: (i, 0))
    whole_small = pl.BlockSpec(small.shape, lambda i: (0, 0, 0))
    summed = pl.pallas_call(
        merge,
        out_shape=shape_of(width, split),
        grid=(4,),
        in_specs=[
            pl.BlockSpec(memory_space=pltpu.SMEM),
            block,
            block,
            whole_small,
            whole_small,
        ],
        out_specs=block,
        compiler_params=pltpu.CompilerParams(vmem_limit_bytes=VMEM_BYTES),
        name="merge",
    )(core.reshape(1), keep, swap(give, "core"), small, swap(small, "core"))
    summed, arrived, arrived_grads, act, pre_grads, boundary_out = lax.optimization_barrier(
        (summed, arrived, arrived_grads, act, pre_grads, boundary_out)
    )
    d_expert_in = lax.dot_general(
        arrived[:, :width], pre_grads, (((0,), (0,)), ((), ())), preferred_element_type=F32
    ).astype(BF16)
    d_expert_out = lax.dot_general(
        act, arrived_grads, (((0,), (0,)), ((), ())), preferred_element_type=F32
    ).astype(BF16)
    gathered = lax.all_to_all(
        summed.reshape(32, width // 32, split), ("shard", "y", "z"), 0, 0, tiled=True
    )
    gathered, d_expert_in, d_expert_out = lax.optimization_barrier(
        (gathered, d_expert_in, d_expert_out)
    )
    piece = jnp.sum(gathered.astype(F32), axis=0).astype(BF16)
    spread = lax.all_to_all(
        jnp.broadcast_to(piece[None], (16,) + piece.shape), ("y", "z"), 0, 0, tiled=True
    ).reshape(half_width, split)
    qkv_sum, out_sum, rest = whole(
        finish,
        [
            shape_of(half_width, 3 * width),
            shape_of(half_width, width),
            shape_of(half_width, 2 * LANES),
        ],
        (core.reshape(1), spread, swap(spread, "core")),
        scalar=True,
        name="finish",
    )
    totals = rest[: 8 + table_rows, LANES:]
    gain_one_sum = totals[:half_rows].reshape(half_width)
    gain_two_sum = totals[half_rows : 2 * half_rows].reshape(half_width)
    table_sum = totals[8:, :heads]
    return (
        boundary_out,
        qkv_sum[None],
        out_sum[None],
        rest[:, :experts][None],
        gain_one_sum[None],
        gain_two_sum[None],
        table_sum[None],
        d_expert_in.reshape(expert_in.shape),
        d_expert_out.reshape(expert_out.shape),
    )


def solution(mesh):
    fine = Mesh(
        mesh.devices.reshape(2, 4, 4, 2, 2), ("section", "y", "z", "core", "shard")
    )
    expert = ("y", "z", "core")
    rows = P("section", None, expert, "shard", None)
    by_pair = P("section", "shard", None)
    by_expert = P("section", MEMBERS, None, None)
    in_specs = (
        rows,
        rows,
        P("shard", None),
        by_pair,
        by_pair,
        by_pair,
        P("section", "shard"),
        P("section", "shard"),
        by_pair,
        by_expert,
        by_expert,
    )
    out_specs = (
        rows,
        by_pair,
        by_pair,
        by_pair,
        P("section", "shard"),
        P("section", "shard"),
        by_pair,
        by_expert,
        by_expert,
    )
    return jax.shard_map(local, mesh=fine, in_specs=in_specs, out_specs=out_specs, check_vma=False)
```

```python
import functools

import jax
import jax.numpy as jnp
from jax import lax
from jax.experimental import pallas as pl
from jax.experimental.pallas import tpu as pltpu
from jax.sharding import Mesh
from jax.sharding import PartitionSpec as P

EPS = 1e-06
F32 = jnp.float32
BF16 = jnp.bfloat16
SLOTS = 8
LANES = 128
HEAD = 64
MEMBERS = ("y", "z", "core", "shard")
VMEM_BYTES = 22 * 1024 * 1024


def dot(a, b):
    return jnp.dot(a, b, preferred_element_type=F32)


def dot_nt(a, b):
    return lax.dot_general(a, b, (((1,), (1,)), ((), ())), preferred_element_type=F32)


def dot_tn(a, b):
    return lax.dot_general(a, b, (((0,), (0,)), ((), ())), preferred_element_type=F32)


def row_scale(values):
    return lax.rsqrt(jnp.mean(values * values, axis=-1, keepdims=True) + EPS)


def iota(shape, axis):
    return lax.broadcasted_iota(jnp.int32, shape, axis)


def one_hot(matches):
    return jnp.where(matches, 1.0, 0.0).astype(BF16)


def stack_heads(pair):
    lane = iota(pair.shape, 1)
    zero = jnp.zeros_like(pair)
    return jnp.concatenate(
        [jnp.where(lane < HEAD, pair, zero), jnp.where(lane >= HEAD, pair, zero)], axis=0
    )


def join_heads(stacked):
    rows = stacked.shape[0] // 2
    return jnp.where(iota((rows, LANES), 1) < HEAD, stacked[:rows], stacked[rows:])


def seen(tokens):
    shape = (2 * tokens, tokens)
    row = iota(shape, 0)
    return iota(shape, 1) <= jnp.where(row < tokens, row, row - tokens)


def soft_probs(queries, key, bias, causal):
    scores = dot_nt(queries, key) * (HEAD**-0.5) + bias
    scores = jnp.where(causal, scores, -jnp.inf)
    raised = jnp.exp(scores - jnp.max(scores, axis=-1, keepdims=True))
    return raised / jnp.sum(raised, axis=-1, keepdims=True)


def assemble(place, parts, wqkv, wout):
    qkv_own, out_own, near, far = parts
    rows, piece, split = qkv_own.shape[0], near.shape[0], qkv_own.shape[1]
    own_at = pl.ds(pl.multiple_of(place[0] * rows, rows), rows)
    base = (1 - place[0]) * rows
    near_at = pl.ds(pl.multiple_of(base + place[1] * piece, piece), piece)
    far_at = pl.ds(pl.multiple_of(base + (1 - place[1]) * piece, piece), piece)
    wqkv[own_at, :] = qkv_own[...]
    wqkv[near_at, :] = near[:, :split]
    wqkv[far_at, :] = far[:, :split]
    wout[own_at, :] = out_own[...]
    wout[near_at, :] = near[:, split:]
    wout[far_at, :] = far[:, split:]


def spread_bias(table, buckets, out):
    picked = buckets[...]
    tokens = picked.shape[0]
    heads = out.shape[0] // tokens
    count = table.shape[0] // heads
    for head in range(heads):
        values = jnp.zeros(picked.shape, F32)
        for bucket in range(count):
            values = jnp.where(picked == bucket, table[bucket * heads + head], values)
        out[head * tokens : (head + 1) * tokens, :] = values


def merge(core, keep, arrived, own_small, other_small, out):
    out[...] = (keep[...].astype(F32) + arrived[...].astype(F32)).astype(BF16)
    rows, lanes = own_small.shape[1], keep.shape[1] - LANES
    step = pl.program_id(0)

    @pl.when((core[0] == 1) & (step % 2 == 0))
    def _():
        share = step // 2
        out[:rows, lanes:] = (own_small[share] + other_small[share]).astype(BF16)


def finish(core, mine, other, qkv_out, out_out, rest_out):
    split, tail, width = mine.shape[1], qkv_out.shape[1] - mine.shape[1], out_out.shape[1]

    def fill(low, high):
        qkv_out[:, :split] = low[...]
        qkv_out[:, split:] = high[:, :tail]
        out_out[...] = high[:, tail : tail + width]
        rest_out[...] = high[:, tail + width :]

    @pl.when(core[0] == 0)
    def _():
        fill(mine, other)

    @pl.when(core[0] == 1)
    def _():
        fill(other, mine)


def mixer_forward(with_grads, *refs):
    if with_grads:
        x_ref, dy_ref, wqkv, wout, wr, gains, bias, srow, scol = refs[:9]
        send, hidden_out, gates_out, proj, mixed, norm1_out, norm2_out = refs[9:]
    else:
        place, x_ref = refs[:2]
        parts, (wr, gains, bias, srow, scol) = refs[2:6], refs[6:11]
        send, hidden_out, gates_out, wqkv, wout, proj, mixed = refs[11:]
        assemble(place, parts, wqkv, wout)
    tokens, width = x_ref.shape
    x = x_ref[...].astype(F32)
    norm1 = (x * row_scale(x) * gains[0:1, :]).astype(BF16)
    proj[...] = dot(norm1, wqkv[...]).astype(BF16)
    causal = seen(tokens)
    for pair in range(width // LANES):
        at = pair * LANES
        queries = stack_heads(proj[:, at : at + LANES])
        key = proj[:, width + at : width + at + LANES]
        value = proj[:, 2 * width + at : 2 * width + at + LANES]
        rows = slice(2 * pair * tokens, 2 * (pair + 1) * tokens)
        probs = soft_probs(queries, key, bias[rows, :], causal).astype(BF16)
        mixed[:, at : at + LANES] = join_heads(dot(probs, value)).astype(BF16)
    hidden = x + dot(mixed[...], wout[...])
    hidden_out[...] = hidden
    norm2 = (hidden * row_scale(hidden) * gains[1:2, :]).astype(BF16)
    logits = dot_nt(norm2, wr[...])
    lane = iota(logits.shape, 1)
    first = jnp.sum(jnp.where(lane == scol[:, 2:3], logits, 0.0), axis=1, keepdims=True)
    second = jnp.sum(jnp.where(lane == scol[:, 3:4], logits, 0.0), axis=1, keepdims=True)
    top = jnp.maximum(first, second)
    first = jnp.exp(first - top)
    second = jnp.exp(second - top)
    gate0 = first / (first + second)
    gate1 = second / (first + second)
    lane = iota((tokens, LANES), 1)
    gates_out[...] = jnp.where(lane == 0, gate0, jnp.where(lane == 1, gate1, 0.0))
    slot = iota((send.shape[0], tokens), 0)
    hits0 = slot == srow[0:1, :]
    hits1 = slot == srow[1:2, :]
    send[:, :width] = dot(one_hot(hits0 | hits1), norm2).astype(BF16)
    if with_grads:
        dy = dy_ref[...].astype(F32)
        send[:, width:] = (
            dot(one_hot(hits0), (gate0 * dy).astype(BF16))
            + dot(one_hot(hits1), (gate1 * dy).astype(BF16))
        ).astype(BF16)
        norm1_out[...] = norm1
        norm2_out[...] = norm2


def grads_out(dy_ref, gates, srow, send):
    tokens = dy_ref.shape[0]
    dy = dy_ref[...].astype(F32)
    slot = iota((send.shape[0], tokens), 0)
    send[...] = (
        dot(one_hot(slot == srow[0:1, :]), (gates[:, 0:1] * dy).astype(BF16))
        + dot(one_hot(slot == srow[1:2, :]), (gates[:, 1:2] * dy).astype(BF16))
    ).astype(BF16)


def combine(back, hidden, gates, scol, out):
    tokens = hidden.shape[0]
    slot = iota((tokens, back.shape[0]), 1)
    result0 = dot(one_hot(slot == scol[:, 0:1]), back[...])
    result1 = dot(one_hot(slot == scol[:, 1:2]), back[...])
    out[...] = (hidden[...] + gates[:, 0:1] * result0 + gates[:, 1:2] * result1).astype(BF16)


def bell(pre):
    return 0.5 * (1.0 + lax.erf(pre * 0.7071067811865476))


def grow(total, step, part):
    total[...] = jnp.where(step == 0, part, total[...] + part)


def experts_forward(rows, up, down, out, total):
    step = pl.program_id(0)
    pre = dot(rows[...], up[...])
    grow(total, step, dot((pre * bell(pre)).astype(BF16), down[...]))

    @pl.when(step == pl.num_programs(0) - 1)
    def _():
        out[...] = total[...].astype(BF16)


def experts_both(rows, up, down, out, act_out, slope_out, total, total_back):
    step = pl.program_id(0)
    width = up.shape[0]
    pre = dot(rows[:, :width], up[...])
    lower = bell(pre)
    act = (pre * lower).astype(BF16)
    slope = lower + pre * jnp.exp(-0.5 * pre * pre) * 0.3989422804014327
    act_out[...] = act
    slope_out[...] = slope.astype(BF16)
    pre_grads = (dot_nt(rows[:, width:], down[...]) * slope).astype(BF16)
    grow(total, step, dot(act, down[...]))
    grow(total_back, step, dot_nt(pre_grads, up[...]))

    @pl.when(step == pl.num_programs(0) - 1)
    def _():
        out[:, :width] = total[...].astype(BF16)
        out[:, width:] = total_back[...].astype(BF16)


def experts_backward(grads, up, down, slope, out, pre_out, total_back):
    step = pl.program_id(0)
    pre_grads = (dot_nt(grads[...], down[...]) * slope[...].astype(F32)).astype(BF16)
    pre_out[...] = pre_grads
    grow(total_back, step, dot_nt(pre_grads, up[...]))

    @pl.when(step == pl.num_programs(0) - 1)
    def _():
        out[...] = total_back[...].astype(BF16)


def mixer_backward(last, *refs):
    if last:
        (core, back, dy_ref, x_ref, res_in, wqkv, wout, wr, gains, bias, scol) = refs[:11]
        (hidden_ref, gates, proj, mixed, norm1, norm2) = refs[11:17]
        (input_grad, keep, give, stats, score_out, proj_grad) = refs[17:]
    else:
        (back, dy_ref, x_ref, wqkv, wout, wr, gains, bias, scol) = refs[:9]
        (hidden_ref, gates, proj) = refs[9:12]
        (input_grad, y_out, res_out, proj_grad) = refs[12:]
    tokens, width = x_ref.shape
    dy = dy_ref[...].astype(F32)
    hidden = hidden_ref[...]
    gate0 = gates[:, 0:1]
    gate1 = gates[:, 1:2]
    slot = iota((tokens, back.shape[0]), 1)
    hits0 = slot == scol[:, 0:1]
    hits1 = slot == scol[:, 1:2]
    if last:
        result0 = res_in[0].astype(F32)
        result1 = res_in[1].astype(F32)
        copy_rows = back[...]
    else:
        result0 = dot(one_hot(hits0), back[:, :width])
        result1 = dot(one_hot(hits1), back[:, :width])
        res_out[0] = result0.astype(BF16)
        res_out[1] = result1.astype(BF16)
        y_out[...] = (hidden + gate0 * result0 + gate1 * result1).astype(BF16)
        copy_rows = back[:, width:]
    gate_grad0 = jnp.sum(result0 * dy, axis=1, keepdims=True)
    gate_grad1 = jnp.sum(result1 * dy, axis=1, keepdims=True)
    inner = gate0 * gate_grad0 + gate1 * gate_grad1
    experts = wr.shape[0]
    lane = iota((tokens, experts), 1)
    logit_grads = (
        jnp.where(lane == scol[:, 2:3], gate0 * (gate_grad0 - inner), 0.0)
        + jnp.where(lane == scol[:, 3:4], gate1 * (gate_grad1 - inner), 0.0)
    ).astype(BF16)
    norm2_grads = dot(one_hot(hits0 | hits1), copy_rows) + dot(logit_grads, wr[...])
    scale2 = row_scale(hidden)
    weighted = norm2_grads * gains[1:2, :]
    inner = jnp.mean(weighted * hidden, axis=-1, keepdims=True)
    hidden_grad = dy + scale2 * weighted - hidden * (scale2 * scale2 * scale2 * inner)
    branch = hidden_grad.astype(BF16)
    mixed_grad = dot_nt(branch, wout[...]).astype(BF16)
    causal = seen(tokens)
    for pair in range(width // LANES):
        at = pair * LANES
        queries = stack_heads(proj[:, at : at + LANES])
        key = proj[:, width + at : width + at + LANES]
        value = proj[:, 2 * width + at : 2 * width + at + LANES]
        outer = stack_heads(mixed_grad[:, at : at + LANES])
        rows = slice(2 * pair * tokens, 2 * (pair + 1) * tokens)
        probs = soft_probs(queries, key, bias[rows, :], causal)
        prob_grad = dot_nt(outer, value)
        inner = jnp.sum(probs * prob_grad, axis=-1, keepdims=True)
        score_grad = (probs * (prob_grad - inner)).astype(BF16)
        if last:
            score_out[rows, :] = score_grad
        query_grad = join_heads(dot(score_grad, key)) * HEAD**-0.5
        key_grad = dot_tn(score_grad, queries) * HEAD**-0.5
        proj_grad[:, at : at + LANES] = query_grad.astype(BF16)
        proj_grad[:, width + at : width + at + LANES] = key_grad.astype(BF16)
        proj_grad[:, 2 * width + at : 2 * width + at + LANES] = dot_tn(
            probs.astype(BF16), outer
        ).astype(BF16)
    norm1_grads = dot_nt(proj_grad[...], wqkv[...])
    x = x_ref[...].astype(F32)
    scale1 = row_scale(x)
    weighted = norm1_grads * gains[0:1, :]
    inner = jnp.mean(weighted * x, axis=-1, keepdims=True)
    input_grad[...] = (
        hidden_grad + scale1 * weighted - x * (scale1 * scale1 * scale1 * inner)
    ).astype(BF16)
    if last:
        stats[0:1, :] = jnp.sum(norm1_grads * x * scale1, axis=0, keepdims=True)
        stats[1:2, :] = jnp.sum(norm2_grads * hidden * scale2, axis=0, keepdims=True)
        stats[2:8, :] = jnp.zeros((6, width), F32)
        split = keep.shape[1]
        tail = 3 * width - split

        def fill(low, high):
            low[...] = dot_tn(norm1[...], proj_grad[:, :split]).astype(BF16)
            high[:, :tail] = dot_tn(norm1[...], proj_grad[:, split:]).astype(BF16)
            high[:, tail : tail + width] = dot_tn(mixed[...], branch).astype(BF16)
            rest = tail + width
            high[:, rest : rest + experts] = dot_tn(norm2[...], logit_grads).astype(BF16)
            high[:, rest + experts :] = jnp.zeros((width, split - rest - experts), BF16)

        @pl.when(core[0] == 0)
        def _():
            fill(keep, give)

        @pl.when(core[0] == 1)
        def _():
            fill(give, keep)


def shape_of(*dims, dtype=BF16):
    return jax.ShapeDtypeStruct(dims, dtype)


def whole(kernel, outs, operands, scratch=(), scalar=False, flops=0, name=None):
    vmem = pl.BlockSpec(memory_space=pltpu.VMEM)
    specs = [vmem] * len(operands)
    if scalar:
        specs[0] = pl.BlockSpec(memory_space=pltpu.SMEM)
    moved = sum(o.size * o.dtype.itemsize for o in list(operands) + list(outs))
    return pl.pallas_call(
        kernel,
        out_shape=outs,
        in_specs=specs,
        out_specs=[vmem] * len(outs),
        scratch_shapes=list(scratch),
        cost_estimate=pl.CostEstimate(flops=flops, bytes_accessed=moved, transcendentals=0),
        compiler_params=pltpu.CompilerParams(vmem_limit_bytes=VMEM_BYTES),
        name=name,
    )(*operands)


CHUNK = 768


def expert_call(kernel, rows, up, down, slope, wide_outs, out_cols, sums, name):
    count = rows.shape[0]
    width, hidden_units = up.shape
    specs = [
        pl.BlockSpec(rows.shape, lambda i: (0, 0)),
        pl.BlockSpec((width, CHUNK), lambda i: (0, i)),
        pl.BlockSpec((CHUNK, width), lambda i: (i, 0)),
    ]
    operands = [rows, up, down]
    per_chunk = pl.BlockSpec((count, CHUNK), lambda i: (0, i))
    if slope is not None:
        specs.append(per_chunk)
        operands.append(slope)
    outs = [shape_of(count, out_cols)] + [shape_of(count, hidden_units)] * wide_outs
    moved = sum(o.size * o.dtype.itemsize for o in operands + outs)
    return pl.pallas_call(
        kernel,
        out_shape=outs,
        grid=(hidden_units // CHUNK,),
        in_specs=specs,
        out_specs=[pl.BlockSpec((count, out_cols), lambda i: (0, 0))] + [per_chunk] * wide_outs,
        scratch_shapes=[pltpu.VMEM((count, width), F32)] * sums,
        cost_estimate=pl.CostEstimate(
            flops=4 * sums * count * width * hidden_units,
            bytes_accessed=moved,
            transcendentals=0,
        ),
        compiler_params=pltpu.CompilerParams(
            dimension_semantics=("arbitrary",), vmem_limit_bytes=VMEM_BYTES
        ),
        name=name,
    )(*operands)


def copy_block(source, target):
    target[...] = source[...]


def nearby(weights):
    block = pl.BlockSpec((weights.shape[0] // 4, weights.shape[1]), lambda i: (i, 0))
    return pl.pallas_call(
        copy_block,
        out_shape=shape_of(*weights.shape),
        grid=(4,),
        in_specs=[block],
        out_specs=block,
        compiler_params=pltpu.CompilerParams(vmem_limit_bytes=VMEM_BYTES),
        name="nearby",
    )(weights)


def trade(rows):
    count, columns = rows.shape
    pieces = rows.reshape(count // SLOTS, SLOTS, columns)
    return lax.all_to_all(pieces, MEMBERS, 0, 0, tiled=True).reshape(count, columns)


def swap(value, axis):
    return lax.ppermute(value, axis, [(0, 1), (1, 0)])


def in_order(index, mine, other, axis):
    return jnp.where(
        index == 0,
        jnp.concatenate([mine, other], axis=axis),
        jnp.concatenate([other, mine], axis=axis),
    )


def local(
    boundary,
    routes,
    buckets,
    query_key_value_weight,
    attention_output_weight,
    w_router,
    gain_attn,
    gain_moe,
    bias_table,
    expert_in,
    expert_out,
):
    section = lax.axis_index("section")
    shard = lax.axis_index("shard")
    core = lax.axis_index("core")
    _, micro, _, positions, width = boundary.shape
    tokens = 2 * positions
    heads = bias_table.shape[2]
    bucket_count = 2 * bias_table.shape[1]
    experts = w_router.shape[2]
    half_width = width // 2
    count = experts * SLOTS

    own_rows = boundary.reshape(micro, positions, width)
    own_routes = routes.reshape(micro, positions, 2)
    up = expert_in[0, 0]
    down = expert_out[0, 0]

    def pick(stacked, index):
        return lax.dynamic_index_in_dim(stacked, index, 0, keepdims=False)

    qkv_half = query_key_value_weight[0]
    out_half = attention_output_weight[0]
    table_rows = bucket_count // 2
    sent_routes = pick(own_routes, 1 - shard).astype(BF16).reshape(1, 2 * positions)
    own_small = jnp.concatenate(
        [
            w_router[0].T,
            gain_attn,
            gain_moe,
            jnp.zeros((5, half_width), BF16),
            jnp.pad(sent_routes, ((0, 0), (0, half_width - 2 * positions))),
            jnp.pad(bias_table[0], ((0, 0), (0, half_width - heads))),
        ],
        axis=0,
    )
    piece_rows = half_width // 2
    piece = jnp.concatenate(
        [
            lax.dynamic_slice_in_dim(qkv_half, core * piece_rows, piece_rows, 0),
            lax.dynamic_slice_in_dim(out_half, core * piece_rows, piece_rows, 0),
        ],
        axis=1,
    )
    far_rows = swap(pick(own_rows, 1 - shard), "shard")
    far_buckets = swap(buckets, "shard")
    far_small = swap(own_small, "shard")
    piece, far_rows, far_buckets, far_small = lax.optimization_barrier(
        (piece, far_rows, far_buckets, far_small)
    )
    near = swap(piece, "shard")
    gain_at, route_at, table_at = experts, experts + 7, experts + 8
    router = in_order(shard, own_small[:experts], far_small[:experts], 1)
    gains = in_order(
        shard, own_small[gain_at:table_at], far_small[gain_at:table_at], 1
    ).astype(F32)
    table = in_order(shard, own_small[table_at:, :heads], far_small[table_at:, :heads], 0)
    far_routes = far_small[route_at, : 2 * positions].astype(jnp.int32).reshape(positions, 2)
    mine = in_order(shard, pick(own_rows, shard), far_rows, 0)
    pairs = in_order(
        shard, pick(own_routes, shard), far_routes, 0
    )
    bucket_full = in_order(shard, buckets, far_buckets, 0)
    bucket_hot = (
        bucket_full[None] == jnp.arange(bucket_count, dtype=jnp.int32)[:, None, None]
    ).astype(BF16)
    (bias,) = whole(
        spread_bias,
        [shape_of(heads * tokens, tokens, dtype=F32)],
        (table.astype(F32).reshape(-1), bucket_full),
        scalar=True,
        name="spread_bias",
    )

    flat = pairs.reshape(-1)
    hits = (flat[:, None] == jnp.arange(experts, dtype=jnp.int32)[None, :]).astype(jnp.int32)
    ranks = jnp.sum(jnp.cumsum(hits, axis=0) * hits, axis=1) - 1
    slots = (flat * SLOTS + ranks).reshape(tokens, 2)
    srow = jnp.pad(slots.T, ((0, 6), (0, 0)))
    scol = jnp.pad(jnp.concatenate([slots, pairs], axis=1), ((0, 0), (0, LANES - 4)))

    mixer_flops = 2 * tokens * width * 4 * width
    forward_shapes = [
        shape_of(tokens, width, dtype=F32),
        shape_of(tokens, LANES, dtype=F32),
    ]
    place = jnp.stack([shard, core]).astype(jnp.int32)
    near, mine, router, gains, bias, bucket_hot, srow, scol, up, down = lax.optimization_barrier(
        (near, mine, router, gains, bias, bucket_hot, srow, scol, nearby(up), nearby(down))
    )
    weight_parts = (qkv_half, out_half, near, swap(near, "core"))
    send, hidden, gates, wqkv, wout = whole(
        functools.partial(mixer_forward, False),
        [shape_of(count, width)]
        + forward_shapes
        + [shape_of(width, 3 * width), shape_of(width, width)],
        (place, mine) + weight_parts + (router, gains, bias, srow, scol),
        scalar=True,
        scratch=[pltpu.VMEM((tokens, 3 * width), BF16), pltpu.VMEM((tokens, width), BF16)],
        flops=mixer_flops,
        name="mixer_forward",
    )
    (result_rows,) = expert_call(
        experts_forward, trade(send), up, down, None, 0, width, 1, "experts_forward"
    )
    (layer_out,) = whole(
        combine,
        [shape_of(tokens, width)],
        (trade(result_rows), hidden, gates, scol),
        name="combine",
    )
    arriving = lax.ppermute(layer_out, "section", [(0, 1)])
    layer_in = jnp.where(section == 0, mine, arriving)

    send, hidden, gates, proj, mixed, norm1, norm2 = whole(
        functools.partial(mixer_forward, True),
        [shape_of(count, 2 * width)]
        + forward_shapes
        + [
            shape_of(tokens, 3 * width),
            shape_of(tokens, width),
            shape_of(tokens, width),
            shape_of(tokens, width),
        ],
        (layer_in, mine, wqkv, wout, router, gains, bias, srow, scol),
        flops=mixer_flops,
        name="mixer_forward_keep",
    )
    arrived = trade(send)
    both, act, slope = expert_call(
        experts_both, arrived, up, down, None, 2, 2 * width, 2, "experts_both"
    )
    input_grad, forward_rows, results = whole(
        functools.partial(mixer_backward, False),
        [
            shape_of(tokens, width),
            shape_of(tokens, width),
            shape_of(2, tokens, width),
        ],
        (trade(both), mine, layer_in, wqkv, wout, router, gains, bias, scol, hidden, gates, proj),
        scratch=[pltpu.VMEM((tokens, 3 * width), BF16)],
        flops=2 * mixer_flops,
        name="mixer_backward",
    )
    arriving = lax.ppermute(input_grad, "section", [(1, 0)])
    grad_in = jnp.where(section == 0, arriving, mine)

    (send,) = whole(
        grads_out, [shape_of(count, width)], (grad_in, gates, srow), name="grads_out"
    )
    arrived_grads = trade(send)
    copy_rows, pre_grads = expert_call(
        experts_backward, arrived_grads, up, down, slope, 1, width, 1, "experts_backward"
    )
    returned = trade(copy_rows)
    split = 13 * LANES
    tail = 3 * width - split
    input_grad, keep, give, stats, score_grads = whole(
        functools.partial(mixer_backward, True),
        [
            shape_of(tokens, width),
            shape_of(width, split),
            shape_of(width, split),
            shape_of(8, width, dtype=F32),
            shape_of(heads * tokens, tokens),
        ],
        (
            core.reshape(1),
            returned,
            grad_in,
            layer_in,
            results,
            wqkv,
            wout,
            router,
            gains,
            bias,
            scol,
            hidden,
            gates,
            proj,
            mixed,
            norm1,
            norm2,
        ),
        scratch=[pltpu.VMEM((tokens, 3 * width), BF16)],
        scalar=True,
        flops=3 * mixer_flops,
        name="mixer_backward_last",
    )

    finished = jnp.where(section == 0, input_grad, forward_rows).reshape(2, positions, width)
    from_other = swap(pick(finished, 1 - shard), "shard")
    boundary_out = jnp.stack(
        [
            jnp.where(shard == 0, pick(finished, shard), from_other),
            jnp.where(shard == 0, from_other, pick(finished, shard)),
        ]
    ).reshape(boundary.shape)

    table_grad = jnp.einsum(
        "bts,hts->bh",
        bucket_hot,
        score_grads.reshape(heads, tokens, tokens),
        preferred_element_type=F32
    )
    half_rows = half_width // LANES
    small = jnp.concatenate(
        [
            stats[0].reshape(2, half_rows, LANES),
            stats[1].reshape(2, half_rows, LANES),
            jnp.zeros((2, 8 - 2 * half_rows, LANES), F32),
            jnp.pad(
                table_grad.reshape(2, table_rows, heads), ((0, 0), (0, 0), (0, LANES - heads))
            ),
        ],
        axis=1,
    )
    small = jnp.pad(small, ((0, 0), (0, 32 - small.shape[1]), (0, 0)))
    block = pl.BlockSpec((width // 4, split), lambda i: (i, 0))
    whole_small = pl.BlockSpec(small.shape, lambda i: (0, 0, 0))
    summed = pl.pallas_call(
        merge,
        out_shape=shape_of(width, split),
        grid=(4,),
        in_specs=[
            pl.BlockSpec(memory_space=pltpu.SMEM),
            block,
            block,
            whole_small,
            whole_small,
        ],
        out_specs=block,
        compiler_params=pltpu.CompilerParams(vmem_limit_bytes=VMEM_BYTES),
        name="merge",
    )(core.reshape(1), keep, swap(give, "core"), small, swap(small, "core"))
    summed, arrived, arrived_grads, act, pre_grads, boundary_out = lax.optimization_barrier(
        (summed, arrived, arrived_grads, act, pre_grads, boundary_out)
    )
    d_expert_in = lax.dot_general(
        arrived[:, :width], pre_grads, (((0,), (0,)), ((), ())), preferred_element_type=F32
    ).astype(BF16)
    d_expert_out = lax.dot_general(
        act, arrived_grads, (((0,), (0,)), ((), ())), preferred_element_type=F32
    ).astype(BF16)
    gathered = lax.all_to_all(
        summed.reshape(32, width // 32, split), ("shard", "y", "z"), 0, 0, tiled=True
    )
    gathered, d_expert_in, d_expert_out = lax.optimization_barrier(
        (gathered, d_expert_in, d_expert_out)
    )
    piece = jnp.sum(gathered.astype(F32), axis=0).astype(BF16)
    spread = lax.all_to_all(
        jnp.broadcast_to(piece[None], (16,) + piece.shape), ("y", "z"), 0, 0, tiled=True
    ).reshape(half_width, split)
    qkv_sum, out_sum, rest = whole(
        finish,
        [
            shape_of(half_width, 3 * width),
            shape_of(half_width, width),
            shape_of(half_width, 2 * LANES),
        ],
        (core.reshape(1), spread, swap(spread, "core")),
        scalar=True,
        name="finish",
    )
    totals = rest[: 8 + table_rows, LANES:]
    gain_one_sum = totals[:half_rows].reshape(half_width)
    gain_two_sum = totals[half_rows : 2 * half_rows].reshape(half_width)
    table_sum = totals[8:, :heads]
    return (
        boundary_out,
        qkv_sum[None],
        out_sum[None],
        rest[:, :experts][None],
        gain_one_sum[None],
        gain_two_sum[None],
        table_sum[None],
        d_expert_in.reshape(expert_in.shape),
        d_expert_out.reshape(expert_out.shape),
    )


def solution(mesh):
    fine = Mesh(
        mesh.devices.reshape(2, 4, 4, 2, 2), ("section", "y", "z", "core", "shard")
    )
    expert = ("y", "z", "core")
    rows = P("section", None, expert, "shard", None)
    by_pair = P("section", "shard", None)
    by_expert = P("section", MEMBERS, None, None)
    in_specs = (
        rows,
        rows,
        P("shard", None),
        by_pair,
        by_pair,
        by_pair,
        P("section", "shard"),
        P("section", "shard"),
        by_pair,
        by_expert,
        by_expert,
    )
    out_specs = (
        rows,
        by_pair,
        by_pair,
        by_pair,
        P("section", "shard"),
        P("section", "shard"),
        by_pair,
        by_expert,
        by_expert,
    )
    return jax.shard_map(local, mesh=fine, in_specs=in_specs, out_specs=out_specs, check_vma=False)
```

```python
import functools

import jax
import jax.numpy as jnp
from jax import lax
from jax.experimental import pallas as pl
from jax.experimental.pallas import tpu as pltpu
from jax.sharding import Mesh
from jax.sharding import PartitionSpec as P

EPS = 1e-06
F32 = jnp.float32
BF16 = jnp.bfloat16
SLOTS = 8
LANES = 128
HEAD = 64
MEMBERS = ("y", "z", "core", "shard")
VMEM_BYTES = 50 * 1024 * 1024
LATE_BYTES = 22 * 1024 * 1024


def dot(a, b):
    return jnp.dot(a, b, preferred_element_type=F32)


def dot_nt(a, b):
    return lax.dot_general(a, b, (((1,), (1,)), ((), ())), preferred_element_type=F32)


def dot_tn(a, b):
    return lax.dot_general(a, b, (((0,), (0,)), ((), ())), preferred_element_type=F32)


def row_scale(values):
    return lax.rsqrt(jnp.mean(values * values, axis=-1, keepdims=True) + EPS)


def iota(shape, axis):
    return lax.broadcasted_iota(jnp.int32, shape, axis)


def one_hot(matches):
    return jnp.where(matches, 1.0, 0.0).astype(BF16)


def stack_heads(pair):
    lane = iota(pair.shape, 1)
    zero = jnp.zeros_like(pair)
    return jnp.concatenate(
        [jnp.where(lane < HEAD, pair, zero), jnp.where(lane >= HEAD, pair, zero)], axis=0
    )


def join_heads(stacked):
    rows = stacked.shape[0] // 2
    return jnp.where(iota((rows, LANES), 1) < HEAD, stacked[:rows], stacked[rows:])


def seen(tokens):
    shape = (2 * tokens, tokens)
    row = iota(shape, 0)
    return iota(shape, 1) <= jnp.where(row < tokens, row, row - tokens)


def soft_probs(queries, key, bias, causal):
    scores = dot_nt(queries, key) * (HEAD**-0.5) + bias
    scores = jnp.where(causal, scores, -jnp.inf)
    raised = jnp.exp(scores - jnp.max(scores, axis=-1, keepdims=True))
    return raised / jnp.sum(raised, axis=-1, keepdims=True)


def assemble(place, parts, wqkv, wout):
    qkv_own, out_own, near, far = parts
    rows, piece, split = qkv_own.shape[0], near.shape[0], qkv_own.shape[1]
    own_at = pl.ds(pl.multiple_of(place[0] * rows, rows), rows)
    base = (1 - place[0]) * rows
    near_at = pl.ds(pl.multiple_of(base + place[1] * piece, piece), piece)
    far_at = pl.ds(pl.multiple_of(base + (1 - place[1]) * piece, piece), piece)
    wqkv[own_at, :] = qkv_own[...]
    wqkv[near_at, :] = near[:, :split]
    wqkv[far_at, :] = far[:, :split]
    wout[own_at, :] = out_own[...]
    wout[near_at, :] = near[:, split:]
    wout[far_at, :] = far[:, split:]


def spread_bias(table, buckets, out):
    picked = buckets[...]
    tokens = picked.shape[0]
    heads = out.shape[0] // tokens
    count = table.shape[0] // heads
    for head in range(heads):
        values = jnp.zeros(picked.shape, F32)
        for bucket in range(count):
            values = jnp.where(picked == bucket, table[bucket * heads + head], values)
        out[head * tokens : (head + 1) * tokens, :] = values


def merge(core, keep, arrived, own_small, other_small, out):
    out[...] = (keep[...].astype(F32) + arrived[...].astype(F32)).astype(BF16)
    rows, lanes = own_small.shape[1], keep.shape[1] - LANES
    step = pl.program_id(0)

    @pl.when((core[0] == 1) & (step % 2 == 0))
    def _():
        share = step // 2
        out[:rows, lanes:] = (own_small[share] + other_small[share]).astype(BF16)


def finish(core, mine, other, qkv_out, out_out, rest_out):
    split, tail, width = mine.shape[1], qkv_out.shape[1] - mine.shape[1], out_out.shape[1]

    def fill(low, high):
        qkv_out[:, :split] = low[...]
        qkv_out[:, split:] = high[:, :tail]
        out_out[...] = high[:, tail : tail + width]
        rest_out[...] = high[:, tail + width :]

    @pl.when(core[0] == 0)
    def _():
        fill(mine, other)

    @pl.when(core[0] == 1)
    def _():
        fill(other, mine)


def mixer_forward(with_grads, *refs):
    if with_grads:
        x_ref, dy_ref, wqkv, wout, wr, gains, bias, srow, scol = refs[:9]
        send, hidden_out, gates_out, proj, mixed, norm1_out, norm2_out = refs[9:]
    else:
        place, x_ref = refs[:2]
        parts, (wr, gains, bias, srow, scol) = refs[2:6], refs[6:11]
        send, hidden_out, gates_out, wqkv, wout, proj, mixed = refs[11:]
        assemble(place, parts, wqkv, wout)
    tokens, width = x_ref.shape
    x = x_ref[...].astype(F32)
    norm1 = (x * row_scale(x) * gains[0:1, :]).astype(BF16)
    proj[...] = dot(norm1, wqkv[...]).astype(BF16)
    causal = seen(tokens)
    for pair in range(width // LANES):
        at = pair * LANES
        queries = stack_heads(proj[:, at : at + LANES])
        key = proj[:, width + at : width + at + LANES]
        value = proj[:, 2 * width + at : 2 * width + at + LANES]
        rows = slice(2 * pair * tokens, 2 * (pair + 1) * tokens)
        probs = soft_probs(queries, key, bias[rows, :], causal).astype(BF16)
        mixed[:, at : at + LANES] = join_heads(dot(probs, value)).astype(BF16)
    hidden = x + dot(mixed[...], wout[...])
    hidden_out[...] = hidden
    norm2 = (hidden * row_scale(hidden) * gains[1:2, :]).astype(BF16)
    logits = dot_nt(norm2, wr[...])
    lane = iota(logits.shape, 1)
    first = jnp.sum(jnp.where(lane == scol[:, 2:3], logits, 0.0), axis=1, keepdims=True)
    second = jnp.sum(jnp.where(lane == scol[:, 3:4], logits, 0.0), axis=1, keepdims=True)
    top = jnp.maximum(first, second)
    first = jnp.exp(first - top)
    second = jnp.exp(second - top)
    gate0 = first / (first + second)
    gate1 = second / (first + second)
    lane = iota((tokens, LANES), 1)
    gates_out[...] = jnp.where(lane == 0, gate0, jnp.where(lane == 1, gate1, 0.0))
    slot = iota((send.shape[0], tokens), 0)
    hits0 = slot == srow[0:1, :]
    hits1 = slot == srow[1:2, :]
    send[:, :width] = dot(one_hot(hits0 | hits1), norm2).astype(BF16)
    if with_grads:
        dy = dy_ref[...].astype(F32)
        send[:, width:] = (
            dot(one_hot(hits0), (gate0 * dy).astype(BF16))
            + dot(one_hot(hits1), (gate1 * dy).astype(BF16))
        ).astype(BF16)
        norm1_out[...] = norm1
        norm2_out[...] = norm2


def grads_out(dy_ref, gates, srow, send):
    tokens = dy_ref.shape[0]
    dy = dy_ref[...].astype(F32)
    slot = iota((send.shape[0], tokens), 0)
    send[...] = (
        dot(one_hot(slot == srow[0:1, :]), (gates[:, 0:1] * dy).astype(BF16))
        + dot(one_hot(slot == srow[1:2, :]), (gates[:, 1:2] * dy).astype(BF16))
    ).astype(BF16)


def combine(back, hidden, gates, scol, out):
    tokens = hidden.shape[0]
    slot = iota((tokens, back.shape[0]), 1)
    result0 = dot(one_hot(slot == scol[:, 0:1]), back[...])
    result1 = dot(one_hot(slot == scol[:, 1:2]), back[...])
    out[...] = (hidden[...] + gates[:, 0:1] * result0 + gates[:, 1:2] * result1).astype(BF16)


def bell(pre):
    return 0.5 * (1.0 + lax.erf(pre * 0.7071067811865476))


def grow(total, step, part):
    total[...] = jnp.where(step == 0, part, total[...] + part)


def experts_forward(rows, up, down, out, total):
    step = pl.program_id(0)
    pre = dot(rows[...], up[...])
    grow(total, step, dot((pre * bell(pre)).astype(BF16), down[...]))

    @pl.when(step == pl.num_programs(0) - 1)
    def _():
        out[...] = total[...].astype(BF16)


def experts_both(rows, up, down, out, act_out, slope_out, total, total_back):
    step = pl.program_id(0)
    width = up.shape[0]
    pre = dot(rows[:, :width], up[...])
    lower = bell(pre)
    act = (pre * lower).astype(BF16)
    slope = lower + pre * jnp.exp(-0.5 * pre * pre) * 0.3989422804014327
    act_out[...] = act
    slope_out[...] = slope.astype(BF16)
    pre_grads = (dot_nt(rows[:, width:], down[...]) * slope).astype(BF16)
    grow(total, step, dot(act, down[...]))
    grow(total_back, step, dot_nt(pre_grads, up[...]))

    @pl.when(step == pl.num_programs(0) - 1)
    def _():
        out[:, :width] = total[...].astype(BF16)
        out[:, width:] = total_back[...].astype(BF16)


def experts_backward(grads, up, down, slope, out, pre_out, total_back):
    step = pl.program_id(0)
    pre_grads = (dot_nt(grads[...], down[...]) * slope[...].astype(F32)).astype(BF16)
    pre_out[...] = pre_grads
    grow(total_back, step, dot_nt(pre_grads, up[...]))

    @pl.when(step == pl.num_programs(0) - 1)
    def _():
        out[...] = total_back[...].astype(BF16)


def mixer_backward(last, *refs):
    if last:
        (core, back, dy_ref, x_ref, res_in, wqkv, wout, wr, gains, bias, scol) = refs[:11]
        (hidden_ref, gates, proj, mixed, norm1, norm2) = refs[11:17]
        (input_grad, keep, give, stats, score_out, proj_grad) = refs[17:]
    else:
        (back, dy_ref, x_ref, wqkv, wout, wr, gains, bias, scol) = refs[:9]
        (hidden_ref, gates, proj) = refs[9:12]
        (input_grad, y_out, res_out, proj_grad) = refs[12:]
    tokens, width = x_ref.shape
    dy = dy_ref[...].astype(F32)
    hidden = hidden_ref[...]
    gate0 = gates[:, 0:1]
    gate1 = gates[:, 1:2]
    slot = iota((tokens, back.shape[0]), 1)
    hits0 = slot == scol[:, 0:1]
    hits1 = slot == scol[:, 1:2]
    if last:
        result0 = res_in[0].astype(F32)
        result1 = res_in[1].astype(F32)
        copy_rows = back[...]
    else:
        result0 = dot(one_hot(hits0), back[:, :width])
        result1 = dot(one_hot(hits1), back[:, :width])
        res_out[0] = result0.astype(BF16)
        res_out[1] = result1.astype(BF16)
        y_out[...] = (hidden + gate0 * result0 + gate1 * result1).astype(BF16)
        copy_rows = back[:, width:]
    gate_grad0 = jnp.sum(result0 * dy, axis=1, keepdims=True)
    gate_grad1 = jnp.sum(result1 * dy, axis=1, keepdims=True)
    inner = gate0 * gate_grad0 + gate1 * gate_grad1
    experts = wr.shape[0]
    lane = iota((tokens, experts), 1)
    logit_grads = (
        jnp.where(lane == scol[:, 2:3], gate0 * (gate_grad0 - inner), 0.0)
        + jnp.where(lane == scol[:, 3:4], gate1 * (gate_grad1 - inner), 0.0)
    ).astype(BF16)
    norm2_grads = dot(one_hot(hits0 | hits1), copy_rows) + dot(logit_grads, wr[...])
    scale2 = row_scale(hidden)
    weighted = norm2_grads * gains[1:2, :]
    inner = jnp.mean(weighted * hidden, axis=-1, keepdims=True)
    hidden_grad = dy + scale2 * weighted - hidden * (scale2 * scale2 * scale2 * inner)
    branch = hidden_grad.astype(BF16)
    mixed_grad = dot_nt(branch, wout[...]).astype(BF16)
    causal = seen(tokens)
    for pair in range(width // LANES):
        at = pair * LANES
        queries = stack_heads(proj[:, at : at + LANES])
        key = proj[:, width + at : width + at + LANES]
        value = proj[:, 2 * width + at : 2 * width + at + LANES]
        outer = stack_heads(mixed_grad[:, at : at + LANES])
        rows = slice(2 * pair * tokens, 2 * (pair + 1) * tokens)
        probs = soft_probs(queries, key, bias[rows, :], causal)
        prob_grad = dot_nt(outer, value)
        inner = jnp.sum(probs * prob_grad, axis=-1, keepdims=True)
        score_grad = (probs * (prob_grad - inner)).astype(BF16)
        if last:
            score_out[rows, :] = score_grad
        query_grad = join_heads(dot(score_grad, key)) * HEAD**-0.5
        key_grad = dot_tn(score_grad, queries) * HEAD**-0.5
        proj_grad[:, at : at + LANES] = query_grad.astype(BF16)
        proj_grad[:, width + at : width + at + LANES] = key_grad.astype(BF16)
        proj_grad[:, 2 * width + at : 2 * width + at + LANES] = dot_tn(
            probs.astype(BF16), outer
        ).astype(BF16)
    norm1_grads = dot_nt(proj_grad[...], wqkv[...])
    x = x_ref[...].astype(F32)
    scale1 = row_scale(x)
    weighted = norm1_grads * gains[0:1, :]
    inner = jnp.mean(weighted * x, axis=-1, keepdims=True)
    input_grad[...] = (
        hidden_grad + scale1 * weighted - x * (scale1 * scale1 * scale1 * inner)
    ).astype(BF16)
    if last:
        stats[0:1, :] = jnp.sum(norm1_grads * x * scale1, axis=0, keepdims=True)
        stats[1:2, :] = jnp.sum(norm2_grads * hidden * scale2, axis=0, keepdims=True)
        stats[2:8, :] = jnp.zeros((6, width), F32)
        split = keep.shape[1]
        tail = 3 * width - split

        def fill(low, high):
            low[...] = dot_tn(norm1[...], proj_grad[:, :split]).astype(BF16)
            high[:, :tail] = dot_tn(norm1[...], proj_grad[:, split:]).astype(BF16)
            high[:, tail : tail + width] = dot_tn(mixed[...], branch).astype(BF16)
            rest = tail + width
            high[:, rest : rest + experts] = dot_tn(norm2[...], logit_grads).astype(BF16)
            high[:, rest + experts :] = jnp.zeros((width, split - rest - experts), BF16)

        @pl.when(core[0] == 0)
        def _():
            fill(keep, give)

        @pl.when(core[0] == 1)
        def _():
            fill(give, keep)


def shape_of(*dims, dtype=BF16):
    return jax.ShapeDtypeStruct(dims, dtype)


def whole(kernel, outs, operands, scratch=(), scalar=False, flops=0, name=None, limit=LATE_BYTES):
    vmem = pl.BlockSpec(memory_space=pltpu.VMEM)
    specs = [vmem] * len(operands)
    if scalar:
        specs[0] = pl.BlockSpec(memory_space=pltpu.SMEM)
    moved = sum(o.size * o.dtype.itemsize for o in list(operands) + list(outs))
    return pl.pallas_call(
        kernel,
        out_shape=outs,
        in_specs=specs,
        out_specs=[vmem] * len(outs),
        scratch_shapes=list(scratch),
        cost_estimate=pl.CostEstimate(flops=flops, bytes_accessed=moved, transcendentals=0),
        compiler_params=pltpu.CompilerParams(vmem_limit_bytes=limit),
        name=name,
    )(*operands)


CHUNK = 768


def expert_call(kernel, rows, up, down, slope, wide_outs, out_cols, sums, name):
    count = rows.shape[0]
    width, hidden_units = up.shape
    specs = [
        pl.BlockSpec(rows.shape, lambda i: (0, 0)),
        pl.BlockSpec((width, CHUNK), lambda i: (0, i)),
        pl.BlockSpec((CHUNK, width), lambda i: (i, 0)),
    ]
    operands = [rows, up, down]
    per_chunk = pl.BlockSpec((count, CHUNK), lambda i: (0, i))
    if slope is not None:
        specs.append(per_chunk)
        operands.append(slope)
    outs = [shape_of(count, out_cols)] + [shape_of(count, hidden_units)] * wide_outs
    moved = sum(o.size * o.dtype.itemsize for o in operands + outs)
    return pl.pallas_call(
        kernel,
        out_shape=outs,
        grid=(hidden_units // CHUNK,),
        in_specs=specs,
        out_specs=[pl.BlockSpec((count, out_cols), lambda i: (0, 0))] + [per_chunk] * wide_outs,
        scratch_shapes=[pltpu.VMEM((count, width), F32)] * sums,
        cost_estimate=pl.CostEstimate(
            flops=4 * sums * count * width * hidden_units,
            bytes_accessed=moved,
            transcendentals=0,
        ),
        compiler_params=pltpu.CompilerParams(
            dimension_semantics=("arbitrary",),
            vmem_limit_bytes=VMEM_BYTES if slope is None else LATE_BYTES,
        ),
        name=name,
    )(*operands)


def trade(rows):
    count, columns = rows.shape
    pieces = rows.reshape(count // SLOTS, SLOTS, columns)
    return lax.all_to_all(pieces, MEMBERS, 0, 0, tiled=True).reshape(count, columns)


def swap(value, axis):
    return lax.ppermute(value, axis, [(0, 1), (1, 0)])


def in_order(index, mine, other, axis):
    return jnp.where(
        index == 0,
        jnp.concatenate([mine, other], axis=axis),
        jnp.concatenate([other, mine], axis=axis),
    )


def local(
    boundary,
    routes,
    buckets,
    query_key_value_weight,
    attention_output_weight,
    w_router,
    gain_attn,
    gain_moe,
    bias_table,
    expert_in,
    expert_out,
):
    section = lax.axis_index("section")
    shard = lax.axis_index("shard")
    core = lax.axis_index("core")
    _, micro, _, positions, width = boundary.shape
    tokens = 2 * positions
    heads = bias_table.shape[2]
    bucket_count = 2 * bias_table.shape[1]
    experts = w_router.shape[2]
    half_width = width // 2
    count = experts * SLOTS

    own_rows = boundary.reshape(micro, positions, width)
    own_routes = routes.reshape(micro, positions, 2)
    up = expert_in[0, 0]
    down = expert_out[0, 0]

    def pick(stacked, index):
        return lax.dynamic_index_in_dim(stacked, index, 0, keepdims=False)

    qkv_half = query_key_value_weight[0]
    out_half = attention_output_weight[0]
    table_rows = bucket_count // 2
    sent_routes = pick(own_routes, 1 - shard).astype(BF16).reshape(1, 2 * positions)
    own_small = jnp.concatenate(
        [
            w_router[0].T,
            gain_attn,
            gain_moe,
            jnp.zeros((5, half_width), BF16),
            jnp.pad(sent_routes, ((0, 0), (0, half_width - 2 * positions))),
            jnp.pad(bias_table[0], ((0, 0), (0, half_width - heads))),
        ],
        axis=0,
    )
    piece_rows = half_width // 2
    piece = jnp.concatenate(
        [
            lax.dynamic_slice_in_dim(qkv_half, core * piece_rows, piece_rows, 0),
            lax.dynamic_slice_in_dim(out_half, core * piece_rows, piece_rows, 0),
        ],
        axis=1,
    )
    far_rows = swap(pick(own_rows, 1 - shard), "shard")
    far_buckets = swap(buckets, "shard")
    far_small = swap(own_small, "shard")
    piece, far_rows, far_buckets, far_small = lax.optimization_barrier(
        (piece, far_rows, far_buckets, far_small)
    )
    near = swap(piece, "shard")
    gain_at, route_at, table_at = experts, experts + 7, experts + 8
    router = in_order(shard, own_small[:experts], far_small[:experts], 1)
    gains = in_order(
        shard, own_small[gain_at:table_at], far_small[gain_at:table_at], 1
    ).astype(F32)
    table = in_order(shard, own_small[table_at:, :heads], far_small[table_at:, :heads], 0)
    far_routes = far_small[route_at, : 2 * positions].astype(jnp.int32).reshape(positions, 2)
    mine = in_order(shard, pick(own_rows, shard), far_rows, 0)
    pairs = in_order(
        shard, pick(own_routes, shard), far_routes, 0
    )
    bucket_full = in_order(shard, buckets, far_buckets, 0)
    bucket_hot = (
        bucket_full[None] == jnp.arange(bucket_count, dtype=jnp.int32)[:, None, None]
    ).astype(BF16)
    (bias,) = whole(
        spread_bias,
        [shape_of(heads * tokens, tokens, dtype=F32)],
        (table.astype(F32).reshape(-1), bucket_full),
        scalar=True,
        name="spread_bias",
        limit=VMEM_BYTES,
    )

    flat = pairs.reshape(-1)
    hits = (flat[:, None] == jnp.arange(experts, dtype=jnp.int32)[None, :]).astype(jnp.int32)
    ranks = jnp.sum(jnp.cumsum(hits, axis=0) * hits, axis=1) - 1
    slots = (flat * SLOTS + ranks).reshape(tokens, 2)
    srow = jnp.pad(slots.T, ((0, 6), (0, 0)))
    scol = jnp.pad(jnp.concatenate([slots, pairs], axis=1), ((0, 0), (0, LANES - 4)))

    mixer_flops = 2 * tokens * width * 4 * width
    forward_shapes = [
        shape_of(tokens, width, dtype=F32),
        shape_of(tokens, LANES, dtype=F32),
    ]
    place = jnp.stack([shard, core]).astype(jnp.int32)
    near, mine, router, gains, bias, bucket_hot, srow, scol = lax.optimization_barrier(
        (near, mine, router, gains, bias, bucket_hot, srow, scol)
    )
    weight_parts = (qkv_half, out_half, near, swap(near, "core"))
    send, hidden, gates, wqkv, wout = whole(
        functools.partial(mixer_forward, False),
        [shape_of(count, width)]
        + forward_shapes
        + [shape_of(width, 3 * width), shape_of(width, width)],
        (place, mine) + weight_parts + (router, gains, bias, srow, scol),
        scalar=True,
        scratch=[pltpu.VMEM((tokens, 3 * width), BF16), pltpu.VMEM((tokens, width), BF16)],
        flops=mixer_flops,
        name="mixer_forward",
        limit=VMEM_BYTES,
    )
    (result_rows,) = expert_call(
        experts_forward, trade(send), up, down, None, 0, width, 1, "experts_forward"
    )
    (layer_out,) = whole(
        combine,
        [shape_of(tokens, width)],
        (trade(result_rows), hidden, gates, scol),
        name="combine",
    )
    arriving = lax.ppermute(layer_out, "section", [(0, 1)])
    layer_in = jnp.where(section == 0, mine, arriving)

    send, hidden, gates, proj, mixed, norm1, norm2 = whole(
        functools.partial(mixer_forward, True),
        [shape_of(count, 2 * width)]
        + forward_shapes
        + [
            shape_of(tokens, 3 * width),
            shape_of(tokens, width),
            shape_of(tokens, width),
            shape_of(tokens, width),
        ],
        (layer_in, mine, wqkv, wout, router, gains, bias, srow, scol),
        flops=mixer_flops,
        name="mixer_forward_keep",
        limit=VMEM_BYTES,
    )
    arrived = trade(send)
    both, act, slope = expert_call(
        experts_both, arrived, up, down, None, 2, 2 * width, 2, "experts_both"
    )
    input_grad, forward_rows, results = whole(
        functools.partial(mixer_backward, False),
        [
            shape_of(tokens, width),
            shape_of(tokens, width),
            shape_of(2, tokens, width),
        ],
        (trade(both), mine, layer_in, wqkv, wout, router, gains, bias, scol, hidden, gates, proj),
        scratch=[pltpu.VMEM((tokens, 3 * width), BF16)],
        flops=2 * mixer_flops,
        name="mixer_backward",
    )
    arriving = lax.ppermute(input_grad, "section", [(1, 0)])
    grad_in = jnp.where(section == 0, arriving, mine)

    (send,) = whole(
        grads_out, [shape_of(count, width)], (grad_in, gates, srow), name="grads_out"
    )
    arrived_grads = trade(send)
    copy_rows, pre_grads = expert_call(
        experts_backward, arrived_grads, up, down, slope, 1, width, 1, "experts_backward"
    )
    returned = trade(copy_rows)
    split = 13 * LANES
    tail = 3 * width - split
    input_grad, keep, give, stats, score_grads = whole(
        functools.partial(mixer_backward, True),
        [
            shape_of(tokens, width),
            shape_of(width, split),
            shape_of(width, split),
            shape_of(8, width, dtype=F32),
            shape_of(heads * tokens, tokens),
        ],
        (
            core.reshape(1),
            returned,
            grad_in,
            layer_in,
            results,
            wqkv,
            wout,
            router,
            gains,
            bias,
            scol,
            hidden,
            gates,
            proj,
            mixed,
            norm1,
            norm2,
        ),
        scratch=[pltpu.VMEM((tokens, 3 * width), BF16)],
        scalar=True,
        flops=3 * mixer_flops,
        name="mixer_backward_last",
    )

    finished = jnp.where(section == 0, input_grad, forward_rows).reshape(2, positions, width)
    from_other = swap(pick(finished, 1 - shard), "shard")
    boundary_out = jnp.stack(
        [
            jnp.where(shard == 0, pick(finished, shard), from_other),
            jnp.where(shard == 0, from_other, pick(finished, shard)),
        ]
    ).reshape(boundary.shape)

    table_grad = jnp.einsum(
        "bts,hts->bh",
        bucket_hot,
        score_grads.reshape(heads, tokens, tokens),
        preferred_element_type=F32
    )
    half_rows = half_width // LANES
    small = jnp.concatenate(
        [
            stats[0].reshape(2, half_rows, LANES),
            stats[1].reshape(2, half_rows, LANES),
            jnp.zeros((2, 8 - 2 * half_rows, LANES), F32),
            jnp.pad(
                table_grad.reshape(2, table_rows, heads), ((0, 0), (0, 0), (0, LANES - heads))
            ),
        ],
        axis=1,
    )
    small = jnp.pad(small, ((0, 0), (0, 32 - small.shape[1]), (0, 0)))
    block = pl.BlockSpec((width // 4, split), lambda i: (i, 0))
    whole_small = pl.BlockSpec(small.shape, lambda i: (0, 0, 0))
    summed = pl.pallas_call(
        merge,
        out_shape=shape_of(width, split),
        grid=(4,),
        in_specs=[
            pl.BlockSpec(memory_space=pltpu.SMEM),
            block,
            block,
            whole_small,
            whole_small,
        ],
        out_specs=block,
        compiler_params=pltpu.CompilerParams(vmem_limit_bytes=LATE_BYTES),
        name="merge",
    )(core.reshape(1), keep, swap(give, "core"), small, swap(small, "core"))
    summed, arrived, arrived_grads, act, pre_grads, boundary_out = lax.optimization_barrier(
        (summed, arrived, arrived_grads, act, pre_grads, boundary_out)
    )
    d_expert_in = lax.dot_general(
        arrived[:, :width], pre_grads, (((0,), (0,)), ((), ())), preferred_element_type=F32
    ).astype(BF16)
    d_expert_out = lax.dot_general(
        act, arrived_grads, (((0,), (0,)), ((), ())), preferred_element_type=F32
    ).astype(BF16)
    gathered = lax.all_to_all(
        summed.reshape(32, width // 32, split), ("shard", "y", "z"), 0, 0, tiled=True
    )
    gathered, d_expert_in, d_expert_out = lax.optimization_barrier(
        (gathered, d_expert_in, d_expert_out)
    )
    piece = jnp.sum(gathered.astype(F32), axis=0).astype(BF16)
    spread = lax.all_to_all(
        jnp.broadcast_to(piece[None], (16,) + piece.shape), ("y", "z"), 0, 0, tiled=True
    ).reshape(half_width, split)
    qkv_sum, out_sum, rest = whole(
        finish,
        [
            shape_of(half_width, 3 * width),
            shape_of(half_width, width),
            shape_of(half_width, 2 * LANES),
        ],
        (core.reshape(1), spread, swap(spread, "core")),
        scalar=True,
        name="finish",
    )
    totals = rest[: 8 + table_rows, LANES:]
    gain_one_sum = totals[:half_rows].reshape(half_width)
    gain_two_sum = totals[half_rows : 2 * half_rows].reshape(half_width)
    table_sum = totals[8:, :heads]
    return (
        boundary_out,
        qkv_sum[None],
        out_sum[None],
        rest[:, :experts][None],
        gain_one_sum[None],
        gain_two_sum[None],
        table_sum[None],
        d_expert_in.reshape(expert_in.shape),
        d_expert_out.reshape(expert_out.shape),
    )


def solution(mesh):
    fine = Mesh(
        mesh.devices.reshape(2, 4, 4, 2, 2), ("section", "y", "z", "core", "shard")
    )
    expert = ("y", "z", "core")
    rows = P("section", None, expert, "shard", None)
    by_pair = P("section", "shard", None)
    by_expert = P("section", MEMBERS, None, None)
    in_specs = (
        rows,
        rows,
        P("shard", None),
        by_pair,
        by_pair,
        by_pair,
        P("section", "shard"),
        P("section", "shard"),
        by_pair,
        by_expert,
        by_expert,
    )
    out_specs = (
        rows,
        by_pair,
        by_pair,
        by_pair,
        P("section", "shard"),
        P("section", "shard"),
        by_pair,
        by_expert,
        by_expert,
    )
    return jax.shard_map(local, mesh=fine, in_specs=in_specs, out_specs=out_specs, check_vma=False)
```

```python
import functools

import jax
import jax.numpy as jnp
from jax import lax
from jax.experimental import pallas as pl
from jax.experimental.pallas import tpu as pltpu
from jax.sharding import Mesh
from jax.sharding import PartitionSpec as P

EPS = 1e-06
F32 = jnp.float32
BF16 = jnp.bfloat16
SLOTS = 8
LANES = 128
HEAD = 64
MEMBERS = ("y", "z", "core", "shard")
VMEM_BYTES = 50 * 1024 * 1024
LATE_BYTES = 22 * 1024 * 1024


def dot(a, b):
    return jnp.dot(a, b, preferred_element_type=F32)


def dot_nt(a, b):
    return lax.dot_general(a, b, (((1,), (1,)), ((), ())), preferred_element_type=F32)


def dot_tn(a, b):
    return lax.dot_general(a, b, (((0,), (0,)), ((), ())), preferred_element_type=F32)


def row_scale(values):
    return lax.rsqrt(jnp.mean(values * values, axis=-1, keepdims=True) + EPS)


def iota(shape, axis):
    return lax.broadcasted_iota(jnp.int32, shape, axis)


def one_hot(matches):
    return jnp.where(matches, 1.0, 0.0).astype(BF16)


def stack_heads(pair):
    lane = iota(pair.shape, 1)
    zero = jnp.zeros_like(pair)
    return jnp.concatenate(
        [jnp.where(lane < HEAD, pair, zero), jnp.where(lane >= HEAD, pair, zero)], axis=0
    )


def join_heads(stacked):
    rows = stacked.shape[0] // 2
    return jnp.where(iota((rows, LANES), 1) < HEAD, stacked[:rows], stacked[rows:])


def seen(tokens):
    shape = (2 * tokens, tokens)
    row = iota(shape, 0)
    return iota(shape, 1) <= jnp.where(row < tokens, row, row - tokens)


def soft_probs(queries, key, bias, causal):
    scores = dot_nt(queries, key) * (HEAD**-0.5) + bias
    scores = jnp.where(causal, scores, -jnp.inf)
    raised = jnp.exp(scores - jnp.max(scores, axis=-1, keepdims=True))
    return raised / jnp.sum(raised, axis=-1, keepdims=True)


def assemble(place, parts, wqkv, wout):
    qkv_own, out_own, near, far = parts
    rows, piece, split = qkv_own.shape[0], near.shape[0], qkv_own.shape[1]
    own_at = pl.ds(pl.multiple_of(place[0] * rows, rows), rows)
    base = (1 - place[0]) * rows
    near_at = pl.ds(pl.multiple_of(base + place[1] * piece, piece), piece)
    far_at = pl.ds(pl.multiple_of(base + (1 - place[1]) * piece, piece), piece)
    wqkv[own_at, :] = qkv_own[...]
    wqkv[near_at, :] = near[:, :split]
    wqkv[far_at, :] = far[:, :split]
    wout[own_at, :] = out_own[...]
    wout[near_at, :] = near[:, split:]
    wout[far_at, :] = far[:, split:]


def spread_bias(table, buckets, out):
    picked = buckets[...]
    tokens = picked.shape[0]
    heads = out.shape[0] // tokens
    count = table.shape[0] // heads
    for head in range(heads):
        values = jnp.zeros(picked.shape, F32)
        for bucket in range(count):
            values = jnp.where(picked == bucket, table[bucket * heads + head], values)
        out[head * tokens : (head + 1) * tokens, :] = values


def merge(core, keep, arrived, own_small, other_small, out):
    out[...] = (keep[...].astype(F32) + arrived[...].astype(F32)).astype(BF16)
    rows, lanes = own_small.shape[1], keep.shape[1] - LANES
    step = pl.program_id(0)

    @pl.when((core[0] == 1) & (step % 2 == 0))
    def _():
        share = step // 2
        out[:rows, lanes:] = (own_small[share] + other_small[share]).astype(BF16)


def finish(core, mine, other, qkv_out, out_out, rest_out):
    split, tail, width = mine.shape[1], qkv_out.shape[1] - mine.shape[1], out_out.shape[1]

    def fill(low, high):
        qkv_out[:, :split] = low[...]
        qkv_out[:, split:] = high[:, :tail]
        out_out[...] = high[:, tail : tail + width]
        rest_out[...] = high[:, tail + width :]

    @pl.when(core[0] == 0)
    def _():
        fill(mine, other)

    @pl.when(core[0] == 1)
    def _():
        fill(other, mine)


def mixer_forward(with_grads, *refs):
    if with_grads:
        x_ref, dy_ref, wqkv, wout, wr, gains, bias, srow, scol = refs[:9]
        send, hidden_out, gates_out, proj, mixed, norm1_out, norm2_out = refs[9:]
    else:
        place, x_ref = refs[:2]
        parts, (wr, gains, bias, srow, scol) = refs[2:6], refs[6:11]
        send, hidden_out, gates_out, wqkv, wout, proj, mixed = refs[11:]
        assemble(place, parts, wqkv, wout)
    tokens, width = x_ref.shape
    x = x_ref[...].astype(F32)
    norm1 = (x * row_scale(x) * gains[0:1, :]).astype(BF16)
    proj[...] = dot(norm1, wqkv[...]).astype(BF16)
    causal = seen(tokens)
    for pair in range(width // LANES):
        at = pair * LANES
        queries = stack_heads(proj[:, at : at + LANES])
        key = proj[:, width + at : width + at + LANES]
        value = proj[:, 2 * width + at : 2 * width + at + LANES]
        rows = slice(2 * pair * tokens, 2 * (pair + 1) * tokens)
        probs = soft_probs(queries, key, bias[rows, :], causal).astype(BF16)
        mixed[:, at : at + LANES] = join_heads(dot(probs, value)).astype(BF16)
    hidden = x + dot(mixed[...], wout[...])
    hidden_out[...] = hidden
    norm2 = (hidden * row_scale(hidden) * gains[1:2, :]).astype(BF16)
    logits = dot_nt(norm2, wr[...])
    lane = iota(logits.shape, 1)
    first = jnp.sum(jnp.where(lane == scol[:, 2:3], logits, 0.0), axis=1, keepdims=True)
    second = jnp.sum(jnp.where(lane == scol[:, 3:4], logits, 0.0), axis=1, keepdims=True)
    top = jnp.maximum(first, second)
    first = jnp.exp(first - top)
    second = jnp.exp(second - top)
    gate0 = first / (first + second)
    gate1 = second / (first + second)
    lane = iota((tokens, LANES), 1)
    gates_out[...] = jnp.where(lane == 0, gate0, jnp.where(lane == 1, gate1, 0.0))
    slot = iota((send.shape[0], tokens), 0)
    hits0 = slot == srow[0:1, :]
    hits1 = slot == srow[1:2, :]
    send[:, :width] = dot(one_hot(hits0 | hits1), norm2).astype(BF16)
    if with_grads:
        dy = dy_ref[...].astype(F32)
        send[:, width:] = (
            dot(one_hot(hits0), (gate0 * dy).astype(BF16))
            + dot(one_hot(hits1), (gate1 * dy).astype(BF16))
        ).astype(BF16)
        norm1_out[...] = norm1
        norm2_out[...] = norm2


def grads_out(dy_ref, gates, srow, send):
    tokens = dy_ref.shape[0]
    dy = dy_ref[...].astype(F32)
    slot = iota((send.shape[0], tokens), 0)
    send[...] = (
        dot(one_hot(slot == srow[0:1, :]), (gates[:, 0:1] * dy).astype(BF16))
        + dot(one_hot(slot == srow[1:2, :]), (gates[:, 1:2] * dy).astype(BF16))
    ).astype(BF16)


def combine(back, hidden, gates, scol, out):
    tokens = hidden.shape[0]
    slot = iota((tokens, back.shape[0]), 1)
    result0 = dot(one_hot(slot == scol[:, 0:1]), back[...])
    result1 = dot(one_hot(slot == scol[:, 1:2]), back[...])
    out[...] = (hidden[...] + gates[:, 0:1] * result0 + gates[:, 1:2] * result1).astype(BF16)


def bell(pre):
    return 0.5 * (1.0 + lax.erf(pre * 0.7071067811865476))


def grow(total, step, part):
    total[...] = jnp.where(step == 0, part, total[...] + part)


def experts_forward(rows, up, down, out, total):
    step = pl.program_id(0)
    pre = dot(rows[...], up[...])
    grow(total, step, dot((pre * bell(pre)).astype(BF16), down[...]))

    @pl.when(step == pl.num_programs(0) - 1)
    def _():
        out[...] = total[...].astype(BF16)


def experts_both(rows, up, down, out, act_out, slope_out, total, total_back):
    step = pl.program_id(0)
    width = up.shape[0]
    pre = dot(rows[:, :width], up[...])
    lower = bell(pre)
    act = (pre * lower).astype(BF16)
    slope = lower + pre * jnp.exp(-0.5 * pre * pre) * 0.3989422804014327
    act_out[...] = act
    slope_out[...] = slope.astype(BF16)
    pre_grads = (dot_nt(rows[:, width:], down[...]) * slope).astype(BF16)
    grow(total, step, dot(act, down[...]))
    grow(total_back, step, dot_nt(pre_grads, up[...]))

    @pl.when(step == pl.num_programs(0) - 1)
    def _():
        out[:, :width] = total[...].astype(BF16)
        out[:, width:] = total_back[...].astype(BF16)


def experts_backward(grads, up, down, slope, out, pre_out, total_back):
    step = pl.program_id(0)
    pre_grads = (dot_nt(grads[...], down[...]) * slope[...].astype(F32)).astype(BF16)
    pre_out[...] = pre_grads
    grow(total_back, step, dot_nt(pre_grads, up[...]))

    @pl.when(step == pl.num_programs(0) - 1)
    def _():
        out[...] = total_back[...].astype(BF16)


def mixer_backward(last, *refs):
    if last:
        (core, back, dy_ref, x_ref, res_in, wqkv, wout, wr, gains, bias, scol) = refs[:11]
        (hidden_ref, gates, proj, mixed, norm1, norm2) = refs[11:17]
        (input_grad, keep, give, stats, score_out, proj_grad) = refs[17:]
    else:
        (back, dy_ref, x_ref, wqkv, wout, wr, gains, bias, scol) = refs[:9]
        (hidden_ref, gates, proj) = refs[9:12]
        (input_grad, y_out, res_out, proj_grad) = refs[12:]
    tokens, width = x_ref.shape
    dy = dy_ref[...].astype(F32)
    hidden = hidden_ref[...]
    gate0 = gates[:, 0:1]
    gate1 = gates[:, 1:2]
    slot = iota((tokens, back.shape[0]), 1)
    hits0 = slot == scol[:, 0:1]
    hits1 = slot == scol[:, 1:2]
    if last:
        result0 = res_in[0].astype(F32)
        result1 = res_in[1].astype(F32)
        copy_rows = back[...]
    else:
        result0 = dot(one_hot(hits0), back[:, :width])
        result1 = dot(one_hot(hits1), back[:, :width])
        res_out[0] = result0.astype(BF16)
        res_out[1] = result1.astype(BF16)
        y_out[...] = (hidden + gate0 * result0 + gate1 * result1).astype(BF16)
        copy_rows = back[:, width:]
    gate_grad0 = jnp.sum(result0 * dy, axis=1, keepdims=True)
    gate_grad1 = jnp.sum(result1 * dy, axis=1, keepdims=True)
    inner = gate0 * gate_grad0 + gate1 * gate_grad1
    experts = wr.shape[0]
    lane = iota((tokens, experts), 1)
    logit_grads = (
        jnp.where(lane == scol[:, 2:3], gate0 * (gate_grad0 - inner), 0.0)
        + jnp.where(lane == scol[:, 3:4], gate1 * (gate_grad1 - inner), 0.0)
    ).astype(BF16)
    norm2_grads = dot(one_hot(hits0 | hits1), copy_rows) + dot(logit_grads, wr[...])
    scale2 = row_scale(hidden)
    weighted = norm2_grads * gains[1:2, :]
    inner = jnp.mean(weighted * hidden, axis=-1, keepdims=True)
    hidden_grad = dy + scale2 * weighted - hidden * (scale2 * scale2 * scale2 * inner)
    branch = hidden_grad.astype(BF16)
    mixed_grad = dot_nt(branch, wout[...]).astype(BF16)
    causal = seen(tokens)
    for pair in range(width // LANES):
        at = pair * LANES
        queries = stack_heads(proj[:, at : at + LANES])
        key = proj[:, width + at : width + at + LANES]
        value = proj[:, 2 * width + at : 2 * width + at + LANES]
        outer = stack_heads(mixed_grad[:, at : at + LANES])
        rows = slice(2 * pair * tokens, 2 * (pair + 1) * tokens)
        probs = soft_probs(queries, key, bias[rows, :], causal)
        prob_grad = dot_nt(outer, value)
        inner = jnp.sum(probs * prob_grad, axis=-1, keepdims=True)
        score_grad = (probs * (prob_grad - inner)).astype(BF16)
        if last:
            score_out[rows, :] = score_grad
        query_grad = join_heads(dot(score_grad, key)) * HEAD**-0.5
        key_grad = dot_tn(score_grad, queries) * HEAD**-0.5
        proj_grad[:, at : at + LANES] = query_grad.astype(BF16)
        proj_grad[:, width + at : width + at + LANES] = key_grad.astype(BF16)
        proj_grad[:, 2 * width + at : 2 * width + at + LANES] = dot_tn(
            probs.astype(BF16), outer
        ).astype(BF16)
    norm1_grads = dot_nt(proj_grad[...], wqkv[...])
    x = x_ref[...].astype(F32)
    scale1 = row_scale(x)
    weighted = norm1_grads * gains[0:1, :]
    inner = jnp.mean(weighted * x, axis=-1, keepdims=True)
    input_grad[...] = (
        hidden_grad + scale1 * weighted - x * (scale1 * scale1 * scale1 * inner)
    ).astype(BF16)
    if last:
        stats[0:1, :] = jnp.sum(norm1_grads * x * scale1, axis=0, keepdims=True)
        stats[1:2, :] = jnp.sum(norm2_grads * hidden * scale2, axis=0, keepdims=True)
        stats[2:8, :] = jnp.zeros((6, width), F32)
        split = keep.shape[1]
        tail = 3 * width - split

        def fill(low, high):
            low[...] = dot_tn(norm1[...], proj_grad[:, :split]).astype(BF16)
            high[:, :tail] = dot_tn(norm1[...], proj_grad[:, split:]).astype(BF16)
            high[:, tail : tail + width] = dot_tn(mixed[...], branch).astype(BF16)
            rest = tail + width
            high[:, rest : rest + experts] = dot_tn(norm2[...], logit_grads).astype(BF16)
            high[:, rest + experts :] = jnp.zeros((width, split - rest - experts), BF16)

        @pl.when(core[0] == 0)
        def _():
            fill(keep, give)

        @pl.when(core[0] == 1)
        def _():
            fill(give, keep)


def shape_of(*dims, dtype=BF16):
    return jax.ShapeDtypeStruct(dims, dtype)


def whole(kernel, outs, operands, scratch=(), scalar=False, flops=0, name=None, limit=LATE_BYTES):
    vmem = pl.BlockSpec(memory_space=pltpu.VMEM)
    specs = [vmem] * len(operands)
    if scalar:
        specs[0] = pl.BlockSpec(memory_space=pltpu.SMEM)
    moved = sum(o.size * o.dtype.itemsize for o in list(operands) + list(outs))
    return pl.pallas_call(
        kernel,
        out_shape=outs,
        in_specs=specs,
        out_specs=[vmem] * len(outs),
        scratch_shapes=list(scratch),
        cost_estimate=pl.CostEstimate(flops=flops, bytes_accessed=moved, transcendentals=0),
        compiler_params=pltpu.CompilerParams(vmem_limit_bytes=limit),
        name=name,
    )(*operands)


CHUNK = 768


def expert_call(kernel, rows, up, down, slope, wide_outs, out_cols, sums, name):
    count = rows.shape[0]
    width, hidden_units = up.shape
    specs = [
        pl.BlockSpec(rows.shape, lambda i: (0, 0)),
        pl.BlockSpec((width, CHUNK), lambda i: (0, i)),
        pl.BlockSpec((CHUNK, width), lambda i: (i, 0)),
    ]
    operands = [rows, up, down]
    per_chunk = pl.BlockSpec((count, CHUNK), lambda i: (0, i))
    if slope is not None:
        specs.append(per_chunk)
        operands.append(slope)
    outs = [shape_of(count, out_cols)] + [shape_of(count, hidden_units)] * wide_outs
    moved = sum(o.size * o.dtype.itemsize for o in operands + outs)
    return pl.pallas_call(
        kernel,
        out_shape=outs,
        grid=(hidden_units // CHUNK,),
        in_specs=specs,
        out_specs=[pl.BlockSpec((count, out_cols), lambda i: (0, 0))] + [per_chunk] * wide_outs,
        scratch_shapes=[pltpu.VMEM((count, width), F32)] * sums,
        cost_estimate=pl.CostEstimate(
            flops=4 * sums * count * width * hidden_units,
            bytes_accessed=moved,
            transcendentals=0,
        ),
        compiler_params=pltpu.CompilerParams(
            dimension_semantics=("arbitrary",),
            vmem_limit_bytes=VMEM_BYTES,
        ),
        name=name,
    )(*operands)


def trade(rows):
    count, columns = rows.shape
    pieces = rows.reshape(count // SLOTS, SLOTS, columns)
    return lax.all_to_all(pieces, MEMBERS, 0, 0, tiled=True).reshape(count, columns)


def swap(value, axis):
    return lax.ppermute(value, axis, [(0, 1), (1, 0)])


def in_order(index, mine, other, axis):
    return jnp.where(
        index == 0,
        jnp.concatenate([mine, other], axis=axis),
        jnp.concatenate([other, mine], axis=axis),
    )


def local(
    boundary,
    routes,
    buckets,
    query_key_value_weight,
    attention_output_weight,
    w_router,
    gain_attn,
    gain_moe,
    bias_table,
    expert_in,
    expert_out,
):
    section = lax.axis_index("section")
    shard = lax.axis_index("shard")
    core = lax.axis_index("core")
    _, micro, _, positions, width = boundary.shape
    tokens = 2 * positions
    heads = bias_table.shape[2]
    bucket_count = 2 * bias_table.shape[1]
    experts = w_router.shape[2]
    half_width = width // 2
    count = experts * SLOTS

    own_rows = boundary.reshape(micro, positions, width)
    own_routes = routes.reshape(micro, positions, 2)
    up = expert_in[0, 0]
    down = expert_out[0, 0]

    def pick(stacked, index):
        return lax.dynamic_index_in_dim(stacked, index, 0, keepdims=False)

    qkv_half = query_key_value_weight[0]
    out_half = attention_output_weight[0]
    table_rows = bucket_count // 2
    sent_routes = pick(own_routes, 1 - shard).astype(BF16).reshape(1, 2 * positions)
    own_small = jnp.concatenate(
        [
            w_router[0].T,
            gain_attn,
            gain_moe,
            jnp.zeros((5, half_width), BF16),
            jnp.pad(sent_routes, ((0, 0), (0, half_width - 2 * positions))),
            jnp.pad(bias_table[0], ((0, 0), (0, half_width - heads))),
        ],
        axis=0,
    )
    piece_rows = half_width // 2
    piece = jnp.concatenate(
        [
            lax.dynamic_slice_in_dim(qkv_half, core * piece_rows, piece_rows, 0),
            lax.dynamic_slice_in_dim(out_half, core * piece_rows, piece_rows, 0),
        ],
        axis=1,
    )
    far_rows = swap(pick(own_rows, 1 - shard), "shard")
    far_buckets = swap(buckets, "shard")
    far_small = swap(own_small, "shard")
    piece, far_rows, far_buckets, far_small = lax.optimization_barrier(
        (piece, far_rows, far_buckets, far_small)
    )
    near = swap(piece, "shard")
    gain_at, route_at, table_at = experts, experts + 7, experts + 8
    router = in_order(shard, own_small[:experts], far_small[:experts], 1)
    gains = in_order(
        shard, own_small[gain_at:table_at], far_small[gain_at:table_at], 1
    ).astype(F32)
    table = in_order(shard, own_small[table_at:, :heads], far_small[table_at:, :heads], 0)
    far_routes = far_small[route_at, : 2 * positions].astype(jnp.int32).reshape(positions, 2)
    mine = in_order(shard, pick(own_rows, shard), far_rows, 0)
    pairs = in_order(
        shard, pick(own_routes, shard), far_routes, 0
    )
    bucket_full = in_order(shard, buckets, far_buckets, 0)
    bucket_hot = (
        bucket_full[None] == jnp.arange(bucket_count, dtype=jnp.int32)[:, None, None]
    ).astype(BF16)
    (bias,) = whole(
        spread_bias,
        [shape_of(heads * tokens, tokens, dtype=F32)],
        (table.astype(F32).reshape(-1), bucket_full),
        scalar=True,
        name="spread_bias",
        limit=VMEM_BYTES,
    )

    flat = pairs.reshape(-1)
    hits = (flat[:, None] == jnp.arange(experts, dtype=jnp.int32)[None, :]).astype(jnp.int32)
    ranks = jnp.sum(jnp.cumsum(hits, axis=0) * hits, axis=1) - 1
    slots = (flat * SLOTS + ranks).reshape(tokens, 2)
    srow = jnp.pad(slots.T, ((0, 6), (0, 0)))
    scol = jnp.pad(jnp.concatenate([slots, pairs], axis=1), ((0, 0), (0, LANES - 4)))

    mixer_flops = 2 * tokens * width * 4 * width
    forward_shapes = [
        shape_of(tokens, width, dtype=F32),
        shape_of(tokens, LANES, dtype=F32),
    ]
    place = jnp.stack([shard, core]).astype(jnp.int32)
    near, mine, router, gains, bias, bucket_hot, srow, scol = lax.optimization_barrier(
        (near, mine, router, gains, bias, bucket_hot, srow, scol)
    )
    weight_parts = (qkv_half, out_half, near, swap(near, "core"))
    send, hidden, gates, wqkv, wout = whole(
        functools.partial(mixer_forward, False),
        [shape_of(count, width)]
        + forward_shapes
        + [shape_of(width, 3 * width), shape_of(width, width)],
        (place, mine) + weight_parts + (router, gains, bias, srow, scol),
        scalar=True,
        scratch=[pltpu.VMEM((tokens, 3 * width), BF16), pltpu.VMEM((tokens, width), BF16)],
        flops=mixer_flops,
        name="mixer_forward",
        limit=VMEM_BYTES,
    )
    (result_rows,) = expert_call(
        experts_forward, trade(send), up, down, None, 0, width, 1, "experts_forward"
    )
    (layer_out,) = whole(
        combine,
        [shape_of(tokens, width)],
        (trade(result_rows), hidden, gates, scol),
        name="combine",
    )
    arriving = lax.ppermute(layer_out, "section", [(0, 1)])
    layer_in = jnp.where(section == 0, mine, arriving)

    send, hidden, gates, proj, mixed, norm1, norm2 = whole(
        functools.partial(mixer_forward, True),
        [shape_of(count, 2 * width)]
        + forward_shapes
        + [
            shape_of(tokens, 3 * width),
            shape_of(tokens, width),
            shape_of(tokens, width),
            shape_of(tokens, width),
        ],
        (layer_in, mine, wqkv, wout, router, gains, bias, srow, scol),
        flops=mixer_flops,
        name="mixer_forward_keep",
        limit=VMEM_BYTES,
    )
    arrived = trade(send)
    both, act, slope = expert_call(
        experts_both, arrived, up, down, None, 2, 2 * width, 2, "experts_both"
    )
    input_grad, forward_rows, results = whole(
        functools.partial(mixer_backward, False),
        [
            shape_of(tokens, width),
            shape_of(tokens, width),
            shape_of(2, tokens, width),
        ],
        (trade(both), mine, layer_in, wqkv, wout, router, gains, bias, scol, hidden, gates, proj),
        scratch=[pltpu.VMEM((tokens, 3 * width), BF16)],
        flops=2 * mixer_flops,
        name="mixer_backward",
    )
    arriving = lax.ppermute(input_grad, "section", [(1, 0)])
    grad_in = jnp.where(section == 0, arriving, mine)

    (send,) = whole(
        grads_out, [shape_of(count, width)], (grad_in, gates, srow), name="grads_out"
    )
    arrived_grads = trade(send)
    copy_rows, pre_grads = expert_call(
        experts_backward, arrived_grads, up, down, slope, 1, width, 1, "experts_backward"
    )
    returned = trade(copy_rows)
    split = 13 * LANES
    tail = 3 * width - split
    input_grad, keep, give, stats, score_grads = whole(
        functools.partial(mixer_backward, True),
        [
            shape_of(tokens, width),
            shape_of(width, split),
            shape_of(width, split),
            shape_of(8, width, dtype=F32),
            shape_of(heads * tokens, tokens),
        ],
        (
            core.reshape(1),
            returned,
            grad_in,
            layer_in,
            results,
            wqkv,
            wout,
            router,
            gains,
            bias,
            scol,
            hidden,
            gates,
            proj,
            mixed,
            norm1,
            norm2,
        ),
        scratch=[pltpu.VMEM((tokens, 3 * width), BF16)],
        scalar=True,
        flops=3 * mixer_flops,
        name="mixer_backward_last",
    )

    finished = jnp.where(section == 0, input_grad, forward_rows).reshape(2, positions, width)
    from_other = swap(pick(finished, 1 - shard), "shard")
    boundary_out = jnp.stack(
        [
            jnp.where(shard == 0, pick(finished, shard), from_other),
            jnp.where(shard == 0, from_other, pick(finished, shard)),
        ]
    ).reshape(boundary.shape)

    table_grad = jnp.einsum(
        "bts,hts->bh",
        bucket_hot,
        score_grads.reshape(heads, tokens, tokens),
        preferred_element_type=F32
    )
    half_rows = half_width // LANES
    small = jnp.concatenate(
        [
            stats[0].reshape(2, half_rows, LANES),
            stats[1].reshape(2, half_rows, LANES),
            jnp.zeros((2, 8 - 2 * half_rows, LANES), F32),
            jnp.pad(
                table_grad.reshape(2, table_rows, heads), ((0, 0), (0, 0), (0, LANES - heads))
            ),
        ],
        axis=1,
    )
    small = jnp.pad(small, ((0, 0), (0, 32 - small.shape[1]), (0, 0)))
    block = pl.BlockSpec((width // 4, split), lambda i: (i, 0))
    whole_small = pl.BlockSpec(small.shape, lambda i: (0, 0, 0))
    summed = pl.pallas_call(
        merge,
        out_shape=shape_of(width, split),
        grid=(4,),
        in_specs=[
            pl.BlockSpec(memory_space=pltpu.SMEM),
            block,
            block,
            whole_small,
            whole_small,
        ],
        out_specs=block,
        compiler_params=pltpu.CompilerParams(vmem_limit_bytes=LATE_BYTES),
        name="merge",
    )(core.reshape(1), keep, swap(give, "core"), small, swap(small, "core"))
    summed, arrived, arrived_grads, act, pre_grads, boundary_out = lax.optimization_barrier(
        (summed, arrived, arrived_grads, act, pre_grads, boundary_out)
    )
    d_expert_in = lax.dot_general(
        arrived[:, :width], pre_grads, (((0,), (0,)), ((), ())), preferred_element_type=F32
    ).astype(BF16)
    d_expert_out = lax.dot_general(
        act, arrived_grads, (((0,), (0,)), ((), ())), preferred_element_type=F32
    ).astype(BF16)
    gathered = lax.all_to_all(
        summed.reshape(32, width // 32, split), ("shard", "y", "z"), 0, 0, tiled=True
    )
    gathered, d_expert_in, d_expert_out = lax.optimization_barrier(
        (gathered, d_expert_in, d_expert_out)
    )
    piece = jnp.sum(gathered.astype(F32), axis=0).astype(BF16)
    spread = lax.all_to_all(
        jnp.broadcast_to(piece[None], (16,) + piece.shape), ("y", "z"), 0, 0, tiled=True
    ).reshape(half_width, split)
    qkv_sum, out_sum, rest = whole(
        finish,
        [
            shape_of(half_width, 3 * width),
            shape_of(half_width, width),
            shape_of(half_width, 2 * LANES),
        ],
        (core.reshape(1), spread, swap(spread, "core")),
        scalar=True,
        name="finish",
    )
    totals = rest[: 8 + table_rows, LANES:]
    gain_one_sum = totals[:half_rows].reshape(half_width)
    gain_two_sum = totals[half_rows : 2 * half_rows].reshape(half_width)
    table_sum = totals[8:, :heads]
    return (
        boundary_out,
        qkv_sum[None],
        out_sum[None],
        rest[:, :experts][None],
        gain_one_sum[None],
        gain_two_sum[None],
        table_sum[None],
        d_expert_in.reshape(expert_in.shape),
        d_expert_out.reshape(expert_out.shape),
    )


def solution(mesh):
    fine = Mesh(
        mesh.devices.reshape(2, 4, 4, 2, 2), ("section", "y", "z", "core", "shard")
    )
    expert = ("y", "z", "core")
    rows = P("section", None, expert, "shard", None)
    by_pair = P("section", "shard", None)
    by_expert = P("section", MEMBERS, None, None)
    in_specs = (
        rows,
        rows,
        P("shard", None),
        by_pair,
        by_pair,
        by_pair,
        P("section", "shard"),
        P("section", "shard"),
        by_pair,
        by_expert,
        by_expert,
    )
    out_specs = (
        rows,
        by_pair,
        by_pair,
        by_pair,
        P("section", "shard"),
        P("section", "shard"),
        by_pair,
        by_expert,
        by_expert,
    )
    return jax.shard_map(local, mesh=fine, in_specs=in_specs, out_specs=out_specs, check_vma=False)
```
